32 devices in a mesh: fsdp: 4 (over z), context: 4 (over x, core), tensor: 2 (over y).
Axes of the slice: x: 2, y: 2, z: 4, core: 2. Of those that a mesh axis runs over, the one named last changes fastest.
Arguments:
- latents: bfloat16 [8, 1024, 1408], P('fsdp', ('context', 'tensor')), may hold values from -6 to 6
- skip_inputs: bfloat16 [2, 8, 1024, 1408], P(None, 'fsdp', ('context', 'tensor')), may hold values from -6 to 6
- text_states: bfloat16 [8, 333, 1024], P('fsdp'), may hold values from -6 to 6
- condition: bfloat16 [8, 1408], P('fsdp'), may hold values from -6 to 6
- positions: int32 [8, 2, 1024], P('fsdp', None, 'context'), may hold values from 0 to 63, as said below
- cotangent: bfloat16 [8, 1024, 1408], P('fsdp', ('context', 'tensor')), may hold values from -6 to 6
- skip_weight: float32 [2, 2816, 1408], P(None, ('fsdp', 'context'), 'tensor'), may hold values from -0.109375 to 0.109375
- mod_weight: float32 [2, 1408, 8448], P(None, ('fsdp', 'context'), 'tensor'), may hold values from -0.15625 to 0.15625
- proj_weight: float32 [2, 1408, 4, 1408], P(None, ('fsdp', 'context'), None, 'tensor'), may hold values from -0.15625 to 0.15625
- output_weight: float32 [2, 2, 1408, 1408], P(None, None, 'tensor', ('fsdp', 'context')), may hold values from -0.625 to 0.625
- text_weight: float32 [2, 1024, 2, 1408], P(None, ('fsdp', 'context'), None, 'tensor'), may hold values from -0.1875 to 0.1875
- up_weight: float32 [2, 1408, 6144], P(None, ('fsdp', 'context'), 'tensor'), may hold values from -0.15625 to 0.15625
- down_weight: float32 [2, 6144, 1408], P(None, 'tensor', ('fsdp', 'context')), may hold values from -0.078125 to 0.078125
- skip_momentum: float32 [2, 2816, 1408], P(None, ('fsdp', 'context'), 'tensor'), may hold values from -160 to 160
- mod_momentum: float32 [2, 1408, 8448], P(None, ('fsdp', 'context'), 'tensor'), may hold values from -160 to 160
- proj_momentum: float32 [2, 1408, 4, 1408], P(None, ('fsdp', 'context'), None, 'tensor'), may hold values from -160 to 160
- output_momentum: float32 [2, 2, 1408, 1408], P(None, None, 'tensor', ('fsdp', 'context')), may hold values from -160 to 160
- text_momentum: float32 [2, 1024, 2, 1408], P(None, ('fsdp', 'context'), None, 'tensor'), may hold values from -160 to 160
- up_momentum: float32 [2, 1408, 6144], P(None, ('fsdp', 'context'), 'tensor'), may hold values from -160 to 160
- down_momentum: float32 [2, 6144, 1408], P(None, 'tensor', ('fsdp', 'context')), may hold values from -160 to 160
- skip_average: float32 [2, 2816, 1408], P(None, ('fsdp', 'context'), 'tensor'), may hold values from -0.109375 to 0.109375
- mod_average: float32 [2, 1408, 8448], P(None, ('fsdp', 'context'), 'tensor'), may hold values from -0.15625 to 0.15625
- proj_average: float32 [2, 1408, 4, 1408], P(None, ('fsdp', 'context'), None, 'tensor'), may hold values from -0.15625 to 0.15625
- output_average: float32 [2, 2, 1408, 1408], P(None, None, 'tensor', ('fsdp', 'context')), may hold values from -0.625 to 0.625
- text_average: float32 [2, 1024, 2, 1408], P(None, ('fsdp', 'context'), None, 'tensor'), may hold values from -0.1875 to 0.1875
- up_average: float32 [2, 1408, 6144], P(None, ('fsdp', 'context'), 'tensor'), may hold values from -0.15625 to 0.15625
- down_average: float32 [2, 6144, 1408], P(None, 'tensor', ('fsdp', 'context')), may hold values from -0.078125 to 0.078125
Outputs:
- block_output: bfloat16 [8, 1024, 1408], P('fsdp', ('context', 'tensor'))
- latents_grad: float32 [8, 1024, 1408], P('fsdp', ('context', 'tensor'))
- skips_grad: float32 [2, 8, 1024, 1408], P(None, 'fsdp', ('context', 'tensor'))
- text_grad: float32 [8, 333, 1024], P('fsdp')
- condition_grad: float32 [8, 1408], P('fsdp')
- new_skip_weight: float32 [2, 2816, 1408], P(None, ('fsdp', 'context'), 'tensor')
- new_mod_weight: float32 [2, 1408, 8448], P(None, ('fsdp', 'context'), 'tensor')
- new_proj_weight: float32 [2, 1408, 4, 1408], P(None, ('fsdp', 'context'), None, 'tensor')
- new_output_weight: float32 [2, 2, 1408, 1408], P(None, None, 'tensor', ('fsdp', 'context'))
- new_text_weight: float32 [2, 1024, 2, 1408], P(None, ('fsdp', 'context'), None, 'tensor')
- new_up_weight: float32 [2, 1408, 6144], P(None, ('fsdp', 'context'), 'tensor')
- new_down_weight: float32 [2, 6144, 1408], P(None, 'tensor', ('fsdp', 'context'))
- new_skip_momentum: float32 [2, 2816, 1408], P(None, ('fsdp', 'context'), 'tensor')
- new_mod_momentum: float32 [2, 1408, 8448], P(None, ('fsdp', 'context'), 'tensor')
- new_proj_momentum: float32 [2, 1408, 4, 1408], P(None, ('fsdp', 'context'), None, 'tensor')
- new_output_momentum: float32 [2, 2, 1408, 1408], P(None, None, 'tensor', ('fsdp', 'context'))
- new_text_momentum: float32 [2, 1024, 2, 1408], P(None, ('fsdp', 'context'), None, 'tensor')
- new_up_momentum: float32 [2, 1408, 6144], P(None, ('fsdp', 'context'), 'tensor')
- new_down_momentum: float32 [2, 6144, 1408], P(None, 'tensor', ('fsdp', 'context'))
- new_skip_average: float32 [2, 2816, 1408], P(None, ('fsdp', 'context'), 'tensor')
- new_mod_average: float32 [2, 1408, 8448], P(None, ('fsdp', 'context'), 'tensor')
- new_proj_average: float32 [2, 1408, 4, 1408], P(None, ('fsdp', 'context'), None, 'tensor')
- new_output_average: float32 [2, 2, 1408, 1408], P(None, None, 'tensor', ('fsdp', 'context'))
- new_text_average: float32 [2, 1024, 2, 1408], P(None, ('fsdp', 'context'), None, 'tensor')
- new_up_average: float32 [2, 1408, 6144], P(None, ('fsdp', 'context'), 'tensor')
- new_down_average: float32 [2, 6144, 1408], P(None, 'tensor', ('fsdp', 'context'))
The draws below stay inside these ranges and needn't reach their ends.
Inputs may be any that keep to these rules, and one draw needn't show every extreme that they name: For each sequence, positions[s, 0, i] and positions[s, 1, i] are i // w and i % w for a grid width w that is 64, 32 or 16; at least one sequence of every draw has width 1024 // 64.
All inputs are finite; a program needn't handle non-finite values.
Results may differ from the reference program's by a relative error of at most 0.025.
Values may be sent and summed in bfloat16 or wider, within the bound.
A program may use at most 512 MiB of HBM per device.

```python
import math
import jax
import jax.numpy as jnp
from jax import lax

D = 1408
HEADS = 16
HD = 88
FF = 6144
DT = 1024
TXT = 333
LEN = 1024
LAYERS = 2
SEQS = 8


def draw_positions(key, part):
    key = jax.random.fold_in(key, 17)
    pick_key, wide_key = jax.random.split(key)
    exponents = jax.random.randint(pick_key, (SEQS,), 4, 7)
    widest = jax.random.randint(wide_key, (), 0, SEQS)
    exponents = jnp.where(jnp.arange(SEQS) == widest, 6, exponents)
    widths = LEN // jnp.left_shift(1, exponents)
    token_index = jnp.arange(LEN)
    grid_rows = token_index[None, :] // widths[:, None]
    grid_cols = token_index[None, :] % widths[:, None]
    return jnp.stack([grid_rows, grid_cols], axis=1).astype(jnp.int32)


def block_levels(rng, dims, pieces, smallest, largest):
    level, own = 1.0, jax.random.fold_in(rng, 6)
    for axis_at, blocks in pieces:
        steps = jnp.exp(jax.random.uniform(jax.random.fold_in(own, axis_at), (blocks,), jnp.float32, smallest / len(pieces), largest / len(pieces)))
        level = level * jnp.repeat(steps, dims[axis_at] // blocks).reshape([-1 if axis == axis_at else 1 for axis in range(len(dims))])
    return level


def scatter_about(own_key, extent, deviation, bound, cuts=(), held_as=jnp.bfloat16):
    entries = jax.random.normal(own_key, extent, jnp.float32) * deviation
    if len(cuts) > 0:
        entries = block_levels(own_key, extent, cuts, -0.22, 0.18) * entries
    return jnp.clip(entries, min=-bound, max=bound).astype(held_as)


def setup_inputs(seed: int = 0) -> dict:
    key_list = jax.random.split(jax.random.key(seed), 28)
    latents = scatter_about(key_list[0], (SEQS, LEN, D), 1.0, 6.0, ((0, 4), (1, 8)))
    skip_inputs = scatter_about(key_list[1], (LAYERS, SEQS, LEN, D), 1.0, 6.0, ((1, 4), (2, 8)))
    text_states = scatter_about(key_list[2], (SEQS, TXT, DT), 1.0, 6.0, ((0, 4),))
    condition = scatter_about(key_list[3], (SEQS, D), 1.0, 6.0, ((0, 4),))
    positions = draw_positions(jax.random.fold_in(key_list[27], 71), 0)
    cotangent = scatter_about(key_list[5], (SEQS, LEN, D), 1.0, 6.0, ((0, 4), (1, 8)))
    skip_weight = scatter_about(key_list[6], (LAYERS, 2 * D, D), (2 * D) ** -0.5, 0.109375, ((1, 16), (2, 2)), jnp.float32)
    mod_weight = scatter_about(key_list[7], (LAYERS, D, 6 * D), D ** -0.5, 0.15625, ((1, 16), (2, 2)), jnp.float32)
    proj_weight = scatter_about(key_list[8], (LAYERS, D, 4, D), D ** -0.5, 0.15625, ((1, 16), (3, 2)), jnp.float32)
    output_weight = scatter_about(key_list[9], (LAYERS, 2, D, D), (D // 16) ** -0.5, 0.625, ((2, 2), (3, 16)), jnp.float32)
    text_weight = scatter_about(key_list[10], (LAYERS, DT, 2, D), DT ** -0.5, 0.1875, ((1, 16), (3, 2)), jnp.float32)
    up_weight = scatter_about(key_list[11], (LAYERS, D, FF), D ** -0.5, 0.15625, ((1, 16), (2, 2)), jnp.float32)
    down_weight = scatter_about(key_list[12], (LAYERS, FF, D), FF ** -0.5, 0.078125, ((1, 2), (2, 16)), jnp.float32)
    skip_momentum = scatter_about(key_list[13], (LAYERS, 2 * D, D), (0.3 * (SEQS * LEN) ** 0.5), 160.0, ((1, 16), (2, 2)), jnp.float32)
    mod_momentum = scatter_about(key_list[14], (LAYERS, D, 6 * D), (0.3 * (SEQS * LEN) ** 0.5), 160.0, ((1, 16), (2, 2)), jnp.float32)
    proj_momentum = scatter_about(key_list[15], (LAYERS, D, 4, D), (0.3 * (SEQS * LEN) ** 0.5), 160.0, ((1, 16), (3, 2)), jnp.float32)
    output_momentum = scatter_about(key_list[16], (LAYERS, 2, D, D), (0.3 * (SEQS * LEN) ** 0.5), 160.0, ((2, 2), (3, 16)), jnp.float32)
    text_momentum = scatter_about(key_list[17], (LAYERS, DT, 2, D), (0.3 * (SEQS * LEN) ** 0.5), 160.0, ((1, 16), (3, 2)), jnp.float32)
    up_momentum = scatter_about(key_list[18], (LAYERS, D, FF), (0.3 * (SEQS * LEN) ** 0.5), 160.0, ((1, 16), (2, 2)), jnp.float32)
    down_momentum = scatter_about(key_list[19], (LAYERS, FF, D), (0.3 * (SEQS * LEN) ** 0.5), 160.0, ((1, 2), (2, 16)), jnp.float32)
    skip_average = scatter_about(key_list[20], (LAYERS, 2 * D, D), (2 * D) ** -0.5, 0.109375, ((1, 16), (2, 2)), jnp.float32)
    mod_average = scatter_about(key_list[21], (LAYERS, D, 6 * D), D ** -0.5, 0.15625, ((1, 16), (2, 2)), jnp.float32)
    proj_average = scatter_about(key_list[22], (LAYERS, D, 4, D), D ** -0.5, 0.15625, ((1, 16), (3, 2)), jnp.float32)
    output_average = scatter_about(key_list[23], (LAYERS, 2, D, D), (D // 16) ** -0.5, 0.625, ((2, 2), (3, 16)), jnp.float32)
    text_average = scatter_about(key_list[24], (LAYERS, DT, 2, D), DT ** -0.5, 0.1875, ((1, 16), (3, 2)), jnp.float32)
    up_average = scatter_about(key_list[25], (LAYERS, D, FF), D ** -0.5, 0.15625, ((1, 16), (2, 2)), jnp.float32)
    down_average = scatter_about(key_list[26], (LAYERS, FF, D), FF ** -0.5, 0.078125, ((1, 2), (2, 16)), jnp.float32)
    return {"latents": latents, "skip_inputs": skip_inputs, "text_states": text_states, "condition": condition, "positions": positions, "cotangent": cotangent, "skip_weight": skip_weight, "mod_weight": mod_weight, "proj_weight": proj_weight, "output_weight": output_weight, "text_weight": text_weight, "up_weight": up_weight, "down_weight": down_weight, "skip_momentum": skip_momentum, "mod_momentum": mod_momentum, "proj_momentum": proj_momentum, "output_momentum": output_momentum, "text_momentum": text_momentum, "up_momentum": up_momentum, "down_momentum": down_momentum, "skip_average": skip_average, "mod_average": mod_average, "proj_average": proj_average, "output_average": output_average, "text_average": text_average, "up_average": up_average, "down_average": down_average}


EPSILON = 1e-06
MOMENTUM = 0.9
AVERAGE_DECAY = 0.8
RATE_FACTOR = 0.5
ROPE_BASE = 10000.0
PRECISE = lax.Precision.HIGHEST

@jax.custom_vjp
def low(v):
    return lax.optimization_barrier(v.astype(jnp.bfloat16)).astype(jnp.float32)

@jax.custom_vjp
def low_back(v):
    return v

def low_keep(v):
    return (low(v), None)

def low_pass(kept, grad):
    return (grad,)

def back_keep(v):
    return (v, None)

def back_low(kept, grad):
    return (low(grad),)
low.defvjp(low_keep, low_pass)
low_back.defvjp(back_keep, back_low)

def rounded(operand):
    return low(low_back(operand))

def precise_dot(operand_left, operand_right):
    return jnp.dot(operand_left, operand_right, precision=PRECISE, preferred_element_type=jnp.float32)

def layer_norm(operand):
    centred = operand - lax.optimization_barrier(jnp.mean(operand, axis=-1, keepdims=True))
    return centred * lax.rsqrt(lax.optimization_barrier(jnp.mean(centred * centred, axis=-1, keepdims=True)) + EPSILON)

def root_norm(operand):
    return operand * lax.rsqrt(lax.optimization_barrier(jnp.mean(operand * operand, axis=-1, keepdims=True)) + EPSILON)

def rope_tables(grid):
    quarter = HD // 4
    frequency = ROPE_BASE ** (-jnp.arange(quarter, dtype=jnp.float32) / quarter)
    row_angle = grid[0].astype(jnp.float32)[:, None] * frequency
    col_angle = grid[1].astype(jnp.float32)[:, None] * frequency
    return (jnp.cos(row_angle), jnp.sin(row_angle), jnp.cos(col_angle), jnp.sin(col_angle))

def rotate(operand, tables):
    cos_row, sin_row, cos_col, sin_col = tables
    first, second, third, fourth = jnp.split(operand, 4, axis=-1)
    return jnp.concatenate([first * cos_row - second * sin_row, second * cos_row + first * sin_row, third * cos_col - fourth * sin_col, fourth * cos_col + third * sin_col], axis=-1)

def to_heads(operand):
    return operand.reshape(operand.shape[0], HEADS, HD).transpose(1, 0, 2)

def from_heads(operand):
    return operand.transpose(1, 0, 2).reshape(operand.shape[1], HEADS * HD)

def attend(queries, keys_low, values_low):
    score_scale = 1.0 / math.sqrt(HD)
    scores = low_back(score_scale * jnp.einsum('hqd,hkd->hqk', queries, keys_low, precision=PRECISE))
    probabilities = jax.nn.softmax(scores, axis=-1)
    return jnp.einsum('hqk,hkd->hqd', low(probabilities), values_low, precision=PRECISE)

def block(layer_index, masters, residual, skip_row, text_low, cond_low, tables):
    w_skip, w_mod, w_proj, w_outs, w_text, w_up, w_down = [low(weight[layer_index]) for weight in masters]
    concat = jnp.concatenate([residual, skip_row], axis=-1)
    after_skip = rounded(precise_dot(low(layer_norm(concat)), w_skip))
    modulation = low(precise_dot(cond_low[None, :], w_mod))[0]
    shift_a, scale_a, gate_a, shift_m, scale_m, gate_m = jnp.split(modulation, 6)
    attn_in = low(layer_norm(after_skip) * (1.0 + scale_a) + shift_a)
    projected = precise_dot(attn_in, w_proj[:, :3].reshape(D, 3 * D)).reshape(LEN, 3, D)
    query_raw = low_back(projected[:, 0])
    key_raw = low_back(projected[:, 1])
    value_low = rounded(projected[:, 2])
    query_low = low(rotate(root_norm(to_heads(query_raw)), tables))
    key_low = low(rotate(root_norm(to_heads(key_raw)), tables))
    attn_low = rounded(from_heads(attend(query_low, key_low, to_heads(value_low))))
    after_attn = after_skip + gate_a * low_back(precise_dot(attn_low, w_outs[0]))
    cross_in = low(layer_norm(after_attn))
    cross_raw = low_back(precise_dot(cross_in, w_proj[:, 3]))
    cross_query = low(root_norm(to_heads(cross_raw)))
    text_proj = precise_dot(text_low, w_text.reshape(DT, 2 * D)).reshape(TXT, 2, D)
    text_key = low(root_norm(to_heads(low_back(text_proj[:, 0]))))
    text_value = rounded(text_proj[:, 1])
    cross_low = rounded(from_heads(attend(cross_query, text_key, to_heads(text_value))))
    after_cross = after_attn + low_back(precise_dot(cross_low, w_outs[1]))
    mlp_in = low(layer_norm(after_cross) * (1.0 + scale_m) + shift_m)
    upward = low_back(precise_dot(mlp_in, w_up))
    hidden_low = low(jax.nn.gelu(upward, approximate=True))
    return after_cross + gate_m * low_back(precise_dot(hidden_low, w_down))

def forward(masters, residual, skip_rows, text_seq, cond_seq, tables):
    text_low = low(text_seq)
    cond_low = low(jax.nn.silu(cond_seq))
    for layer_index in range(LAYERS):
        residual = block(layer_index, masters, residual, skip_rows[layer_index], text_low, cond_low, tables)
    return residual

def reference(latents, skip_inputs, text_states, condition, positions, cotangent, skip_weight, mod_weight, proj_weight, output_weight, text_weight, up_weight, down_weight, skip_momentum, mod_momentum, proj_momentum, output_momentum, text_momentum, up_momentum, down_momentum, skip_average, mod_average, proj_average, output_average, text_average, up_average, down_average):
    masters = (skip_weight, mod_weight, proj_weight, output_weight, text_weight, up_weight, down_weight)
    momenta = (skip_momentum, mod_momentum, proj_momentum, output_momentum, text_momentum, up_momentum, down_momentum)
    averages = (skip_average, mod_average, proj_average, output_average, text_average, up_average, down_average)

    def per_sequence(summed, inputs):
        latent_seq, skip_seq, text_seq, cond_seq, grid_seq, cot_seq = inputs
        tables = rope_tables(grid_seq)

        def run(weights_in, latent_in, skip_in, text_in, cond_in):
            return forward(weights_in, latent_in, skip_in, text_in, cond_in, tables)
        output, pull = jax.vjp(run, masters, latent_seq, skip_seq, text_seq, cond_seq)
        grads = pull(cot_seq)
        summed = jax.tree.map(jnp.add, summed, grads[0])
        return (summed, (output.astype(jnp.bfloat16), grads[1], grads[2], grads[3], grads[4]))
    zeros_start = jax.tree.map(jnp.zeros_like, masters)
    sequences = (latents.astype(jnp.float32), jnp.moveaxis(skip_inputs.astype(jnp.float32), 1, 0), text_states.astype(jnp.float32), condition.astype(jnp.float32), positions, cotangent.astype(jnp.float32))
    summed, (outputs, latent_grads, skip_grads, text_grads, cond_grads) = lax.scan(per_sequence, zeros_start, sequences)
    skip_grads = jnp.moveaxis(skip_grads, 0, 1)
    spreads = ((2 * D) ** (-0.5), D ** (-0.5), D ** (-0.5), (D // 16) ** (-0.5), DT ** (-0.5), D ** (-0.5), FF ** (-0.5))
    tokens_total = SEQS * LEN
    new_weights = []
    new_momenta = []
    new_averages = []
    for weight, moment, average, gradient, spread in zip(masters, momenta, averages, summed, spreads):
        rate = RATE_FACTOR * spread / math.sqrt(tokens_total)
        moment_new = MOMENTUM * moment + gradient
        weight_new = weight - rate * (gradient + MOMENTUM * moment_new)
        new_weights.append(weight_new)
        new_momenta.append(moment_new)
        new_averages.append(AVERAGE_DECAY * average + (1.0 - AVERAGE_DECAY) * weight_new)
    return (outputs, latent_grads, skip_grads, text_grads, cond_grads, new_weights[0], new_weights[1], new_weights[2], new_weights[3], new_weights[4], new_weights[5], new_weights[6], new_momenta[0], new_momenta[1], new_momenta[2], new_momenta[3], new_momenta[4], new_momenta[5], new_momenta[6], new_averages[0], new_averages[1], new_averages[2], new_averages[3], new_averages[4], new_averages[5], new_averages[6])
```

```python
import math
from types import SimpleNamespace
import jax
import jax.numpy as jnp
from jax import lax
from jax.experimental import pallas as pl
from jax.experimental.pallas import tpu as pltpu
from jax.sharding import PartitionSpec as P

HD = 88
EPSILON = 1e-06
SCORE_SCALE = 1.0 / math.sqrt(HD)
LOW = jnp.bfloat16
MIB = 1 << 20


def vmem(mebibytes):
    return pltpu.CompilerParams(vmem_limit_bytes=mebibytes * MIB)


TOKEN = jax.ShapeDtypeStruct((8, 128), jnp.float32)
TOKEN_SPEC = pl.BlockSpec((8, 128), lambda *place: (0, 0))
FREE = pl.BlockSpec(memory_space=pl.ANY)
IN_HBM = pl.BlockSpec(memory_space=pltpu.HBM)
WHOLE = pl.BlockSpec(memory_space=pltpu.VMEM)


def cost(flops, moved, transcendentals=0):
    share = 1000
    return pl.CostEstimate(
        flops=flops // share,
        bytes_accessed=moved // share,
        transcendentals=transcendentals // share,
    )


def mark(token_ref):
    token_ref[...] = jnp.zeros(token_ref.shape, jnp.float32)


def gate(operand, after):
    return pl.pallas_call(
        lambda *refs: None,
        in_specs=[IN_HBM] + [FREE] * len(after),
        out_specs=IN_HBM,
        out_shape=jax.ShapeDtypeStruct(operand.shape, operand.dtype),
        input_output_aliases={0: 0},
    )(operand, *after)


def contract(left, right, left_dim, right_dim):
    return lax.dot_general(
        left, right, (((left_dim,), (right_dim,)), ((), ())), preferred_element_type=jnp.float32
    )


def head(operand, index):
    return operand[:, index * HD : (index + 1) * HD]


def head_marks(width):
    heads = width // HD
    column = lax.broadcasted_iota(jnp.int32, (width, heads), 0)
    first = lax.broadcasted_iota(jnp.int32, (width, heads), 1) * HD
    return jnp.where((column >= first) & (column < first + HD), 1.0, 0.0).astype(LOW)


def halves(operand):
    upper = operand.astype(LOW)
    return upper, (operand - upper.astype(jnp.float32)).astype(LOW)


def head_mean(operand, marks):
    return contract(operand.astype(LOW), marks, 1, 0) / HD


def to_columns(operand, marks):
    upper, lower = halves(operand)
    return contract(upper, marks, 1, 1) + contract(lower, marks, 1, 1)


def root_factor(operand, marks):
    return to_columns(lax.rsqrt(head_mean(operand * operand, marks) + EPSILON), marks)


def root_back(operand, upstream, marks):
    factor = root_factor(operand, marks)
    normed = operand * factor
    mean = head_mean(upstream * normed, marks).astype(LOW)
    return factor * (upstream - normed * contract(mean, marks, 1, 1))


def swap_quarters(operand):
    quarter = HD // 4
    column = lax.broadcasted_iota(jnp.int32, operand.shape, 1)
    left = jnp.concatenate([operand[:, quarter:], operand[:, :quarter]], axis=-1)
    right = jnp.concatenate([operand[:, -quarter:], operand[:, :-quarter]], axis=-1)
    return jnp.where(column % (2 * quarter) < quarter, left, right)


def turn_kernel(query_ref, key_ref, cos_ref, sin_ref, *refs):
    query_out, key_out, token_ref = refs[-3:]
    mark(token_ref)
    cos, sin = cos_ref[...], sin_ref[...]
    marks = head_marks(cos.shape[1])
    for source, target in ((query_ref, query_out), (key_ref, key_out)):
        value = source[...]
        value = value * root_factor(value, marks)
        target[...] = (value * cos + swap_quarters(value) * sin).astype(LOW)


def row_blocks(operand):
    rows, width = operand.shape
    return pl.BlockSpec((min(rows, 128), width), lambda i: (i, 0))


def turn(query_raw, key_raw, cos, sin, after):
    rows, width = query_raw.shape
    spec = row_blocks(query_raw)
    shape = jax.ShapeDtypeStruct((rows, width), LOW)
    return pl.pallas_call(
        turn_kernel,
        grid=(rows // min(rows, 128),),
        in_specs=[spec] * 4 + [FREE] * len(after),
        out_specs=[spec, spec, TOKEN_SPEC],
        out_shape=[shape, shape, TOKEN],
        compiler_params=vmem(32),
        cost_estimate=cost(100 * rows * width, 20 * rows * width),
    )(query_raw, key_raw, cos, sin, *after)


def turn_back_kernel(grad_ref, raw_ref, cos_ref, sin_ref, *refs):
    out_ref, token_ref = refs[-2:]
    mark(token_ref)
    cos, sin = cos_ref[...], sin_ref[...]
    grad = grad_ref[...].astype(jnp.float32)
    grad = grad * cos - swap_quarters(grad) * sin
    out_ref[...] = root_back(raw_ref[...], grad, head_marks(cos.shape[1])).astype(LOW)


def turn_back(grad, raw, cos, sin, after):
    rows, width = raw.shape
    spec = row_blocks(raw)
    return pl.pallas_call(
        turn_back_kernel,
        grid=(rows // min(rows, 128),),
        in_specs=[spec] * 4 + [FREE] * len(after),
        out_specs=[spec, TOKEN_SPEC],
        out_shape=[jax.ShapeDtypeStruct((rows, width), LOW), TOKEN],
        compiler_params=vmem(32),
        cost_estimate=cost(100 * rows * width, 16 * rows * width),
    )(grad, raw, cos, sin, *after)


def root_kernel(raw_ref, *refs):
    out_ref, token_ref = refs[-2:]
    mark(token_ref)
    raw = raw_ref[...]
    out_ref[...] = (raw * root_factor(raw, head_marks(raw.shape[1]))).astype(LOW)


def root(raw, after):
    rows, width = raw.shape
    spec = row_blocks(raw)
    return pl.pallas_call(
        root_kernel,
        grid=(rows // min(rows, 128),),
        in_specs=[spec] + [FREE] * len(after),
        out_specs=[spec, TOKEN_SPEC],
        out_shape=[jax.ShapeDtypeStruct((rows, width), LOW), TOKEN],
        compiler_params=vmem(32),
        cost_estimate=cost(50 * rows * width, 6 * rows * width),
    )(raw, *after)


def flat(ref):
    value = ref[...]
    return value.reshape(value.shape[0] * value.shape[2], value.shape[3])


def attend_kernel(count, query_ref, *refs):
    keys, values = refs[:count], refs[count : 2 * count]
    out_ref, lse_ref = refs[-2:]
    query = flat(query_ref)
    keys = [flat(ref) for ref in keys]
    values = [flat(ref) for ref in values]
    pieces = []
    for index in range(query.shape[1] // HD):
        query_head = head(query, index)
        scores = [contract(head(key, index), query_head, 1, 1) for key in keys]
        peak = scores[0].max(axis=0, keepdims=True)
        for score in scores[1:]:
            peak = jnp.maximum(peak, score.max(axis=0, keepdims=True))
        mass = 0.0
        out = 0.0
        for score, value in zip(scores, values):
            weight = jnp.exp((score - peak) * SCORE_SCALE)
            mass = mass + weight.sum(axis=0, keepdims=True)
            out = out + contract(head(value, index), weight.astype(LOW), 0, 0)
        pieces.append((out / mass).T.astype(LOW))
        lse_ref[0, index : index + 1, :] = peak * SCORE_SCALE + jnp.log(mass)
    out_ref[...] = jnp.concatenate(pieces, axis=-1).reshape(out_ref.shape)


def block_of(operand):
    parts, _, tokens, width = operand.shape
    return pl.BlockSpec((parts, 1, tokens, width), lambda s: (0, s, 0, 0))


def attend(query, keys, values, after):
    parts, seqs, tokens, width = query.shape
    heads = width // HD
    count = len(keys)
    pairs = seqs * heads * (parts * tokens) ** 2 * count
    return pl.pallas_call(
        lambda *refs: attend_kernel(count, *refs),
        grid=(seqs,),
        in_specs=[block_of(query)] * (1 + 2 * count) + [FREE] * len(after),
        out_specs=[
            block_of(query),
            pl.BlockSpec((1, heads, parts * tokens), lambda s: (s, 0, 0)),
        ],
        out_shape=[
            jax.ShapeDtypeStruct(query.shape, LOW),
            jax.ShapeDtypeStruct((seqs, heads, parts * tokens), jnp.float32),
        ],
        compiler_params=vmem(48),
        cost_estimate=cost(8 * pairs * 128, 20 * query.size, pairs),
    )(query, *keys, *values, *after)


def attend_back_kernel(count, query_ref, raw_ref, grad_ref, lse_ref, cos_ref, sin_ref, *refs):
    key_refs, value_refs = refs[:count], refs[count : 2 * count]
    outs = refs[-2 * count - 2 :]
    query_out, key_outs, value_outs = outs[0], outs[1 : count + 1], outs[count + 1 : -1]
    mark(outs[-1])
    query, raw, grad = flat(query_ref), flat(raw_ref), flat(grad_ref)
    cos, sin = flat(cos_ref), flat(sin_ref)
    keys = [flat(ref) for ref in key_refs]
    values = [flat(ref) for ref in value_refs]
    query_pieces = []
    key_pieces = [[] for _ in keys]
    value_pieces = [[] for _ in keys]
    for index in range(query.shape[1] // HD):
        query_head, grad_head = head(query, index), head(grad, index)
        lse = lse_ref[0, index : index + 1, :]
        weights = []
        weight_grads = []
        delta = 0.0
        for key, value in zip(keys, values):
            weight = jnp.exp(contract(head(key, index), query_head, 1, 1) * SCORE_SCALE - lse)
            weight_grad = contract(head(value, index), grad_head, 1, 1)
            delta = delta + (weight * weight_grad).sum(axis=0, keepdims=True)
            weights.append(weight)
            weight_grads.append(weight_grad)
        query_grad = 0.0
        for place, key in enumerate(keys):
            weight = weights[place]
            score_grad = (weight * (weight_grads[place] - delta)).astype(LOW)
            query_grad = query_grad + contract(head(key, index), score_grad, 0, 0)
            key_pieces[place].append(
                (contract(score_grad, query_head, 1, 0) * SCORE_SCALE).astype(LOW)
            )
            value_pieces[place].append(contract(weight.astype(LOW), grad_head, 1, 0).astype(LOW))
        query_pieces.append(query_grad.T * SCORE_SCALE)
    query_grad = jnp.concatenate(query_pieces, axis=-1)
    query_grad = query_grad * cos - swap_quarters(query_grad) * sin
    query_grad = root_back(raw, query_grad, head_marks(raw.shape[1]))
    query_out[...] = query_grad.astype(LOW).reshape(query_out.shape)
    for target, pieces in zip(key_outs, key_pieces):
        target[...] = jnp.concatenate(pieces, axis=-1).reshape(target.shape)
    for target, pieces in zip(value_outs, value_pieces):
        target[...] = jnp.concatenate(pieces, axis=-1).reshape(target.shape)


def attend_back(query, raw, grad, lse, cos, sin, keys, values, after):
    parts, seqs, tokens, width = query.shape
    heads = width // HD
    count = len(keys)
    pairs = seqs * heads * (parts * tokens) ** 2 * count
    shape = jax.ShapeDtypeStruct(query.shape, LOW)
    spec = block_of(query)
    outs = pl.pallas_call(
        lambda *refs: attend_back_kernel(count, *refs),
        grid=(seqs,),
        in_specs=[
            spec,
            spec,
            spec,
            pl.BlockSpec((1, heads, parts * tokens), lambda s: (s, 0, 0)),
            block_of(cos),
            block_of(sin),
        ]
        + [spec] * (2 * count)
        + [FREE] * len(after),
        out_specs=[spec] * (1 + 2 * count) + [TOKEN_SPEC],
        out_shape=[shape] * (1 + 2 * count) + [TOKEN],
        compiler_params=vmem(56),
        cost_estimate=cost(20 * pairs * 128, 40 * query.size, pairs),
    )(query, raw, grad, lse, cos, sin, *keys, *values, *after)
    return outs[0], list(outs[1 : 1 + count]), list(outs[1 + count : -1]), outs[-1]


def text_probs(query, key, index, count):
    scores = contract(head(key, index), head(query, index), 1, 1) * SCORE_SCALE
    inside = lax.broadcasted_iota(jnp.int32, scores.shape, 0) < count
    scores = jnp.where(inside, scores, -1e30)
    weight = jnp.exp(scores - scores.max(axis=0, keepdims=True))
    return weight / weight.sum(axis=0, keepdims=True)


def cross_kernel(count, raw_ref, key_ref, value_ref, *refs):
    out_ref, token_ref = refs[-2:]
    mark(token_ref)
    raw, key, value = raw_ref[0], key_ref[0], value_ref[0]
    query = (raw * root_factor(raw, head_marks(raw.shape[1]))).astype(LOW)
    pieces = []
    for index in range(value.shape[1] // HD):
        probs = text_probs(query, key, index, count)
        pieces.append(contract(head(value, index), probs.astype(LOW), 0, 0).T.astype(LOW))
    out_ref[0] = jnp.concatenate(pieces, axis=-1)


def sequence_block(operand):
    return pl.BlockSpec((1,) + operand.shape[1:], lambda s: (s, 0, 0))


def cross(query_raw, key, value, count, after):
    seqs, tokens, width = query_raw.shape
    pairs = seqs * tokens * key.shape[1] * (width // HD)
    return pl.pallas_call(
        lambda *refs: cross_kernel(count, *refs),
        grid=(seqs,),
        in_specs=[sequence_block(operand) for operand in (query_raw, key, value)]
        + [FREE] * len(after),
        out_specs=[sequence_block(query_raw), TOKEN_SPEC],
        out_shape=[jax.ShapeDtypeStruct(query_raw.shape, LOW), TOKEN],
        compiler_params=vmem(32),
        cost_estimate=cost(8 * pairs * 128, 6 * query_raw.size + 4 * key.size, pairs),
    )(query_raw, key, value, *after)


def cross_back_kernel(count, raw_ref, key_raw_ref, key_ref, value_ref, grad_ref, *refs):
    query_out, key_out, value_out, token_ref = refs[-4:]
    mark(token_ref)
    raw, key_raw = raw_ref[0], key_raw_ref[0]
    key, value, grad = key_ref[0], value_ref[0], grad_ref[0]
    marks = head_marks(raw.shape[1])
    query = (raw * root_factor(raw, marks)).astype(LOW)
    query_pieces, key_pieces, value_pieces = [], [], []
    for index in range(value.shape[1] // HD):
        probs = text_probs(query, key, index, count)
        grad_head = head(grad, index)
        probs_grad = contract(head(value, index), grad_head, 1, 1)
        delta = (probs * probs_grad).sum(axis=0, keepdims=True)
        score_grad = (probs * (probs_grad - delta)).astype(LOW)
        query_pieces.append(contract(head(key, index), score_grad, 0, 0).T * SCORE_SCALE)
        key_pieces.append(contract(score_grad, head(query, index), 1, 0) * SCORE_SCALE)
        value_pieces.append(contract(probs.astype(LOW), grad_head, 1, 0).astype(LOW))
    query_grad = jnp.concatenate(query_pieces, axis=-1)
    query_out[0] = root_back(raw, query_grad, marks).astype(LOW)
    key_grad = jnp.concatenate(key_pieces, axis=-1)
    key_out[0] = root_back(key_raw, key_grad, marks).astype(LOW)
    value_out[0] = jnp.concatenate(value_pieces, axis=-1)


def cross_back(query_raw, key_raw, key, value, grad, count, after):
    seqs, tokens, width = query_raw.shape
    pairs = seqs * tokens * key_raw.shape[1] * (width // HD)
    return pl.pallas_call(
        lambda *refs: cross_back_kernel(count, *refs),
        grid=(seqs,),
        in_specs=[sequence_block(operand) for operand in (query_raw, key_raw, key, value, grad)]
        + [FREE] * len(after),
        out_specs=[sequence_block(operand) for operand in (query_raw, key_raw, value)]
        + [TOKEN_SPEC],
        out_shape=[
            jax.ShapeDtypeStruct(operand.shape, LOW) for operand in (query_raw, key_raw, value)
        ]
        + [TOKEN],
        compiler_params=vmem(40),
        cost_estimate=cost(20 * pairs * 128, 10 * query_raw.size + 10 * key_raw.size, pairs),
    )(query_raw, key_raw, key, value, grad, *after)


def spread_kernel(cos_ref, sin_ref, cos_out, sin_out):
    for source, target in ((cos_ref, cos_out), (sin_ref, sin_out)):
        target[...] = jnp.concatenate([source[...]] * (target.shape[1] // HD), axis=-1)


def spread_heads(cos, sin, width):
    shape = jax.ShapeDtypeStruct((cos.shape[0], width), jnp.float32)
    return pl.pallas_call(
        spread_kernel,
        in_specs=[WHOLE] * 2,
        out_specs=[WHOLE] * 2,
        out_shape=[shape] * 2,
        compiler_params=vmem(32),
    )(cos, sin)


def add_kernel(count, cut, *refs):
    outs = refs[-count - 1 : -1]
    mark(refs[-1])
    for index in range(count):
        left, right = refs[2 * index][0], refs[2 * index + 1][0]
        total = left.astype(jnp.float32) + right.astype(jnp.float32)
        if cut:
            total = total.reshape(cut, -1, total.shape[1])
            outs[index][:, 0] = total.astype(LOW)
        else:
            outs[index][0] = total.astype(LOW)


def add_pairs(pairs, cut, after):
    count, rows, width = pairs[0][0].shape
    spec = pl.BlockSpec((1, rows, width), lambda j: (j, 0, 0))
    if cut:
        out_spec = pl.BlockSpec((cut, 1, rows // cut, width), lambda j: (0, j, 0, 0))
        shape = jax.ShapeDtypeStruct((cut, count, rows // cut, width), LOW)
    else:
        out_spec = spec
        shape = jax.ShapeDtypeStruct((count, rows, width), LOW)
    operands = [operand for pair in pairs for operand in pair]
    return pl.pallas_call(
        lambda *refs: add_kernel(len(pairs), cut, *refs),
        grid=(count,),
        in_specs=[spec] * len(operands) + [FREE] * len(after),
        out_specs=[out_spec] * len(pairs) + [TOKEN_SPEC],
        out_shape=[shape] * len(pairs) + [TOKEN],
        compiler_params=vmem(40),
        cost_estimate=cost(len(pairs) * pairs[0][0].size, 6 * len(pairs) * pairs[0][0].size),
    )(*operands, *after)


D = 1408
FF = 6144
DT = 1024
MOMENTUM = 0.9
AVERAGE_DECAY = 0.8
RATE_FACTOR = 0.5
ROPE_BASE = 10000.0
PRECISE = lax.Precision.HIGHEST
FSDP, CONTEXT, TENSOR = "fsdp", "context", "tensor"
MESH = pl.DeviceIdType.MESH


def low(operand):
    return operand.astype(LOW)


def wide(operand):
    return operand.astype(jnp.float32)


def layer_norm(operand):
    centred = operand - jnp.mean(operand, axis=-1, keepdims=True)
    return centred * lax.rsqrt(jnp.mean(centred * centred, axis=-1, keepdims=True) + EPSILON)


def layer_norm_back(operand, upstream):
    centred = operand - jnp.mean(operand, axis=-1, keepdims=True)
    factor = lax.rsqrt(jnp.mean(centred * centred, axis=-1, keepdims=True) + EPSILON)
    normed = centred * factor
    return factor * (
        upstream
        - jnp.mean(upstream, axis=-1, keepdims=True)
        - normed * jnp.mean(upstream * normed, axis=-1, keepdims=True)
    )


CORE, CHIP = 1, 2


def in_rows(operand):
    rows, width = operand.shape[-2:]
    if width % 128 and rows % 128 == 0:
        return operand.reshape(-1, 8, width)
    return operand


def swap_context(operand, bit):
    size = lax.axis_size(CONTEXT)
    pairs = [(i, i ^ bit) for i in range(size)]
    return lax.ppermute(in_rows(operand), CONTEXT, pairs).reshape(operand.shape)


def swap_tensor(operand):
    return lax.ppermute(in_rows(operand), TENSOR, [(0, 1), (1, 0)]).reshape(operand.shape)


def shift_fsdp(operand, step):
    size = lax.axis_size(FSDP)
    return lax.ppermute(operand, FSDP, [(i, (i + step) % size) for i in range(size)])


def paired():
    return lax.axis_size(TENSOR) == 2


def tensor_order(own, other, axis):
    first = lax.axis_index(TENSOR) == 0
    return jnp.concatenate(
        [jnp.where(first, own, other), jnp.where(first, other, own)], axis=axis
    )


def gather_tensor(own):
    if paired():
        return [own, swap_tensor(own)]
    return [lax.all_gather(own, TENSOR, axis=0, tiled=True)]


def term_shapes(rows, width):
    if paired():
        return [(rows // 2, width, jnp.float32), (rows // 2, width, LOW)]
    return [(rows, width, LOW)]


def split_terms(total):
    return own_and_other(total) if paired() else [total]


def sum_tensor(terms):
    if paired():
        return terms[0] + wide(swap_tensor(terms[1]))
    return wide(lax.psum_scatter(terms[0], TENSOR, scatter_dimension=0, tiled=True))


def columns_of(operand):
    parts = jnp.split(operand, lax.axis_size(TENSOR), axis=-1)
    if paired():
        first = lax.axis_index(TENSOR) == 0
        return [jnp.where(first, parts[0], parts[1]), jnp.where(first, parts[1], parts[0])]
    return parts


def join_columns(parts):
    if paired():
        return tensor_order(parts[0], parts[1], -1)
    return jnp.concatenate(parts, axis=-1)


def gather_fsdp_small(own):
    size = lax.axis_size(FSDP)
    place = lax.axis_index(FSDP)
    out = jnp.zeros((size,) + own.shape, own.dtype)
    out = lax.dynamic_update_index_in_dim(out, own, place, 0)
    for step in range(1, size):
        out = lax.dynamic_update_index_in_dim(
            out, shift_fsdp(own, step), (place - step + size) % size, 0
        )
    return out


def sum_fsdp_small(parts):
    size = lax.axis_size(FSDP)
    place = lax.axis_index(FSDP)
    total = lax.dynamic_index_in_dim(parts, place, 0, keepdims=False)
    for step in range(1, size):
        part = lax.dynamic_index_in_dim(parts, (place + step) % size, 0, keepdims=False)
        total = total + shift_fsdp(part, step)
    return total


def sum_context(total):
    for bit in (CORE, CHIP):
        total = total + swap_context(total, bit)
    return total


def gather_context(own):
    parts = [(0, own)]
    for bit in (CHIP, CORE):
        parts = parts + [(offset ^ bit, swap_context(part, bit)) for offset, part in parts]
    return parts


def multiply(body, lefts, rights, turned, extras, outs, after, tile=512):
    width = outs[0][1]
    tile = min(tile, width)
    counts = [len(lefts), len(rights), len(extras)]
    first, second, third = counts[0], sum(counts[:2]), sum(counts)

    def kernel(*refs):
        results, token_ref = refs[-len(outs) - 1 : -1], refs[-1]
        mark(token_ref)
        values = [ref[...] for ref in refs[:third]]
        for result, value in zip(
            results, body(values[:first], values[first:second], values[second:third])
        ):
            result[...] = value.astype(result.dtype)

    def column_block(rows):
        return pl.BlockSpec((rows, tile), lambda j: (0, j))

    def right_block(right):
        if turned:
            return pl.BlockSpec((tile, right.shape[1]), lambda j: (j, 0))
        return column_block(right.shape[0])

    flops = 2 * sum(right.size for right in rights) * outs[0][0]
    return pl.pallas_call(
        kernel,
        grid=(pl.cdiv(width, tile),),
        in_specs=[pl.BlockSpec(left.shape, lambda j: (0, 0)) for left in lefts]
        + [right_block(right) for right in rights]
        + [column_block(extra.shape[0]) for extra in extras]
        + [FREE] * len(after),
        out_specs=[column_block(rows) for rows, _, _ in outs] + [TOKEN_SPEC],
        out_shape=[jax.ShapeDtypeStruct((rows, wide_by), kind) for rows, wide_by, kind in outs]
        + [TOKEN],
        compiler_params=vmem(40),
        cost_estimate=cost(flops, 2 * sum(right.size for right in rights)),
    )(*lefts, *rights, *extras, *after)


def stacked(pieces, right, dim):
    parts = [contract(piece, right, 1, dim) for piece in pieces]
    return parts[0] if len(parts) == 1 else jnp.concatenate(parts, axis=0)


def own_and_other(total):
    rows = total.shape[0] // 2
    return [total[:rows], total[rows:]]


GELU_SCALE, GELU_CUBE = math.sqrt(2.0 / math.pi), 0.044715


def gelu(value):
    return 0.5 * value * (1.0 + jnp.tanh(GELU_SCALE * (value + GELU_CUBE * value**3)))


def gelu_slope(value):
    bend = jnp.tanh(GELU_SCALE * (value + GELU_CUBE * value**3))
    slope = GELU_SCALE * (1.0 + 3.0 * GELU_CUBE * value * value)
    return 0.5 * (1.0 + bend) + 0.5 * value * (1.0 - bend * bend) * slope


def meet_core():
    place = lax.axis_index(CONTEXT)
    other = {CONTEXT: place + 1 - 2 * (place % 2)}
    barrier = pltpu.get_barrier_semaphore()
    pl.semaphore_signal(barrier, inc=1, device_id=other, device_id_type=MESH)
    pl.semaphore_wait(barrier, 1)
    return other


def share_kernel(count, widths, *refs):
    sources, outs = refs[:count], refs[-count // 2 * widths - 4 :]
    targets, token_ref = outs[: count // 2 * widths], outs[-4]
    local_sem, send_sem, recv_sem = outs[-3:]
    mark(token_ref)
    place = lax.axis_index(CONTEXT)
    other = meet_core()
    copies = []
    for source_at in range(count):
        part, chip = source_at // 2, source_at % 2
        slot = (place + CHIP * chip) % 4
        for index in range(widths):
            sem = source_at * widths + index
            source = sources[source_at].at[:, index]
            target = targets[part * widths + index].at[:, slot]
            remote = pltpu.make_async_remote_copy(
                src_ref=source,
                dst_ref=target,
                send_sem=send_sem.at[sem],
                recv_sem=recv_sem.at[sem],
                device_id=other,
                device_id_type=MESH,
            )
            remote.start()
            own = pltpu.make_async_copy(source, target, local_sem.at[sem])
            own.start()
            copies += [remote, own]
    for copy in copies:
        copy.wait()


def share_core(pieces, after, ident):
    along, widths, rows, width = pieces[0].shape
    count = len(pieces)
    size = lax.axis_size(CONTEXT)
    total = count // 2 * widths
    shape = jax.ShapeDtypeStruct((along, size, rows, width), LOW)
    outs = pl.pallas_call(
        lambda *refs: share_kernel(count, widths, *refs),
        in_specs=[WHOLE] * count + [FREE] * len(after),
        out_specs=[IN_HBM] * total + [WHOLE],
        out_shape=[shape] * total + [TOKEN],
        scratch_shapes=[pltpu.SemaphoreType.DMA((count * widths,))] * 3,
        compiler_params=pltpu.CompilerParams(
            collective_id=ident, has_side_effects=True, vmem_limit_bytes=40 * MIB
        ),
        cost_estimate=cost(0, 6 * count * pieces[0].size * 2),
    )(*pieces, *after)
    held = [out.reshape(along * size * rows, width) for out in outs[:-1]]
    return [held[part * widths : (part + 1) * widths] for part in range(count // 2)], outs[-1]


def pack_of(shards):
    return jnp.stack([low(shard) for shard in shards], axis=0)


def gather_fsdp(shards, after):
    return lax.all_gather(gate(pack_of(shards), after), FSDP, axis=0, tiled=False)


def across(along, spread, after):
    along = gate(along, after) if after else along
    parts = [along, swap_context(along, CHIP)]
    if not spread:
        return parts
    if paired():
        first = swap_tensor(along)
        parts[1] = gate(parts[1], (first,))
        return parts + [first, swap_tensor(parts[1])]
    many = [lax.all_gather(part, TENSOR, axis=0) for part in parts]
    return [part[i] for i in range(lax.axis_size(TENSOR)) for part in many]


class Order:
    def __init__(self):
        self.after = ()
        self.count = 0

    def ident(self):
        self.count += 1
        return self.count - 1

    def need(self, *operands):
        self.after = self.after + operands

    def put(self, outs):
        *outs, token = outs
        self.after = (token,)
        return outs

    def multiply(self, body, lefts, rights, turned, extras, outs, tile=512):
        return self.put(multiply(body, lefts, rights, turned, extras, outs, self.after, tile))


def grad_kernel(which, spread, tile, counts, waits, *refs):
    count = sum(counts)
    lefts, rights = refs[:count], refs[count : count + len(which)]
    outs = refs[count + len(which) + waits :]
    kept, given = outs[: max(spread, 1)], outs[max(spread, 1) : 2 * max(spread, 1)]
    token_ref = outs[2 * max(spread, 1)]
    turned, cut, sent, came, send_sem, recv_sem = outs[2 * max(spread, 1) + 1 :]
    mark(token_ref)
    other = meet_core()
    place = lax.axis_index(CONTEXT)
    tiles = rights[0].shape[1] // tile
    rows = cut.shape[3]
    along = lax.axis_size(FSDP)
    block = rows // along
    for index, pieces in enumerate(counts):
        start = sum(counts[:index])
        depth = 0
        for left in lefts[start : start + pieces]:
            turned[:, depth : depth + left.shape[0]] = left[...].astype(jnp.float32).T
            depth += left.shape[0]
        for core in range(2):
            for chip in range(2):
                at = (place // 2 + chip) % 2 * 2 + (place % 2 + core) % 2
                pieces = [
                    turned[pl.ds(pl.multiple_of((4 * z + at) * block, 8), block), :]
                    for z in range(along)
                ]
                cut[index, core, chip] = low(jnp.concatenate(pieces, axis=0))
    units = []
    for job, left in enumerate(which):
        for chip in range(2):
            out = (kept, given)[chip]
            out = out[job % spread].at[job // spread] if spread else out[0].at[job]
            units.append((left, rights[job], chip, out))

    def columns(index):
        if isinstance(index, int):
            return pl.ds(index * tile, tile)
        return pl.ds(pl.multiple_of(index * tile, tile), tile)

    def copy(unit, index):
        sem = unit * tiles + index
        return pltpu.make_async_remote_copy(
            src_ref=sent.at[unit, index],
            dst_ref=came.at[unit, index],
            send_sem=send_sem.at[sem],
            recv_sem=recv_sem.at[sem],
            device_id=other,
            device_id_type=MESH,
        )

    def each(step):
        if tiles == 1:
            step(0)
        else:
            lax.fori_loop(0, tiles, lambda index, carry: (step(index), carry)[1], 0)

    for unit, (left, right, chip, out) in enumerate(units):

        def give(index, unit=unit, left=left, right=right, chip=chip):
            sent[unit, index] = low(contract(cut[left, 1, chip], right[:, columns(index)], 1, 0))
            copy(unit, index).start()

        each(give)
    for unit, (left, right, chip, out) in enumerate(units):

        def keep(index, unit=unit, left=left, right=right, chip=chip, out=out):
            term = contract(cut[left, 0, chip], right[:, columns(index)], 1, 0)
            copy(unit, index).wait_recv()
            out[:, columns(index)] = low(term + wide(came[unit, index]))

        each(keep)
    for unit in range(len(units)):

        def done(index, unit=unit):
            copy(unit, index).wait_send()

        each(done)


def grad_core(lefts, rights, which, spread, after, ident):
    depth, width = rights[0].shape
    counts = [len(pieces) for pieces in lefts]
    lefts = [piece for pieces in lefts for piece in pieces]
    features = lefts[0].shape[1]
    rows = features // 4
    jobs = len(which)
    count = max(spread, 1)
    tile = width
    for candidate in (512, 384):
        if width > 1408 and width % candidate == 0:
            tile = candidate
            break
    tiles = width // tile
    shape = jax.ShapeDtypeStruct((jobs // count, rows, width), LOW)
    outs = pl.pallas_call(
        lambda *refs: grad_kernel(which, spread, tile, counts, len(after), *refs),
        in_specs=[WHOLE] * (len(lefts) + jobs) + [FREE] * len(after),
        out_specs=[WHOLE] * (2 * count + 1),
        out_shape=[shape] * (2 * count) + [TOKEN],
        scratch_shapes=[
            pltpu.VMEM((features, depth), jnp.float32),
            pltpu.VMEM((len(counts), 2, 2, rows, depth), LOW),
            pltpu.VMEM((2 * jobs, tiles, rows, tile), LOW),
            pltpu.VMEM((2 * jobs, tiles, rows, tile), LOW),
            pltpu.SemaphoreType.DMA((2 * jobs * tiles,)),
            pltpu.SemaphoreType.DMA((2 * jobs * tiles,)),
        ],
        compiler_params=pltpu.CompilerParams(
            collective_id=ident, has_side_effects=True, vmem_limit_bytes=56 * MIB
        ),
        cost_estimate=cost(8 * jobs * rows * width * depth, 6 * jobs * width * rows),
    )(*lefts, *rights, *after)
    if spread:
        return list(outs[:count]), list(outs[count:-1]), outs[-1]
    return outs


def sum_parts(kept, given, order):
    if paired():
        pairs = [(kept[0], swap_tensor(kept[1])), (given[0], swap_tensor(given[1]))]
        return order.put(add_pairs(pairs, 0, order.after))
    return [
        lax.psum_scatter(jnp.stack(parts), TENSOR, scatter_dimension=0, tiled=False)
        for parts in (kept, given)
    ]


def sum_rest(kept, came, order):
    (total,) = order.put(add_pairs([(kept, came)], lax.axis_size(FSDP), order.after))
    return lax.psum_scatter(total, FSDP, scatter_dimension=0, tiled=False)


def sum_text(total):
    place = lax.axis_index(CONTEXT)
    steps = [
        (lambda operand: swap_context(operand, CORE), place % 2),
        (lambda operand: swap_context(operand, CHIP), place // 2),
    ]
    if paired():
        steps.append((swap_tensor, lax.axis_index(TENSOR)))
    for swap, bit in steps:
        half = total.shape[0] // 2
        kept = lax.dynamic_slice_in_dim(total, bit * half, half, axis=0)
        given = lax.dynamic_slice_in_dim(total, (1 - bit) * half, half, axis=0)
        total = low(wide(kept) + wide(swap(given)))
    if not paired():
        total = lax.psum(total, TENSOR)
    for swap, bit in reversed(steps):
        other = swap(total)
        first = bit == 0
        total = jnp.concatenate(
            [jnp.where(first, total, other), jnp.where(first, other, total)], axis=0
        )
    return total


def per_token(operand, rows):
    seqs, _, width = operand.shape
    return jnp.broadcast_to(operand, (seqs, rows // seqs, width)).reshape(rows, width)


def per_sequence(operand, seqs):
    return operand.reshape(seqs, -1, operand.shape[-1]).sum(axis=1)


def layer_forward(residual, skip_rows, modulation, text, tables, weights, order, steps):
    rows, features = residual.shape
    parts = lax.axis_size(TENSOR)
    every = rows * parts
    seqs = modulation[0].shape[0]
    shift_a, scale_a, gate_a, shift_m, scale_m, gate_m = [
        per_token(piece, rows) for piece in modulation
    ]
    cos, sin = tables
    kept = SimpleNamespace()
    kept.concat = jnp.concatenate([residual, wide(skip_rows)], axis=-1)
    kept.concat_low = low(layer_norm(kept.concat))
    width = weights.skip[0].shape[1]
    skipped = order.multiply(
        lambda lefts, rights, _: [contract(lefts[0], right, 1, 0) for right in rights],
        [kept.concat_low],
        weights.skip,
        False,
        [],
        [(rows, width, LOW)] * parts,
    )
    after_skip = wide(join_columns(skipped))
    kept.after_skip = after_skip
    kept.attn_all = gather_tensor(low(layer_norm(after_skip) * (1.0 + scale_a) + shift_a))
    steps.skipped()
    kept.query_raw, kept.key_raw, value_low = order.multiply(
        lambda lefts, rights, _: [stacked(lefts, right, 0) for right in rights],
        kept.attn_all,
        [weights.query, weights.key, weights.value],
        False,
        [],
        [(every, width, jnp.float32)] * 2 + [(every, width, LOW)],
    )
    blocks = (parts, seqs, rows // seqs, width)
    query_low, key_low = order.put(turn(kept.query_raw, kept.key_raw, cos, sin, order.after))
    kept.query_low = query_low.reshape(blocks)
    kept.keys = [part.reshape(blocks) for _, part in gather_context(key_low)]
    kept.values = [part.reshape(blocks) for _, part in gather_context(value_low)]
    steps.turned()
    attn_low, kept.attn_lse = attend(kept.query_low, kept.keys, kept.values, order.after)
    order.after = (kept.attn_lse,)
    kept.attn_low = attn_low.reshape(-1, width)
    terms = order.multiply(
        lambda lefts, rights, _: split_terms(contract(lefts[0], rights[0], 1, 1)),
        [kept.attn_low],
        [weights.attn_out],
        True,
        [],
        term_shapes(every, features),
    )
    kept.attn_branch = sum_tensor(terms)
    steps.attended()
    kept.after_attn = after_skip + gate_a * kept.attn_branch
    kept.cross_in = low(layer_norm(kept.after_attn))
    raws = order.multiply(
        lambda lefts, rights, _: [contract(lefts[0], right, 1, 0) for right in rights],
        [kept.cross_in],
        weights.cross_query,
        False,
        [],
        [(rows, width, jnp.float32)] * parts,
    )
    kept.cross_raw = [raw.reshape(blocks[1:]) for raw in raws]
    kept.cross_low = []
    for raw, key, value in zip(kept.cross_raw, text.keys, text.values):
        (out,) = order.put(cross(raw, key, value, text.count, order.after))
        kept.cross_low.append(out.reshape(rows, width))
    (kept.after_cross,) = order.multiply(
        lambda lefts, rights, extras: [
            sum((contract(left, right, 1, 1) for left, right in zip(lefts, rights)), extras[0])
        ],
        kept.cross_low,
        weights.cross_out,
        True,
        [kept.after_attn],
        [(rows, features, jnp.float32)],
    )
    after_cross = kept.after_cross
    kept.mlp_all = gather_tensor(low(layer_norm(after_cross) * (1.0 + scale_m) + shift_m))
    steps.crossed()

    def raise_and_bend(lefts, rights, _):
        upward = stacked(lefts, rights[0], 0)
        return [upward, gelu(upward)]

    hidden = weights.up.shape[1]
    kept.upward, kept.hidden_low = order.multiply(
        raise_and_bend,
        kept.mlp_all,
        [weights.up],
        False,
        [],
        [(every, hidden, jnp.float32), (every, hidden, LOW)],
    )
    steps.raised()
    terms = order.multiply(
        lambda lefts, rights, _: split_terms(contract(lefts[0], rights[0], 1, 1)),
        [kept.hidden_low],
        [weights.down],
        True,
        [],
        term_shapes(every, features),
    )
    kept.mlp_branch = sum_tensor(terms)
    steps.lowered()
    return after_cross + gate_m * kept.mlp_branch, kept


def layer_backward(grad_res, kept, weights, modulation, tables, text, text_low, order, earlier):
    rows, features = grad_res.shape
    parts = lax.axis_size(TENSOR)
    every = rows * parts
    seqs = modulation[0].shape[0]
    shift_a, scale_a, gate_a, shift_m, scale_m, gate_m = [
        per_token(piece, rows) for piece in modulation
    ]
    cos, sin = tables
    reduced = SimpleNamespace()

    def product(lefts, rights, which, spread):
        outs = order.put(grad_core(lefts, rights, which, spread, order.after, order.ident()))
        return outs if spread else (outs[0], swap_context(outs[1], CHIP))

    mlp_grad = gather_tensor(low(gate_m * grad_res))
    earlier.start()
    grad_gate_m = per_sequence(grad_res * kept.mlp_branch, seqs)
    (up_grad,) = order.multiply(
        lambda lefts, rights, extras: [stacked(lefts, rights[0], 0) * gelu_slope(extras[0])],
        mlp_grad,
        [weights.down],
        False,
        [kept.upward],
        [(every, kept.upward.shape[1], LOW)],
    )
    terms = order.multiply(
        lambda lefts, rights, _: split_terms(contract(lefts[0], rights[0], 1, 1)),
        [up_grad],
        [weights.up],
        True,
        [],
        term_shapes(every, features),
    )
    mlp_in_grad = sum_tensor(terms)
    order.need(*earlier.sums())
    down = product([mlp_grad], [kept.hidden_low], (0,), 0)
    earlier.first()
    up = product([kept.mlp_all], [up_grad], (0,), 0)
    grad_shift_m = per_sequence(mlp_in_grad, seqs)
    grad_scale_m = per_sequence(mlp_in_grad * layer_norm(kept.after_cross), seqs)
    grad_res = grad_res + layer_norm_back(kept.after_cross, mlp_in_grad * (1.0 + scale_m))

    cross_grad = low(grad_res)
    width = weights.cross_out[0].shape[1]
    out_grads = order.multiply(
        lambda lefts, rights, _: [contract(lefts[0], right, 1, 0) for right in rights],
        [cross_grad],
        weights.cross_out,
        False,
        [],
        [(rows, width, LOW)] * parts,
    )
    cross_q, text_key_grad, text_value_grad = [], [], []
    for part, out_grad in enumerate(out_grads):
        raw = kept.cross_raw[part]
        query_grad, key_grad, value_grad = order.put(
            cross_back(
                raw,
                text.raws[part],
                text.keys[part],
                text.values[part],
                out_grad.reshape(raw.shape),
                text.count,
                order.after,
            )
        )
        cross_q.append(query_grad.reshape(rows, width))
        text_key_grad.append(key_grad.reshape(-1, width))
        text_value_grad.append(value_grad.reshape(-1, width))
    (cross_in_grad,) = order.multiply(
        lambda lefts, rights, _: [
            sum(contract(left, right, 1, 1) for left, right in zip(lefts, rights))
        ],
        cross_q,
        weights.cross_query,
        True,
        [],
        [(rows, features, jnp.float32)],
    )
    grad_res = grad_res + layer_norm_back(kept.after_attn, cross_in_grad)

    attn_grad = gather_tensor(low(gate_a * grad_res))
    earlier.second()
    grad_gate_a = per_sequence(grad_res * kept.attn_branch, seqs)
    crossed = product(
        [[cross_grad], [kept.cross_in]],
        kept.cross_low + cross_q,
        (0,) * parts + (1,) * parts,
        parts,
    )
    texts = product([[text_low]], text_key_grad + text_value_grad, (0,) * (2 * parts), parts)
    (out_grad,) = order.multiply(
        lambda lefts, rights, _: [stacked(lefts, rights[0], 0)],
        attn_grad,
        [weights.attn_out],
        False,
        [],
        [(every, width, LOW)],
    )
    blocks = kept.query_low.shape
    order.need(*earlier.more())
    query_grad, key_parts, value_parts = order.put(
        attend_back(
            kept.query_low,
            kept.query_raw.reshape(blocks),
            out_grad.reshape(blocks),
            kept.attn_lse,
            cos.reshape(blocks),
            sin.reshape(blocks),
            kept.keys,
            kept.values,
            order.after,
        )
    )
    query_grad = query_grad.reshape(-1, width)

    key_parts, value_parts = [
        [piece.reshape(1, -1, width) for piece in pieces] for pieces in (key_parts, value_parts)
    ]
    near = [
        (pieces[place], swap_context(pieces[place + 2], CORE))
        for pieces in (key_parts, value_parts)
        for place in range(2)
    ]
    reduced.down = sum_rest(*down, order)
    key_near, key_far, value_near, value_far = order.put(add_pairs(near, 0, order.after))
    whole = [
        (key_near, swap_context(key_far, CHIP)),
        (value_near, swap_context(value_far, CHIP)),
    ]
    reduced.up = sum_rest(*up, order)
    (text_part,) = order.multiply(
        lambda lefts, rights, _: [
            sum(contract(left, right, 1, 1) for left, right in zip(lefts, rights))
        ],
        text_key_grad + text_value_grad,
        weights.text_key + weights.text_value,
        True,
        [],
        [(text_low.shape[0], text_low.shape[1], jnp.float32)],
        256,
    )
    crossed = sum_parts(*crossed, order)
    earlier.third()
    key_grad, value_grad = order.put(add_pairs(whole, 0, order.after))
    crossed = (crossed[0], swap_context(gate(crossed[1], order.after), CHIP))
    (key_grad,) = order.put(turn_back(key_grad[0], kept.key_raw, cos, sin, order.after))
    value_grad = value_grad[0]
    terms = order.multiply(
        lambda lefts, rights, _: split_terms(
            sum(contract(left, right, 1, 1) for left, right in zip(lefts, rights))
        ),
        [query_grad, key_grad, value_grad],
        [weights.query, weights.key, weights.value],
        True,
        [],
        term_shapes(every, features),
    )
    attn_in_grad = sum_tensor(terms)
    attended = product(
        [attn_grad, kept.attn_all],
        [kept.attn_low, query_grad, key_grad, value_grad],
        (0, 1, 1, 1),
        0,
    )
    texts = sum_parts(*texts, order)
    texts = (texts[0], swap_context(texts[1], CHIP))
    grad_shift_a = per_sequence(attn_in_grad, seqs)
    grad_scale_a = per_sequence(attn_in_grad * layer_norm(kept.after_skip), seqs)
    grad_res = grad_res + layer_norm_back(kept.after_skip, attn_in_grad * (1.0 + scale_a))

    skip_grad = columns_of(low(grad_res))
    (concat_grad,) = order.multiply(
        lambda lefts, rights, _: [
            sum(contract(left, right, 1, 1) for left, right in zip(lefts, rights))
        ],
        skip_grad,
        weights.skip,
        True,
        [],
        [(rows, 2 * features, jnp.float32)],
    )
    later = SimpleNamespace()

    def start():
        later.skipped = product([[kept.concat_low]], skip_grad, (0,) * parts, parts)
        reduced.cross = sum_rest(*crossed, order)

    def first():
        reduced.attention = sum_rest(*attended, order)

    def second():
        reduced.text = sum_rest(*texts, order)
        kept, given = sum_parts(*later.skipped, order)
        later.skipped = (kept, swap_context(given, CHIP))

    def third():
        reduced.skip = sum_rest(*later.skipped, order)

    later.start, later.first, later.second, later.third = start, first, second, third
    concat_grad = layer_norm_back(kept.concat, concat_grad)
    mod_grad = jnp.concatenate(
        [grad_shift_a, grad_scale_a, grad_gate_a, grad_shift_m, grad_scale_m, grad_gate_m], axis=-1
    )
    mod_columns = columns_of(mod_grad)
    if paired():
        mod_columns = mod_columns[0] + swap_tensor(mod_columns[1])
    else:
        mod_columns = lax.psum_scatter(
            jnp.stack(mod_columns), TENSOR, scatter_dimension=0, tiled=False
        )
    mod_all = gather_fsdp_small(sum_context(mod_columns))
    mod_all = mod_all.reshape(-1, mod_all.shape[-1])
    later.sums = lambda: (reduced.down, reduced.up)
    later.more = lambda: (reduced.cross, reduced.attention)
    return concat_grad[:, :features], concat_grad[:, features:], mod_all, text_part, reduced, later


def shards(
    latents,
    skip_inputs,
    text_states,
    condition,
    positions,
    cotangent,
    *tensors,
):
    masters, momenta, averages = tensors[:7], tensors[7:14], tensors[14:]
    (
        skip_weight,
        mod_weight,
        proj_weight,
        output_weight,
        text_weight,
        up_weight,
        down_weight,
    ) = masters
    layers = skip_weight.shape[0]
    along = lax.axis_size(FSDP)
    size = lax.axis_size(CONTEXT)
    parts = lax.axis_size(TENSOR)
    seqs, tokens = latents.shape[0], latents.shape[1]
    text_count = text_states.shape[1]
    every = range(layers)

    def cross_of(layer):
        return [proj_weight[layer, :, 3], output_weight[layer, 1].T]

    def attention_of(layer):
        return [proj_weight[layer, :, j] for j in range(3)] + [output_weight[layer, 0].T]

    order = Order()
    weights = [SimpleNamespace() for _ in every]
    skip_along = gather_fsdp_small(pack_of([skip_weight[0]]))
    arrived = (skip_along,)
    skip_parts = across(skip_along, True, ())
    started = (skip_parts[1],)
    cross_along = [gather_fsdp_small(gate(pack_of(cross_of(0)), arrived))]
    skips = [skip_along]
    for layer in every[1:]:
        skips.append(gather_fsdp_small(gate(pack_of([skip_weight[layer]]), started)))
        cross_along.append(gather_fsdp_small(gate(pack_of(cross_of(layer)), started)))
    attention = [gather_fsdp(attention_of(0), arrived)]
    text_along = gather_fsdp([text_weight[i, :, j] for i in every for j in range(2)], arrived)
    ups = [gather_fsdp([up_weight[0]], arrived)]
    downs = [gather_fsdp([down_weight[0].T], arrived)]
    for layer in every[1:]:
        attention.append(gather_fsdp(attention_of(layer), started))
        ups.append(gather_fsdp([up_weight[layer]], started))
        downs.append(gather_fsdp([down_weight[layer].T], started))

    attention_parts, cross_parts, up_parts, down_parts = {}, {}, {}, {}
    skip_parts = {0: skip_parts}

    def hold_skip(layer):
        (held,) = order.put(share_core(skip_parts[layer], order.after, order.ident()))
        weights[layer].skip = [part[0] for part in held]

    def hold_attention(layer):
        (held,) = order.put(share_core(attention_parts[layer], order.after, order.ident()))
        place = weights[layer]
        place.query, place.key, place.value, place.attn_out = held[0]

    def hold_cross(layer):
        (held,) = order.put(share_core(cross_parts[layer], order.after, order.ident()))
        weights[layer].cross_query = [part[0] for part in held]
        weights[layer].cross_out = [part[1] for part in held]

    def hold_up(layer):
        (held,) = order.put(share_core(up_parts[layer], order.after, order.ident()))
        weights[layer].up = held[0][0]

    def hold_down(layer):
        (held,) = order.put(share_core(down_parts[layer], order.after, order.ident()))
        weights[layer].down = held[0][0]

    padded = -(-text_count // 128) * 128
    text_low = jnp.pad(text_states, ((0, 0), (0, padded - text_count), (0, 0)))
    text_low = text_low.reshape(seqs * padded, -1)
    texts = [SimpleNamespace(count=text_count) for _ in every]

    def hold_text():
        (held,) = order.put(share_core(text_parts[0], order.after, order.ident()))
        for layer in every:
            weights[layer].text_key = [part[2 * layer] for part in held]
            weights[layer].text_value = [part[2 * layer + 1] for part in held]

    def read_text(layer):
        text = texts[layer]
        place = weights[layer]
        width = place.text_key[0].shape[1]
        outs = order.multiply(
            lambda lefts, rights, _: [contract(lefts[0], right, 1, 0) for right in rights],
            [text_low],
            place.text_key + place.text_value,
            False,
            [],
            [(seqs * padded, width, jnp.float32)] * parts + [(seqs * padded, width, LOW)] * parts,
            256,
        )
        blocks = (seqs, padded, width)
        keys = [order.put(root(raw, order.after))[0] for raw in outs[:parts]]
        text.raws = [raw.reshape(blocks) for raw in outs[:parts]]
        text.keys = [key.reshape(blocks) for key in keys]
        text.values = [value.reshape(blocks) for value in outs[parts:]]

    text_parts = {}
    attention_parts[0] = across(attention[0], False, (skip_parts[0][-1],))
    order.need(cross_along[0])
    hold_skip(0)

    def steps_of(layer):
        steps = SimpleNamespace()
        coming = layer + 1 if layer + 1 < layers else None

        def skipped():
            if not layer:
                text_parts[0] = across(text_along, True, order.after)
            hold_attention(layer)

        def turned():
            if layer:
                read_text(layer)
            else:
                cross_parts[layer] = across(cross_along[layer], True, order.after)

        def attended():
            if layer:
                down_parts[layer] = across(downs[layer], False, order.after)
                hold_up(layer)
            else:
                up_parts[layer] = across(ups[layer], False, order.after)
                hold_text()
                down_parts[layer] = across(downs[layer], False, order.after)
                read_text(layer)
                if coming:
                    order.need(skips[coming])
            hold_cross(layer)
            if coming:
                skip_parts[coming] = across(skips[coming], True, order.after)

        def crossed():
            if not layer:
                hold_up(layer)
            if coming:
                attention_parts[coming] = across(attention[coming], False, order.after)
                order.need(cross_along[coming])

        def raised():
            hold_down(layer)
            if coming:
                cross_parts[coming] = across(cross_along[coming], True, order.after)

        def lowered():
            if coming:
                hold_skip(coming)
                up_parts[coming] = across(ups[coming], False, order.after)

        steps.skipped, steps.turned, steps.attended = skipped, turned, attended
        steps.crossed, steps.raised, steps.lowered = crossed, raised, lowered
        return steps

    cond_float = wide(condition)
    cond_silu, silu_pull = jax.vjp(jax.nn.silu, cond_float)
    cond_all = gather_fsdp_small(low(cond_silu)).reshape(along * seqs, cond_float.shape[1])
    rows = mod_weight.shape[1]
    place = lax.axis_index(FSDP) * size + lax.axis_index(CONTEXT)
    cond_rows = lax.dynamic_slice_in_dim(cond_all, place * rows, rows, axis=1)
    mod_low = low(mod_weight)
    mod_part = contract(cond_rows, mod_low, 1, 1)
    mod_part = gate(mod_part, arrived).reshape((along, seqs) + mod_part.shape[1:])
    mod_part = sum_fsdp_small(mod_part)
    mod_part = low(sum_context(gate(mod_part, (skip_parts[0][-1],))))
    if paired():
        mod_full = tensor_order(mod_part, swap_tensor(mod_part), -1)
    else:
        mod_full = lax.all_gather(mod_part, TENSOR, axis=2, tiled=True)
    modulations = [
        jnp.split(wide(mod_full[:, layer])[:, None, :], 6, axis=-1) for layer in every
    ]

    quarter = HD // 4
    frequency = ROPE_BASE ** (-jnp.arange(quarter, dtype=jnp.float32) / quarter)
    grid = positions.reshape(seqs, 2, parts, tokens)
    if paired():
        mine = lax.axis_index(TENSOR)
        grid = jnp.concatenate(
            [
                lax.dynamic_slice_in_dim(grid, mine, 1, axis=2),
                lax.dynamic_slice_in_dim(grid, 1 - mine, 1, axis=2),
            ],
            axis=2,
        )
    grid = wide(grid.transpose(2, 0, 3, 1).reshape(parts * seqs * tokens, 2))
    row_angle = grid[:, :1] * frequency
    col_angle = grid[:, 1:] * frequency
    cos = jnp.concatenate([jnp.cos(row_angle)] * 2 + [jnp.cos(col_angle)] * 2, axis=-1)
    sin = jnp.concatenate(
        [-jnp.sin(row_angle), jnp.sin(row_angle), -jnp.sin(col_angle), jnp.sin(col_angle)], axis=-1
    )
    tables = spread_heads(cos, sin, proj_weight.shape[-1])

    own = (seqs * tokens, latents.shape[-1])
    residual = wide(latents).reshape(own)
    stored = []
    for layer in every:
        residual, kept = layer_forward(
            residual,
            skip_inputs[layer].reshape(own),
            modulations[layer],
            texts[layer],
            tables,
            weights[layer],
            order,
            steps_of(layer),
        )
        stored.append(kept)
    block_output = low(residual).reshape(latents.shape)

    grad_res = wide(cotangent).reshape(own)
    cond_total = 0.0
    text_total = 0.0
    skip_grads = [None] * layers
    gradients = [None] * layers
    later = SimpleNamespace(
        start=lambda: None, first=lambda: None, second=lambda: None, third=lambda: None, sums=lambda: (), more=lambda: ()
    )
    for layer in reversed(every):
        grad_res, skip_grads[layer], mod_all, text_part, reduced, later = layer_backward(
            grad_res,
            stored[layer],
            weights[layer],
            modulations[layer],
            tables,
            texts[layer],
            text_low,
            order,
            later,
        )
        reduced.mod = jnp.einsum("bk,bc->kc", wide(cond_rows), mod_all, precision=PRECISE)
        cond_total = cond_total + jnp.einsum(
            "bc,kc->bk", mod_all, wide(mod_low[layer]), precision=PRECISE
        )
        text_total = text_total + text_part
        gradients[layer] = reduced
    later.start()
    later.first()
    later.second()
    later.third()
    gradients = [
        (
            wide(each.skip[0]),
            each.mod,
            wide(jnp.concatenate([each.attention[1:], each.cross[1:]], axis=0)).transpose(1, 0, 2),
            wide(jnp.stack([each.attention[0], each.cross[0]], axis=0)).transpose(0, 2, 1),
            wide(each.text).transpose(1, 0, 2),
            wide(each.up[0]),
            wide(each.down[0]).T,
        )
        for each in gradients
    ]
    text_sum = sum_text(low(text_total))
    text_sum = wide(text_sum).reshape(seqs, padded, -1)[:, :text_count]
    if paired():
        cond_total = cond_total + swap_tensor(cond_total)
    else:
        cond_total = lax.psum(cond_total, TENSOR)
    sent = cond_total.reshape(along, seqs, rows)
    here = lax.axis_index(FSDP)
    cond_sum = jnp.zeros((along, size, seqs, rows), jnp.float32)
    for step in range(along):
        part = lax.dynamic_index_in_dim(sent, (here + step) % along, 0, keepdims=False)
        if step:
            part = shift_fsdp(part, step)
        for offset, piece in gather_context(part):
            cond_sum = lax.dynamic_update_slice(
                cond_sum,
                piece[None, None],
                ((here - step + along) % along, lax.axis_index(CONTEXT) ^ offset, 0, 0),
            )
    cond_sum = cond_sum.transpose(2, 0, 1, 3).reshape(seqs, along * size * rows)
    condition_grad = silu_pull(cond_sum)[0]
    skips_grad = jnp.stack(skip_grads, axis=0).reshape(skip_inputs.shape)

    spreads = (
        (2 * D) ** (-0.5),
        D ** (-0.5),
        D ** (-0.5),
        (D // 16) ** (-0.5),
        DT ** (-0.5),
        D ** (-0.5),
        FF ** (-0.5),
    )
    tokens_total = seqs * along * tokens * size * parts
    new_weights = []
    new_momenta = []
    new_averages = []
    for index in range(len(masters)):
        gradient = jnp.stack([gradients[layer][index] for layer in every], axis=0)
        rate = RATE_FACTOR * spreads[index] / math.sqrt(tokens_total)
        moment_new = MOMENTUM * momenta[index] + gradient
        weight_new = masters[index] - rate * (gradient + MOMENTUM * moment_new)
        new_weights.append(weight_new)
        new_momenta.append(moment_new)
        new_averages.append(
            AVERAGE_DECAY * averages[index] + (1.0 - AVERAGE_DECAY) * weight_new
        )
    return (
        block_output,
        grad_res.reshape(latents.shape),
        skips_grad,
        text_sum,
        condition_grad,
        *new_weights,
        *new_momenta,
        *new_averages,
    )


def solution(mesh):
    weight_specs = (
        P(None, (FSDP, CONTEXT), TENSOR),
        P(None, (FSDP, CONTEXT), TENSOR),
        P(None, (FSDP, CONTEXT), None, TENSOR),
        P(None, None, TENSOR, (FSDP, CONTEXT)),
        P(None, (FSDP, CONTEXT), None, TENSOR),
        P(None, (FSDP, CONTEXT), TENSOR),
        P(None, TENSOR, (FSDP, CONTEXT)),
    )
    in_specs = (
        P(FSDP, (CONTEXT, TENSOR), None),
        P(None, FSDP, (CONTEXT, TENSOR), None),
        P(FSDP, None, None),
        P(FSDP, None),
        P(FSDP, None, CONTEXT),
        P(FSDP, (CONTEXT, TENSOR), None),
    ) + weight_specs * 3
    out_specs = (
        P(FSDP, (CONTEXT, TENSOR), None),
        P(FSDP, (CONTEXT, TENSOR), None),
        P(None, FSDP, (CONTEXT, TENSOR), None),
        P(FSDP, None, None),
        P(FSDP, None),
    ) + weight_specs * 3
    return jax.shard_map(shards, mesh=mesh, in_specs=in_specs, out_specs=out_specs, check_vma=False)
```

```python
import math
from types import SimpleNamespace
import jax
import jax.numpy as jnp
from jax import lax
from jax.experimental import pallas as pl
from jax.experimental.pallas import tpu as pltpu
from jax.sharding import PartitionSpec as P

HD = 88
EPSILON = 1e-06
SCORE_SCALE = 1.0 / math.sqrt(HD)
LOW = jnp.bfloat16
MIB = 1 << 20


def vmem(mebibytes):
    return pltpu.CompilerParams(vmem_limit_bytes=mebibytes * MIB)


TOKEN = jax.ShapeDtypeStruct((8, 128), jnp.float32)
TOKEN_SPEC = pl.BlockSpec((8, 128), lambda *place: (0, 0))
FREE = pl.BlockSpec(memory_space=pl.ANY)
IN_HBM = pl.BlockSpec(memory_space=pltpu.HBM)
WHOLE = pl.BlockSpec(memory_space=pltpu.VMEM)


def cost(flops, moved, transcendentals=0):
    share = 1000
    return pl.CostEstimate(
        flops=flops // share,
        bytes_accessed=moved // share,
        transcendentals=transcendentals // share,
    )


def mark(token_ref):
    token_ref[...] = jnp.zeros(token_ref.shape, jnp.float32)


def gate(operand, after):
    return pl.pallas_call(
        lambda *refs: None,
        in_specs=[IN_HBM] + [IN_HBM] * len(after),
        out_specs=IN_HBM,
        out_shape=jax.ShapeDtypeStruct(operand.shape, operand.dtype),
        input_output_aliases={0: 0},
    )(operand, *after)


def contract(left, right, left_dim, right_dim):
    return lax.dot_general(
        left, right, (((left_dim,), (right_dim,)), ((), ())), preferred_element_type=jnp.float32
    )


def head(operand, index):
    return operand[:, index * HD : (index + 1) * HD]


def head_marks(width):
    heads = width // HD
    column = lax.broadcasted_iota(jnp.int32, (width, heads), 0)
    first = lax.broadcasted_iota(jnp.int32, (width, heads), 1) * HD
    return jnp.where((column >= first) & (column < first + HD), 1.0, 0.0).astype(LOW)


def halves(operand):
    upper = operand.astype(LOW)
    return upper, (operand - upper.astype(jnp.float32)).astype(LOW)


def head_mean(operand, marks):
    return contract(operand.astype(LOW), marks, 1, 0) / HD


def to_columns(operand, marks):
    upper, lower = halves(operand)
    return contract(upper, marks, 1, 1) + contract(lower, marks, 1, 1)


def root_factor(operand, marks):
    return to_columns(lax.rsqrt(head_mean(operand * operand, marks) + EPSILON), marks)


def root_back(operand, upstream, marks):
    factor = root_factor(operand, marks)
    normed = operand * factor
    mean = head_mean(upstream * normed, marks).astype(LOW)
    return factor * (upstream - normed * contract(mean, marks, 1, 1))


def swap_quarters(operand):
    quarter = HD // 4
    column = lax.broadcasted_iota(jnp.int32, operand.shape, 1)
    left = jnp.concatenate([operand[:, quarter:], operand[:, :quarter]], axis=-1)
    right = jnp.concatenate([operand[:, -quarter:], operand[:, :-quarter]], axis=-1)
    return jnp.where(column % (2 * quarter) < quarter, left, right)


def turn_kernel(query_ref, key_ref, cos_ref, sin_ref, *refs):
    query_out, key_out, token_ref = refs[-3:]
    mark(token_ref)
    cos, sin = cos_ref[...], sin_ref[...]
    marks = head_marks(cos.shape[1])
    for source, target in ((query_ref, query_out), (key_ref, key_out)):
        value = source[...]
        value = value * root_factor(value, marks)
        target[...] = (value * cos + swap_quarters(value) * sin).astype(LOW)


def row_blocks(operand):
    rows, width = operand.shape
    return pl.BlockSpec((min(rows, 128), width), lambda i: (i, 0))


def turn(query_raw, key_raw, cos, sin, after):
    rows, width = query_raw.shape
    spec = row_blocks(query_raw)
    shape = jax.ShapeDtypeStruct((rows, width), LOW)
    return pl.pallas_call(
        turn_kernel,
        grid=(rows // min(rows, 128),),
        in_specs=[spec] * 4 + [IN_HBM] * len(after),
        out_specs=[spec, spec, TOKEN_SPEC],
        out_shape=[shape, shape, TOKEN],
        compiler_params=vmem(32),
        cost_estimate=cost(100 * rows * width, 20 * rows * width),
    )(query_raw, key_raw, cos, sin, *after)


def turn_back_kernel(grad_ref, raw_ref, cos_ref, sin_ref, *refs):
    out_ref, token_ref = refs[-2:]
    mark(token_ref)
    cos, sin = cos_ref[...], sin_ref[...]
    grad = grad_ref[...].astype(jnp.float32)
    grad = grad * cos - swap_quarters(grad) * sin
    out_ref[...] = root_back(raw_ref[...], grad, head_marks(cos.shape[1])).astype(LOW)


def turn_back(grad, raw, cos, sin, after):
    rows, width = raw.shape
    spec = row_blocks(raw)
    return pl.pallas_call(
        turn_back_kernel,
        grid=(rows // min(rows, 128),),
        in_specs=[spec] * 4 + [IN_HBM] * len(after),
        out_specs=[spec, TOKEN_SPEC],
        out_shape=[jax.ShapeDtypeStruct((rows, width), LOW), TOKEN],
        compiler_params=vmem(32),
        cost_estimate=cost(100 * rows * width, 16 * rows * width),
    )(grad, raw, cos, sin, *after)


def root_kernel(raw_ref, *refs):
    out_ref, token_ref = refs[-2:]
    mark(token_ref)
    raw = raw_ref[...]
    out_ref[...] = (raw * root_factor(raw, head_marks(raw.shape[1]))).astype(LOW)


def root(raw, after):
    rows, width = raw.shape
    spec = row_blocks(raw)
    return pl.pallas_call(
        root_kernel,
        grid=(rows // min(rows, 128),),
        in_specs=[spec] + [IN_HBM] * len(after),
        out_specs=[spec, TOKEN_SPEC],
        out_shape=[jax.ShapeDtypeStruct((rows, width), LOW), TOKEN],
        compiler_params=vmem(32),
        cost_estimate=cost(50 * rows * width, 6 * rows * width),
    )(raw, *after)


def flat(ref):
    value = ref[...]
    return value.reshape(value.shape[0] * value.shape[2], value.shape[3])


def attend_kernel(count, query_ref, *refs):
    keys, values = refs[:count], refs[count : 2 * count]
    out_ref, lse_ref = refs[-2:]
    query = flat(query_ref)
    keys = [flat(ref) for ref in keys]
    values = [flat(ref) for ref in values]
    pieces = []
    for index in range(query.shape[1] // HD):
        query_head = head(query, index)
        scores = [contract(head(key, index), query_head, 1, 1) for key in keys]
        peak = scores[0].max(axis=0, keepdims=True)
        for score in scores[1:]:
            peak = jnp.maximum(peak, score.max(axis=0, keepdims=True))
        mass = 0.0
        out = 0.0
        for score, value in zip(scores, values):
            weight = jnp.exp((score - peak) * SCORE_SCALE)
            mass = mass + weight.sum(axis=0, keepdims=True)
            out = out + contract(head(value, index), weight.astype(LOW), 0, 0)
        pieces.append((out / mass).T.astype(LOW))
        lse_ref[0, index : index + 1, :] = peak * SCORE_SCALE + jnp.log(mass)
    out_ref[...] = jnp.concatenate(pieces, axis=-1).reshape(out_ref.shape)


def block_of(operand):
    parts, _, tokens, width = operand.shape
    return pl.BlockSpec((parts, 1, tokens, width), lambda s: (0, s, 0, 0))


def attend(query, keys, values, after):
    parts, seqs, tokens, width = query.shape
    heads = width // HD
    count = len(keys)
    pairs = seqs * heads * (parts * tokens) ** 2 * count
    return pl.pallas_call(
        lambda *refs: attend_kernel(count, *refs),
        grid=(seqs,),
        in_specs=[block_of(query)] * (1 + 2 * count) + [IN_HBM] * len(after),
        out_specs=[
            block_of(query),
            pl.BlockSpec((1, heads, parts * tokens), lambda s: (s, 0, 0)),
        ],
        out_shape=[
            jax.ShapeDtypeStruct(query.shape, LOW),
            jax.ShapeDtypeStruct((seqs, heads, parts * tokens), jnp.float32),
        ],
        compiler_params=vmem(48),
        cost_estimate=cost(8 * pairs * 128, 20 * query.size, pairs),
    )(query, *keys, *values, *after)


def attend_back_kernel(count, query_ref, raw_ref, grad_ref, lse_ref, cos_ref, sin_ref, *refs):
    key_refs, value_refs = refs[:count], refs[count : 2 * count]
    outs = refs[-2 * count - 2 :]
    query_out, key_outs, value_outs = outs[0], outs[1 : count + 1], outs[count + 1 : -1]
    mark(outs[-1])
    query, raw, grad = flat(query_ref), flat(raw_ref), flat(grad_ref)
    cos, sin = flat(cos_ref), flat(sin_ref)
    keys = [flat(ref) for ref in key_refs]
    values = [flat(ref) for ref in value_refs]
    query_pieces = []
    key_pieces = [[] for _ in keys]
    value_pieces = [[] for _ in keys]
    for index in range(query.shape[1] // HD):
        query_head, grad_head = head(query, index), head(grad, index)
        lse = lse_ref[0, index : index + 1, :]
        weights = []
        weight_grads = []
        delta = 0.0
        for key, value in zip(keys, values):
            weight = jnp.exp(contract(head(key, index), query_head, 1, 1) * SCORE_SCALE - lse)
            weight_grad = contract(head(value, index), grad_head, 1, 1)
            delta = delta + (weight * weight_grad).sum(axis=0, keepdims=True)
            weights.append(weight)
            weight_grads.append(weight_grad)
        query_grad = 0.0
        for place, key in enumerate(keys):
            weight = weights[place]
            score_grad = (weight * (weight_grads[place] - delta)).astype(LOW)
            query_grad = query_grad + contract(head(key, index), score_grad, 0, 0)
            key_pieces[place].append(
                (contract(score_grad, query_head, 1, 0) * SCORE_SCALE).astype(LOW)
            )
            value_pieces[place].append(contract(weight.astype(LOW), grad_head, 1, 0).astype(LOW))
        query_pieces.append(query_grad.T * SCORE_SCALE)
    query_grad = jnp.concatenate(query_pieces, axis=-1)
    query_grad = query_grad * cos - swap_quarters(query_grad) * sin
    query_grad = root_back(raw, query_grad, head_marks(raw.shape[1]))
    query_out[...] = query_grad.astype(LOW).reshape(query_out.shape)
    for target, pieces in zip(key_outs, key_pieces):
        target[...] = jnp.concatenate(pieces, axis=-1).reshape(target.shape)
    for target, pieces in zip(value_outs, value_pieces):
        target[...] = jnp.concatenate(pieces, axis=-1).reshape(target.shape)


def attend_back(query, raw, grad, lse, cos, sin, keys, values, after):
    parts, seqs, tokens, width = query.shape
    heads = width // HD
    count = len(keys)
    pairs = seqs * heads * (parts * tokens) ** 2 * count
    shape = jax.ShapeDtypeStruct(query.shape, LOW)
    spec = block_of(query)
    outs = pl.pallas_call(
        lambda *refs: attend_back_kernel(count, *refs),
        grid=(seqs,),
        in_specs=[
            spec,
            spec,
            spec,
            pl.BlockSpec((1, heads, parts * tokens), lambda s: (s, 0, 0)),
            block_of(cos),
            block_of(sin),
        ]
        + [spec] * (2 * count)
        + [IN_HBM] * len(after),
        out_specs=[spec] * (1 + 2 * count) + [TOKEN_SPEC],
        out_shape=[shape] * (1 + 2 * count) + [TOKEN],
        compiler_params=vmem(56),
        cost_estimate=cost(20 * pairs * 128, 40 * query.size, pairs),
    )(query, raw, grad, lse, cos, sin, *keys, *values, *after)
    return outs[0], list(outs[1 : 1 + count]), list(outs[1 + count : -1]), outs[-1]


def text_probs(query, key, index, count):
    scores = contract(head(key, index), head(query, index), 1, 1) * SCORE_SCALE
    inside = lax.broadcasted_iota(jnp.int32, scores.shape, 0) < count
    scores = jnp.where(inside, scores, -1e30)
    weight = jnp.exp(scores - scores.max(axis=0, keepdims=True))
    return weight / weight.sum(axis=0, keepdims=True)


def cross_kernel(count, raw_ref, key_ref, value_ref, *refs):
    out_ref, token_ref = refs[-2:]
    mark(token_ref)
    raw, key, value = raw_ref[0], key_ref[0], value_ref[0]
    query = (raw * root_factor(raw, head_marks(raw.shape[1]))).astype(LOW)
    pieces = []
    for index in range(value.shape[1] // HD):
        probs = text_probs(query, key, index, count)
        pieces.append(contract(head(value, index), probs.astype(LOW), 0, 0).T.astype(LOW))
    out_ref[0] = jnp.concatenate(pieces, axis=-1)


def sequence_block(operand):
    return pl.BlockSpec((1,) + operand.shape[1:], lambda s: (s, 0, 0))


def cross(query_raw, key, value, count, after):
    seqs, tokens, width = query_raw.shape
    pairs = seqs * tokens * key.shape[1] * (width // HD)
    return pl.pallas_call(
        lambda *refs: cross_kernel(count, *refs),
        grid=(seqs,),
        in_specs=[sequence_block(operand) for operand in (query_raw, key, value)]
        + [IN_HBM] * len(after),
        out_specs=[sequence_block(query_raw), TOKEN_SPEC],
        out_shape=[jax.ShapeDtypeStruct(query_raw.shape, LOW), TOKEN],
        compiler_params=vmem(32),
        cost_estimate=cost(8 * pairs * 128, 6 * query_raw.size + 4 * key.size, pairs),
    )(query_raw, key, value, *after)


def cross_back_kernel(count, raw_ref, key_raw_ref, key_ref, value_ref, grad_ref, *refs):
    query_out, key_out, value_out, token_ref = refs[-4:]
    mark(token_ref)
    raw, key_raw = raw_ref[0], key_raw_ref[0]
    key, value, grad = key_ref[0], value_ref[0], grad_ref[0]
    marks = head_marks(raw.shape[1])
    query = (raw * root_factor(raw, marks)).astype(LOW)
    query_pieces, key_pieces, value_pieces = [], [], []
    for index in range(value.shape[1] // HD):
        probs = text_probs(query, key, index, count)
        grad_head = head(grad, index)
        probs_grad = contract(head(value, index), grad_head, 1, 1)
        delta = (probs * probs_grad).sum(axis=0, keepdims=True)
        score_grad = (probs * (probs_grad - delta)).astype(LOW)
        query_pieces.append(contract(head(key, index), score_grad, 0, 0).T * SCORE_SCALE)
        key_pieces.append(contract(score_grad, head(query, index), 1, 0) * SCORE_SCALE)
        value_pieces.append(contract(probs.astype(LOW), grad_head, 1, 0).astype(LOW))
    query_grad = jnp.concatenate(query_pieces, axis=-1)
    query_out[0] = root_back(raw, query_grad, marks).astype(LOW)
    key_grad = jnp.concatenate(key_pieces, axis=-1)
    key_out[0] = root_back(key_raw, key_grad, marks).astype(LOW)
    value_out[0] = jnp.concatenate(value_pieces, axis=-1)


def cross_back(query_raw, key_raw, key, value, grad, count, after):
    seqs, tokens, width = query_raw.shape
    pairs = seqs * tokens * key_raw.shape[1] * (width // HD)
    return pl.pallas_call(
        lambda *refs: cross_back_kernel(count, *refs),
        grid=(seqs,),
        in_specs=[sequence_block(operand) for operand in (query_raw, key_raw, key, value, grad)]
        + [IN_HBM] * len(after),
        out_specs=[sequence_block(operand) for operand in (query_raw, key_raw, value)]
        + [TOKEN_SPEC],
        out_shape=[
            jax.ShapeDtypeStruct(operand.shape, LOW) for operand in (query_raw, key_raw, value)
        ]
        + [TOKEN],
        compiler_params=vmem(40),
        cost_estimate=cost(20 * pairs * 128, 10 * query_raw.size + 10 * key_raw.size, pairs),
    )(query_raw, key_raw, key, value, grad, *after)


def spread_kernel(cos_ref, sin_ref, cos_out, sin_out):
    for source, target in ((cos_ref, cos_out), (sin_ref, sin_out)):
        target[...] = jnp.concatenate([source[...]] * (target.shape[1] // HD), axis=-1)


def spread_heads(cos, sin, width):
    shape = jax.ShapeDtypeStruct((cos.shape[0], width), jnp.float32)
    return pl.pallas_call(
        spread_kernel,
        in_specs=[WHOLE] * 2,
        out_specs=[WHOLE] * 2,
        out_shape=[shape] * 2,
        compiler_params=vmem(32),
    )(cos, sin)


def add_kernel(count, cut, *refs):
    outs = refs[-count - 1 : -1]
    mark(refs[-1])
    for index in range(count):
        left, right = refs[2 * index][0], refs[2 * index + 1][0]
        total = left.astype(jnp.float32) + right.astype(jnp.float32)
        if cut:
            total = total.reshape(cut, -1, total.shape[1])
            outs[index][:, 0] = total.astype(LOW)
        else:
            outs[index][0] = total.astype(LOW)


def add_pairs(pairs, cut, after):
    count, rows, width = pairs[0][0].shape
    spec = pl.BlockSpec((1, rows, width), lambda j: (j, 0, 0))
    if cut:
        out_spec = pl.BlockSpec((cut, 1, rows // cut, width), lambda j: (0, j, 0, 0))
        shape = jax.ShapeDtypeStruct((cut, count, rows // cut, width), LOW)
    else:
        out_spec = spec
        shape = jax.ShapeDtypeStruct((count, rows, width), LOW)
    operands = [operand for pair in pairs for operand in pair]
    return pl.pallas_call(
        lambda *refs: add_kernel(len(pairs), cut, *refs),
        grid=(count,),
        in_specs=[spec] * len(operands) + [IN_HBM] * len(after),
        out_specs=[out_spec] * len(pairs) + [TOKEN_SPEC],
        out_shape=[shape] * len(pairs) + [TOKEN],
        compiler_params=vmem(40),
        cost_estimate=cost(len(pairs) * pairs[0][0].size, 6 * len(pairs) * pairs[0][0].size),
    )(*operands, *after)


D = 1408
FF = 6144
DT = 1024
MOMENTUM = 0.9
AVERAGE_DECAY = 0.8
RATE_FACTOR = 0.5
ROPE_BASE = 10000.0
PRECISE = lax.Precision.HIGHEST
FSDP, CONTEXT, TENSOR = "fsdp", "context", "tensor"
MESH = pl.DeviceIdType.MESH


def low(operand):
    return operand.astype(LOW)


def wide(operand):
    return operand.astype(jnp.float32)


def layer_norm(operand):
    centred = operand - jnp.mean(operand, axis=-1, keepdims=True)
    return centred * lax.rsqrt(jnp.mean(centred * centred, axis=-1, keepdims=True) + EPSILON)


def layer_norm_back(operand, upstream):
    centred = operand - jnp.mean(operand, axis=-1, keepdims=True)
    factor = lax.rsqrt(jnp.mean(centred * centred, axis=-1, keepdims=True) + EPSILON)
    normed = centred * factor
    return factor * (
        upstream
        - jnp.mean(upstream, axis=-1, keepdims=True)
        - normed * jnp.mean(upstream * normed, axis=-1, keepdims=True)
    )


CORE, CHIP = 1, 2


def in_rows(operand):
    rows, width = operand.shape[-2:]
    if width % 128 and rows % 128 == 0:
        return operand.reshape(-1, 8, width)
    return operand


def swap_context(operand, bit):
    size = lax.axis_size(CONTEXT)
    pairs = [(i, i ^ bit) for i in range(size)]
    return lax.ppermute(in_rows(operand), CONTEXT, pairs).reshape(operand.shape)


def swap_tensor(operand):
    return lax.ppermute(in_rows(operand), TENSOR, [(0, 1), (1, 0)]).reshape(operand.shape)


def shift_fsdp(operand, step):
    size = lax.axis_size(FSDP)
    return lax.ppermute(operand, FSDP, [(i, (i + step) % size) for i in range(size)])


def paired():
    return lax.axis_size(TENSOR) == 2


def tensor_order(own, other, axis):
    first = lax.axis_index(TENSOR) == 0
    return jnp.concatenate(
        [jnp.where(first, own, other), jnp.where(first, other, own)], axis=axis
    )


def gather_tensor(own):
    if paired():
        return [own, swap_tensor(own)]
    return [lax.all_gather(own, TENSOR, axis=0, tiled=True)]


def term_shapes(rows, width):
    if paired():
        return [(rows // 2, width, jnp.float32), (rows // 2, width, LOW)]
    return [(rows, width, LOW)]


def split_terms(total):
    return own_and_other(total) if paired() else [total]


def sum_tensor(terms):
    if paired():
        return terms[0] + wide(swap_tensor(terms[1]))
    return wide(lax.psum_scatter(terms[0], TENSOR, scatter_dimension=0, tiled=True))


def columns_of(operand):
    parts = jnp.split(operand, lax.axis_size(TENSOR), axis=-1)
    if paired():
        first = lax.axis_index(TENSOR) == 0
        return [jnp.where(first, parts[0], parts[1]), jnp.where(first, parts[1], parts[0])]
    return parts


def join_columns(parts):
    if paired():
        return tensor_order(parts[0], parts[1], -1)
    return jnp.concatenate(parts, axis=-1)


def gather_fsdp_small(own):
    size = lax.axis_size(FSDP)
    place = lax.axis_index(FSDP)
    out = jnp.zeros((size,) + own.shape, own.dtype)
    out = lax.dynamic_update_index_in_dim(out, own, place, 0)
    for step in range(1, size):
        out = lax.dynamic_update_index_in_dim(
            out, shift_fsdp(own, step), (place - step + size) % size, 0
        )
    return out


def sum_fsdp_small(parts):
    size = lax.axis_size(FSDP)
    place = lax.axis_index(FSDP)
    total = lax.dynamic_index_in_dim(parts, place, 0, keepdims=False)
    for step in range(1, size):
        part = lax.dynamic_index_in_dim(parts, (place + step) % size, 0, keepdims=False)
        total = total + shift_fsdp(part, step)
    return total


def sum_context(total):
    for bit in (CORE, CHIP):
        total = total + swap_context(total, bit)
    return total


def gather_context(own):
    parts = [(0, own)]
    for bit in (CHIP, CORE):
        parts = parts + [(offset ^ bit, swap_context(part, bit)) for offset, part in parts]
    return parts


def multiply(body, lefts, rights, turned, extras, outs, after, tile=512):
    width = outs[0][1]
    tile = min(tile, width)
    counts = [len(lefts), len(rights), len(extras)]
    first, second, third = counts[0], sum(counts[:2]), sum(counts)

    def kernel(*refs):
        results, token_ref = refs[-len(outs) - 1 : -1], refs[-1]
        mark(token_ref)
        values = [ref[...] for ref in refs[:third]]
        for result, value in zip(
            results, body(values[:first], values[first:second], values[second:third])
        ):
            result[...] = value.astype(result.dtype)

    def column_block(rows):
        return pl.BlockSpec((rows, tile), lambda j: (0, j))

    def right_block(right):
        if turned:
            return pl.BlockSpec((tile, right.shape[1]), lambda j: (j, 0))
        return column_block(right.shape[0])

    flops = 2 * sum(right.size for right in rights) * outs[0][0]
    return pl.pallas_call(
        kernel,
        grid=(pl.cdiv(width, tile),),
        in_specs=[pl.BlockSpec(left.shape, lambda j: (0, 0)) for left in lefts]
        + [right_block(right) for right in rights]
        + [column_block(extra.shape[0]) for extra in extras]
        + [IN_HBM] * len(after),
        out_specs=[column_block(rows) for rows, _, _ in outs] + [TOKEN_SPEC],
        out_shape=[jax.ShapeDtypeStruct((rows, wide_by), kind) for rows, wide_by, kind in outs]
        + [TOKEN],
        compiler_params=vmem(40),
        cost_estimate=cost(flops, 2 * sum(right.size for right in rights)),
    )(*lefts, *rights, *extras, *after)


def stacked(pieces, right, dim):
    parts = [contract(piece, right, 1, dim) for piece in pieces]
    return parts[0] if len(parts) == 1 else jnp.concatenate(parts, axis=0)


def own_and_other(total):
    rows = total.shape[0] // 2
    return [total[:rows], total[rows:]]


GELU_SCALE, GELU_CUBE = math.sqrt(2.0 / math.pi), 0.044715


def gelu(value):
    return 0.5 * value * (1.0 + jnp.tanh(GELU_SCALE * (value + GELU_CUBE * value**3)))


def gelu_slope(value):
    bend = jnp.tanh(GELU_SCALE * (value + GELU_CUBE * value**3))
    slope = GELU_SCALE * (1.0 + 3.0 * GELU_CUBE * value * value)
    return 0.5 * (1.0 + bend) + 0.5 * value * (1.0 - bend * bend) * slope


def meet_core():
    place = lax.axis_index(CONTEXT)
    other = {CONTEXT: place + 1 - 2 * (place % 2)}
    barrier = pltpu.get_barrier_semaphore()
    pl.semaphore_signal(barrier, inc=1, device_id=other, device_id_type=MESH)
    pl.semaphore_wait(barrier, 1)
    return other


FAR = "far"


def partner(kind):
    if isinstance(kind, list):
        return {**partner(kind[0]), **partner(kind[1])}
    return partner_on_axis(kind)


def partner_on_axis(kind):
    place = lax.axis_index(CONTEXT)
    if kind == TENSOR:
        return {TENSOR: 1 - lax.axis_index(TENSOR)}
    if kind == CORE:
        return {CONTEXT: place + 1 - 2 * (place % 2)}
    if kind == CHIP:
        return {CONTEXT: (place + CHIP) % 4}
    if kind == FAR:
        return {CONTEXT: (place + CHIP + 1 - 2 * (place % 2)) % 4}
    size = lax.axis_size(FSDP)
    return {FSDP: (lax.axis_index(FSDP) + kind[0]) % size}


def meet(kinds):
    barrier = pltpu.get_barrier_semaphore()
    for kind in kinds:
        pl.semaphore_signal(barrier, inc=1, device_id=partner(kind), device_id_type=MESH)
    pl.semaphore_wait(barrier, len(kinds))


def sending(source, target, sems, index, kind):
    return pltpu.make_async_remote_copy(
        src_ref=source,
        dst_ref=target,
        send_sem=sems.at[0, index],
        recv_sem=sems.at[1, index],
        device_id=partner(kind),
        device_id_type=MESH,
    )


def distinct(kinds):
    return [kind for index, kind in enumerate(kinds) if kind not in kinds[:index]]


def exchange_kernel(kinds, *refs):
    count = len(kinds)
    sources, targets, token_ref, sems = refs[:count], refs[-count - 2 : -2], refs[-2], refs[-1]
    mark(token_ref)
    meet(distinct(kinds))
    copies = [
        sending(source, target, sems, index, kind)
        for index, (source, target, kind) in enumerate(zip(sources, targets, kinds))
    ]
    for copy in copies:
        copy.start()
    for copy in copies:
        copy.wait()


def exchange(items, after, ident):
    operands, kinds = zip(*items)
    return pl.pallas_call(
        lambda *refs: exchange_kernel(list(kinds), *refs),
        in_specs=[FREE] * len(items) + [IN_HBM] * len(after),
        out_specs=[FREE] * len(items) + [WHOLE],
        out_shape=[jax.ShapeDtypeStruct(operand.shape, operand.dtype) for operand in operands]
        + [TOKEN],
        scratch_shapes=[pltpu.SemaphoreType.DMA((2, len(items)))],
        compiler_params=pltpu.CompilerParams(
            collective_id=ident, has_side_effects=True, vmem_limit_bytes=16 * MIB
        ),
        cost_estimate=cost(0, 0),
    )(*operands, *after)


def share_kernel(count, places, *refs):
    widths = len(places)
    total = 1 + places[-1][0]
    sources, outs = refs[:count], refs[-count // 2 * total - 4 :]
    targets, token_ref = outs[:-4], outs[-4]
    local_sem, send_sem, recv_sem = outs[-3:]
    mark(token_ref)
    place = lax.axis_index(CONTEXT)
    other = meet_core()
    copies = []
    for source_at in range(count):
        part, chip = source_at // 2, source_at % 2
        slot = (place + CHIP * chip) % 4
        for index in range(widths):
            sem = source_at * widths + index
            source = sources[source_at].at[:, index]
            out_at, half = places[index]
            target = targets[part * total + out_at]
            target = target.at[:, slot] if half is None else target.at[:, slot, half]
            remote = pltpu.make_async_remote_copy(
                src_ref=source,
                dst_ref=target,
                send_sem=send_sem.at[sem],
                recv_sem=recv_sem.at[sem],
                device_id=other,
                device_id_type=MESH,
            )
            remote.start()
            own = pltpu.make_async_copy(source, target, local_sem.at[sem])
            own.start()
            copies += [remote, own]
    for copy in copies:
        copy.wait()


def share_core(pieces, after, ident, halved=False):
    along, widths, rows, width = pieces[0].shape
    count = len(pieces)
    size = lax.axis_size(CONTEXT)
    places = [(index, None) for index in range(widths)]
    shapes = [(along, size, rows, width)] * widths
    if halved:
        places = [(0, 0), (0, 1)] + [(index, None) for index in range(1, widths - 1)]
        shapes = [(along, size, 2, rows, width)] + shapes[2:]
    total = count // 2 * len(shapes)
    outs = pl.pallas_call(
        lambda *refs: share_kernel(count, places, *refs),
        in_specs=[WHOLE] * count + [IN_HBM] * len(after),
        out_specs=[IN_HBM] * total + [WHOLE],
        out_shape=[jax.ShapeDtypeStruct(shape, LOW) for shape in shapes] * (count // 2) + [TOKEN],
        scratch_shapes=[pltpu.SemaphoreType.DMA((count * widths,))] * 3,
        compiler_params=pltpu.CompilerParams(
            collective_id=ident, has_side_effects=True, vmem_limit_bytes=40 * MIB
        ),
        cost_estimate=cost(0, 6 * count * pieces[0].size * 2),
    )(*pieces, *after)
    held = [out.reshape(-1, width) for out in outs[:-1]]
    each = len(shapes)
    return [held[part * each : (part + 1) * each] for part in range(count // 2)], outs[-1]


def pack_of(shards):
    return jnp.stack([low(shard) for shard in shards], axis=0)


def gather_fsdp(shards, after):
    return lax.all_gather(gate(pack_of(shards), after), FSDP, axis=0, tiled=False)


def across(along, spread, after):
    along = gate(along, after) if after else along
    parts = [along, swap_context(along, CHIP)]
    if not spread:
        return parts
    if paired():
        first = swap_tensor(along)
        parts[1] = gate(parts[1], (first,))
        return parts + [first, swap_tensor(parts[1])]
    many = [lax.all_gather(part, TENSOR, axis=0) for part in parts]
    return [part[i] for i in range(lax.axis_size(TENSOR)) for part in many]


class Order:
    def __init__(self):
        self.after = ()
        self.count = 0

    def ident(self):
        self.count += 1
        return self.count - 1

    def need(self, *operands):
        self.after = self.after + operands

    def put(self, outs):
        *outs, token = outs
        self.after = (token,)
        return outs

    def multiply(self, body, lefts, rights, turned, extras, outs, tile=512):
        return self.put(multiply(body, lefts, rights, turned, extras, outs, self.after, tile))


def grad_kernel(which, spread, tile, counts, waits, *refs):
    count = sum(counts)
    lefts, rights = refs[:count], refs[count : count + len(which)]
    outs = refs[count + len(which) + waits :]
    kept, given = outs[: max(spread, 1)], outs[max(spread, 1) : 2 * max(spread, 1)]
    token_ref = outs[2 * max(spread, 1)]
    turned, cut, sent, came, send_sem, recv_sem = outs[2 * max(spread, 1) + 1 :]
    mark(token_ref)
    other = meet_core()
    place = lax.axis_index(CONTEXT)
    tiles = rights[0].shape[1] // tile
    rows = cut.shape[3]
    along = lax.axis_size(FSDP)
    block = rows // along
    for index, pieces in enumerate(counts):
        start = sum(counts[:index])
        depth = 0
        for left in lefts[start : start + pieces]:
            turned[:, depth : depth + left.shape[0]] = left[...].astype(jnp.float32).T
            depth += left.shape[0]
        for core in range(2):
            for chip in range(2):
                at = (place // 2 + chip) % 2 * 2 + (place % 2 + core) % 2
                pieces = [
                    turned[pl.ds(pl.multiple_of((4 * z + at) * block, 8), block), :]
                    for z in range(along)
                ]
                cut[index, core, chip] = low(jnp.concatenate(pieces, axis=0))
    units = []
    for job, left in enumerate(which):
        for chip in range(2):
            out = (kept, given)[chip]
            out = out[job % spread].at[job // spread] if spread else out[0].at[job]
            units.append((left, rights[job], chip, out))

    def columns(index):
        if isinstance(index, int):
            return pl.ds(index * tile, tile)
        return pl.ds(pl.multiple_of(index * tile, tile), tile)

    def copy(unit, index):
        sem = unit * tiles + index
        return pltpu.make_async_remote_copy(
            src_ref=sent.at[unit, index],
            dst_ref=came.at[unit, index],
            send_sem=send_sem.at[sem],
            recv_sem=recv_sem.at[sem],
            device_id=other,
            device_id_type=MESH,
        )

    def each(step):
        if tiles == 1:
            step(0)
        else:
            lax.fori_loop(0, tiles, lambda index, carry: (step(index), carry)[1], 0)

    for unit, (left, right, chip, out) in enumerate(units):

        def give(index, unit=unit, left=left, right=right, chip=chip):
            sent[unit, index] = low(contract(cut[left, 1, chip], right[:, columns(index)], 1, 0))
            copy(unit, index).start()

        each(give)
    for unit, (left, right, chip, out) in enumerate(units):

        def keep(index, unit=unit, left=left, right=right, chip=chip, out=out):
            term = contract(cut[left, 0, chip], right[:, columns(index)], 1, 0)
            copy(unit, index).wait_recv()
            out[:, columns(index)] = low(term + wide(came[unit, index]))

        each(keep)
    for unit in range(len(units)):

        def done(index, unit=unit):
            copy(unit, index).wait_send()

        each(done)


def grad_core(lefts, rights, which, spread, after, ident):
    depth, width = rights[0].shape
    counts = [len(pieces) for pieces in lefts]
    lefts = [piece for pieces in lefts for piece in pieces]
    features = lefts[0].shape[1]
    rows = features // 4
    jobs = len(which)
    count = max(spread, 1)
    tile = width
    for candidate in (512, 384):
        if width > 1408 and width % candidate == 0:
            tile = candidate
            break
    tiles = width // tile
    shape = jax.ShapeDtypeStruct((jobs // count, rows, width), LOW)
    outs = pl.pallas_call(
        lambda *refs: grad_kernel(which, spread, tile, counts, len(after), *refs),
        in_specs=[WHOLE] * (len(lefts) + jobs) + [IN_HBM] * len(after),
        out_specs=[WHOLE] * (2 * count + 1),
        out_shape=[shape] * (2 * count) + [TOKEN],
        scratch_shapes=[
            pltpu.VMEM((features, depth), jnp.float32),
            pltpu.VMEM((len(counts), 2, 2, rows, depth), LOW),
            pltpu.VMEM((2 * jobs, tiles, rows, tile), LOW),
            pltpu.VMEM((2 * jobs, tiles, rows, tile), LOW),
            pltpu.SemaphoreType.DMA((2 * jobs * tiles,)),
            pltpu.SemaphoreType.DMA((2 * jobs * tiles,)),
        ],
        compiler_params=pltpu.CompilerParams(
            collective_id=ident, has_side_effects=True, vmem_limit_bytes=56 * MIB
        ),
        cost_estimate=cost(8 * jobs * rows * width * depth, 6 * jobs * width * rows),
    )(*lefts, *rights, *after)
    if spread:
        return list(outs[:count]), list(outs[count:-1]), outs[-1]
    return outs


def sum_parts(kept, given, order):
    if paired():
        pairs = [(kept[0], swap_tensor(kept[1])), (given[0], swap_tensor(given[1]))]
        return order.put(add_pairs(pairs, 0, order.after))
    return [
        lax.psum_scatter(jnp.stack(parts), TENSOR, scatter_dimension=0, tiled=False)
        for parts in (kept, given)
    ]


def sum_rest(kept, came, order):
    (total,) = order.put(add_pairs([(kept, came)], lax.axis_size(FSDP), order.after))
    return lax.psum_scatter(total, FSDP, scatter_dimension=0, tiled=False)


def sum_text(total):
    place = lax.axis_index(CONTEXT)
    steps = [
        (lambda operand: swap_context(operand, CORE), place % 2),
        (lambda operand: swap_context(operand, CHIP), place // 2),
    ]
    if paired():
        steps.append((swap_tensor, lax.axis_index(TENSOR)))
    for swap, bit in steps:
        half = total.shape[0] // 2
        kept = lax.dynamic_slice_in_dim(total, bit * half, half, axis=0)
        given = lax.dynamic_slice_in_dim(total, (1 - bit) * half, half, axis=0)
        total = low(wide(kept) + wide(swap(given)))
    if not paired():
        total = lax.psum(total, TENSOR)
    for swap, bit in reversed(steps):
        other = swap(total)
        first = bit == 0
        total = jnp.concatenate(
            [jnp.where(first, total, other), jnp.where(first, other, total)], axis=0
        )
    return total


def per_token(operand, rows):
    seqs, _, width = operand.shape
    return jnp.broadcast_to(operand, (seqs, rows // seqs, width)).reshape(rows, width)


def per_sequence(operand, seqs):
    return operand.reshape(seqs, -1, operand.shape[-1]).sum(axis=1)


def layer_forward(residual, skip_rows, modulation, text, tables, weights, order, steps):
    rows, features = residual.shape
    parts = lax.axis_size(TENSOR)
    every = rows * parts
    seqs = modulation[0].shape[0]
    shift_a, scale_a, gate_a, shift_m, scale_m, gate_m = [
        per_token(piece, rows) for piece in modulation
    ]
    cos, sin = tables
    kept = SimpleNamespace()
    kept.concat = jnp.concatenate([residual, wide(skip_rows)], axis=-1)
    kept.concat_low = low(layer_norm(kept.concat))
    width = weights.skip[0].shape[1]
    skipped = order.multiply(
        lambda lefts, rights, _: [contract(lefts[0], right, 1, 0) for right in rights],
        [kept.concat_low],
        weights.skip,
        False,
        [],
        [(rows, width, LOW)] * parts,
    )
    after_skip = wide(join_columns(skipped))
    kept.after_skip = after_skip
    kept.attn_all = gather_tensor(low(layer_norm(after_skip) * (1.0 + scale_a) + shift_a))
    steps.skipped()
    kept.query_raw, kept.key_raw, value_low = order.multiply(
        lambda lefts, rights, _: [stacked(lefts, right, 0) for right in rights],
        kept.attn_all,
        [weights.query, weights.key, weights.value],
        False,
        [],
        [(every, width, jnp.float32)] * 2 + [(every, width, LOW)],
    )
    blocks = (parts, seqs, rows // seqs, width)
    query_low, key_low = order.put(turn(kept.query_raw, kept.key_raw, cos, sin, order.after))
    kept.query_low = query_low.reshape(blocks)
    kept.keys = [part.reshape(blocks) for _, part in gather_context(key_low)]
    kept.values = [part.reshape(blocks) for _, part in gather_context(value_low)]
    steps.turned()
    attn_low, kept.attn_lse = attend(kept.query_low, kept.keys, kept.values, order.after)
    order.after = (kept.attn_lse,)
    kept.attn_low = attn_low.reshape(-1, width)
    terms = order.multiply(
        lambda lefts, rights, _: split_terms(contract(lefts[0], rights[0], 1, 1)),
        [kept.attn_low],
        [weights.attn_out],
        True,
        [],
        term_shapes(every, features),
    )
    kept.attn_branch = sum_tensor(terms)
    steps.attended()
    kept.after_attn = after_skip + gate_a * kept.attn_branch
    kept.cross_in = low(layer_norm(kept.after_attn))
    raws = order.multiply(
        lambda lefts, rights, _: [contract(lefts[0], right, 1, 0) for right in rights],
        [kept.cross_in],
        weights.cross_query,
        False,
        [],
        [(rows, width, jnp.float32)] * parts,
    )
    kept.cross_raw = [raw.reshape(blocks[1:]) for raw in raws]
    kept.cross_low = []
    for raw, key, value in zip(kept.cross_raw, text.keys, text.values):
        (out,) = order.put(cross(raw, key, value, text.count, order.after))
        kept.cross_low.append(out.reshape(rows, width))
    (kept.after_cross,) = order.multiply(
        lambda lefts, rights, extras: [
            sum((contract(left, right, 1, 1) for left, right in zip(lefts, rights)), extras[0])
        ],
        kept.cross_low,
        weights.cross_out,
        True,
        [kept.after_attn],
        [(rows, features, jnp.float32)],
    )
    after_cross = kept.after_cross
    kept.mlp_all = gather_tensor(low(layer_norm(after_cross) * (1.0 + scale_m) + shift_m))
    steps.crossed()

    def raise_and_bend(lefts, rights, _):
        upward = stacked(lefts, rights[0], 0)
        return [upward, gelu(upward)]

    hidden = weights.up.shape[1]
    kept.upward, kept.hidden_low = order.multiply(
        raise_and_bend,
        kept.mlp_all,
        [weights.up],
        False,
        [],
        [(every, hidden, jnp.float32), (every, hidden, LOW)],
    )
    steps.raised()
    terms = order.multiply(
        lambda lefts, rights, _: split_terms(contract(lefts[0], rights[0], 1, 1)),
        [kept.hidden_low],
        [weights.down],
        True,
        [],
        term_shapes(every, features),
    )
    kept.mlp_branch = sum_tensor(terms)
    steps.lowered()
    return after_cross + gate_m * kept.mlp_branch, kept


def modulate(columns):
    if paired():
        total = columns[0] + swap_tensor(columns[1])
    else:
        total = lax.psum_scatter(jnp.stack(columns), TENSOR, scatter_dimension=0, tiled=False)
    mod_all = gather_fsdp_small(sum_context(total))
    return mod_all.reshape(-1, mod_all.shape[-1])


def layer_backward(grad_res, kept, weights, modulation, tables, text, text_low, order, earlier, last):
    rows, features = grad_res.shape
    parts = lax.axis_size(TENSOR)
    every = rows * parts
    seqs = modulation[0].shape[0]
    shift_a, scale_a, gate_a, shift_m, scale_m, gate_m = [
        per_token(piece, rows) for piece in modulation
    ]
    cos, sin = tables
    reduced = SimpleNamespace()

    def product(lefts, rights, which, spread):
        outs = order.put(grad_core(lefts, rights, which, spread, order.after, order.ident()))
        return outs if spread else (outs[0], swap_context(outs[1], CHIP))

    mlp_grad = gather_tensor(low(gate_m * grad_res))
    earlier.start()
    grad_gate_m = per_sequence(grad_res * kept.mlp_branch, seqs)
    (up_grad,) = order.multiply(
        lambda lefts, rights, extras: [stacked(lefts, rights[0], 0) * gelu_slope(extras[0])],
        mlp_grad,
        [weights.down],
        False,
        [kept.upward],
        [(every, kept.upward.shape[1], LOW)],
    )
    terms = order.multiply(
        lambda lefts, rights, _: split_terms(contract(lefts[0], rights[0], 1, 1)),
        [up_grad],
        [weights.up],
        True,
        [],
        term_shapes(every, features),
    )
    mlp_in_grad = sum_tensor(terms)
    order.need(*earlier.sums())
    down = product([mlp_grad], [kept.hidden_low], (0,), 0)
    earlier.first()
    up = product([kept.mlp_all], [up_grad], (0,), 0)
    grad_shift_m = per_sequence(mlp_in_grad, seqs)
    grad_scale_m = per_sequence(mlp_in_grad * layer_norm(kept.after_cross), seqs)
    grad_res = grad_res + layer_norm_back(kept.after_cross, mlp_in_grad * (1.0 + scale_m))

    cross_grad = low(grad_res)
    width = weights.cross_out[0].shape[1]
    out_grads = order.multiply(
        lambda lefts, rights, _: [contract(lefts[0], right, 1, 0) for right in rights],
        [cross_grad],
        weights.cross_out,
        False,
        [],
        [(rows, width, LOW)] * parts,
    )
    cross_q, text_key_grad, text_value_grad = [], [], []
    for part, out_grad in enumerate(out_grads):
        raw = kept.cross_raw[part]
        query_grad, key_grad, value_grad = order.put(
            cross_back(
                raw,
                text.raws[part],
                text.keys[part],
                text.values[part],
                out_grad.reshape(raw.shape),
                text.count,
                order.after,
            )
        )
        cross_q.append(query_grad.reshape(rows, width))
        text_key_grad.append(key_grad.reshape(-1, width))
        text_value_grad.append(value_grad.reshape(-1, width))
    (cross_in_grad,) = order.multiply(
        lambda lefts, rights, _: [
            sum(contract(left, right, 1, 1) for left, right in zip(lefts, rights))
        ],
        cross_q,
        weights.cross_query,
        True,
        [],
        [(rows, features, jnp.float32)],
    )
    grad_res = grad_res + layer_norm_back(kept.after_attn, cross_in_grad)

    attn_grad = gather_tensor(low(gate_a * grad_res))
    earlier.second()
    grad_gate_a = per_sequence(grad_res * kept.attn_branch, seqs)
    crossed = product(
        [[cross_grad], [kept.cross_in]],
        kept.cross_low + cross_q,
        (0,) * parts + (1,) * parts,
        parts,
    )
    texts = product([[text_low]], text_key_grad + text_value_grad, (0,) * (2 * parts), parts)
    (out_grad,) = order.multiply(
        lambda lefts, rights, _: [stacked(lefts, rights[0], 0)],
        attn_grad,
        [weights.attn_out],
        False,
        [],
        [(every, width, LOW)],
    )
    blocks = kept.query_low.shape
    order.need(*earlier.more())
    query_grad, key_parts, value_parts = order.put(
        attend_back(
            kept.query_low,
            kept.query_raw.reshape(blocks),
            out_grad.reshape(blocks),
            kept.attn_lse,
            cos.reshape(blocks),
            sin.reshape(blocks),
            kept.keys,
            kept.values,
            order.after,
        )
    )
    query_grad = query_grad.reshape(-1, width)

    key_parts, value_parts = [
        [piece.reshape(1, -1, width) for piece in pieces] for pieces in (key_parts, value_parts)
    ]
    near = [
        (pieces[place], swap_context(pieces[place + 2], CORE))
        for pieces in (key_parts, value_parts)
        for place in range(2)
    ]
    reduced.down = sum_rest(*down, order)
    key_near, key_far, value_near, value_far = order.put(add_pairs(near, 0, order.after))
    whole = [
        (key_near, swap_context(key_far, CHIP)),
        (value_near, swap_context(value_far, CHIP)),
    ]
    reduced.up = sum_rest(*up, order)
    (text_part,) = order.multiply(
        lambda lefts, rights, _: [
            sum(contract(left, right, 1, 1) for left, right in zip(lefts, rights))
        ],
        text_key_grad + text_value_grad,
        weights.text_key + weights.text_value,
        True,
        [],
        [(text_low.shape[0], text_low.shape[1], jnp.float32)],
        256,
    )
    earlier.third()
    key_grad, value_grad = order.put(add_pairs(whole, 0, order.after))
    (key_grad,) = order.put(turn_back(key_grad[0], kept.key_raw, cos, sin, order.after))
    value_grad = value_grad[0]
    terms = order.multiply(
        lambda lefts, rights, _: split_terms(
            sum(contract(left, right, 1, 1) for left, right in zip(lefts, rights))
        ),
        [query_grad, key_grad, value_grad],
        [weights.query, weights.key, weights.value],
        True,
        [],
        term_shapes(every, features),
    )
    attn_in_grad = sum_tensor(terms)
    order.need(*earlier.most())
    attn_own, attn_given = order.put(
        grad_core(
            [attn_grad, kept.attn_all],
            [kept.attn_low, query_grad, key_grad, value_grad],
            (0, 1, 1, 1),
            0,
            order.after,
            order.ident(),
        )
    )
    attended = (attn_own,) if last else (attn_own, swap_context(attn_given, CHIP))
    crossed = sum_parts(*crossed, order)
    crossed = (crossed[0], swap_context(crossed[1], CHIP))
    texts = sum_parts(*texts, order)
    texts = (texts[0], swap_context(texts[1], CHIP))
    grad_shift_a = per_sequence(attn_in_grad, seqs)
    grad_scale_a = per_sequence(attn_in_grad * layer_norm(kept.after_skip), seqs)
    grad_res = grad_res + layer_norm_back(kept.after_skip, attn_in_grad * (1.0 + scale_a))

    skip_grad = columns_of(low(grad_res))
    (concat_grad,) = order.multiply(
        lambda lefts, rights, _: [
            sum(contract(left, right, 1, 1) for left, right in zip(lefts, rights))
        ],
        skip_grad,
        weights.skip,
        True,
        [],
        [(rows, 2 * features, jnp.float32)],
    )
    mod_grad = jnp.concatenate(
        [grad_shift_a, grad_scale_a, grad_gate_a, grad_shift_m, grad_scale_m, grad_gate_m], axis=-1
    )
    later = SimpleNamespace()

    def start():
        later.skipped = product([[kept.concat_low]], skip_grad, (0,) * parts, parts)
        reduced.cross = sum_rest(*crossed, order)

    def first():
        reduced.attention = sum_rest(*attended, order)

    def second():
        reduced.text = sum_rest(*texts, order)
        kept, given = sum_parts(*later.skipped, order)
        later.skipped = (kept, swap_context(given, CHIP))

    def third():
        reduced.skip = sum_rest(*later.skipped, order)

    def end(text_total):
        if not last:
            start()
            first()
            second()
            third()
            return modulate(columns_of(mod_grad)), sum_text(text_total)
        order.need(reduced.up)
        (own, other), (chip_own, chip_other) = product(
            [[kept.concat_low]], skip_grad, (0,) * parts, parts
        )
        order.need(*earlier.rest())
        reduced.cross = sum_rest(*crossed, order)
        reduced.text = sum_rest(*texts, order)
        columns = columns_of(mod_grad)
        came = order.put(
            exchange(
                [
                    (other, TENSOR),
                    (chip_other, TENSOR),
                    (attn_given, CHIP),
                    (columns[1], TENSOR),
                ],
                order.after,
                order.ident(),
            )
        )
        columns_came = came[3]
        order.need(reduced.cross, reduced.text)
        reduced.attention = sum_rest(attended[0], came[2], order)
        own, chip_own = order.put(
            add_pairs([(own, came[0]), (chip_own, came[1])], 0, order.after)
        )
        total = columns[0] + columns_came
        chip_came, *totals = order.put(
            exchange(
                [(chip_own, CHIP), (total, CHIP), (total, CORE), (total, FAR)],
                order.after,
                order.ident(),
            )
        )
        text_total = gate(text_total, order.after)
        order.need(reduced.attention)
        reduced.skip = sum_rest(own, chip_came, order)
        mod_all = gather_fsdp_small(total + totals[0] + totals[1] + totals[2])
        return mod_all.reshape(-1, mod_all.shape[-1]), sum_text(text_total)

    later.start, later.first, later.second, later.third = start, first, second, third
    later.end = end
    concat_grad = layer_norm_back(kept.concat, concat_grad)
    later.columns = lambda: modulate(columns_of(mod_grad))
    later.sums = lambda: (reduced.down, reduced.up)
    later.more = lambda: (reduced.cross, reduced.attention)
    later.most = lambda: (reduced.text,)
    later.rest = lambda: (reduced.skip,)
    return concat_grad[:, :features], concat_grad[:, features:], text_part, reduced, later


def shards(
    latents,
    skip_inputs,
    text_states,
    condition,
    positions,
    cotangent,
    *tensors,
):
    masters, momenta, averages = tensors[:7], tensors[7:14], tensors[14:]
    (
        skip_weight,
        mod_weight,
        proj_weight,
        output_weight,
        text_weight,
        up_weight,
        down_weight,
    ) = masters
    layers = skip_weight.shape[0]
    along = lax.axis_size(FSDP)
    size = lax.axis_size(CONTEXT)
    parts = lax.axis_size(TENSOR)
    seqs, tokens = latents.shape[0], latents.shape[1]
    text_count = text_states.shape[1]
    every = range(layers)

    def cross_of(layer):
        return [proj_weight[layer, :, 3], output_weight[layer, 1].T]

    def halves_of(shard):
        half = shard.shape[0] // 2
        return [shard[:half], shard[half:]]

    def attention_of(layer):
        return [proj_weight[layer, :, j] for j in range(3)] + [output_weight[layer, 0].T]

    order = Order()
    weights = [SimpleNamespace() for _ in every]
    skip_along = gather_fsdp_small(pack_of([skip_weight[0]]))
    arrived = (skip_along,)
    skip_parts = across(skip_along, True, ())
    started = (skip_parts[1],)
    mixed = gather_fsdp(attention_of(0) + cross_of(0), arrived)
    attention, crosses, skips = [mixed[:, :4]], [mixed[:, 4:]], [None]
    text_along = gather_fsdp([text_weight[i, :, j] for i in every for j in range(2)], arrived)
    ups = [gather_fsdp([up_weight[0]], arrived)]
    downs = [gather_fsdp([down_weight[0].T], arrived)]
    for layer in every[1:]:
        mixed = gather_fsdp(
            attention_of(layer) + cross_of(layer) + halves_of(skip_weight[layer]), started
        )
        attention.append(mixed[:, :4])
        crosses.append(mixed[:, 4:6])
        skips.append(mixed[:, 6:])
        ups.append(gather_fsdp([up_weight[layer]], started))
        downs.append(gather_fsdp([down_weight[layer].T], started))

    attention_parts, cross_parts, up_parts, down_parts = {}, {}, {}, {}
    skip_parts = {0: skip_parts}

    def hold_skip(layer):
        (held,) = order.put(
            share_core(skip_parts[layer], order.after, order.ident(), layer > 0)
        )
        weights[layer].skip = [part[0] for part in held]

    def hold_attention(layer):
        (held,) = order.put(share_core(attention_parts[layer], order.after, order.ident()))
        place = weights[layer]
        place.query, place.key, place.value, place.attn_out = held[0]

    def hold_cross(layer):
        (held,) = order.put(share_core(cross_parts[layer], order.after, order.ident()))
        weights[layer].cross_query = [part[0] for part in held]
        weights[layer].cross_out = [part[1] for part in held]

    def hold_up(layer):
        (held,) = order.put(share_core(up_parts[layer], order.after, order.ident()))
        weights[layer].up = held[0][0]

    def hold_down(layer):
        (held,) = order.put(share_core(down_parts[layer], order.after, order.ident()))
        weights[layer].down = held[0][0]

    padded = -(-text_count // 128) * 128
    text_low = jnp.pad(text_states, ((0, 0), (0, padded - text_count), (0, 0)))
    text_low = text_low.reshape(seqs * padded, -1)
    texts = [SimpleNamespace(count=text_count) for _ in every]

    def hold_text():
        (held,) = order.put(share_core(text_parts[0], order.after, order.ident()))
        for layer in every:
            weights[layer].text_key = [part[2 * layer] for part in held]
            weights[layer].text_value = [part[2 * layer + 1] for part in held]

    def read_text(layer):
        text = texts[layer]
        place = weights[layer]
        width = place.text_key[0].shape[1]
        outs = order.multiply(
            lambda lefts, rights, _: [contract(lefts[0], right, 1, 0) for right in rights],
            [text_low],
            place.text_key + place.text_value,
            False,
            [],
            [(seqs * padded, width, jnp.float32)] * parts + [(seqs * padded, width, LOW)] * parts,
            256,
        )
        blocks = (seqs, padded, width)
        keys = [order.put(root(raw, order.after))[0] for raw in outs[:parts]]
        text.raws = [raw.reshape(blocks) for raw in outs[:parts]]
        text.keys = [key.reshape(blocks) for key in keys]
        text.values = [value.reshape(blocks) for value in outs[parts:]]

    text_parts = {}
    attention_parts[0] = across(attention[0], False, (skip_parts[0][-1],))
    hold_skip(0)

    def steps_of(layer):
        steps = SimpleNamespace()
        coming = layer + 1 if layer + 1 < layers else None

        def skipped():
            if not layer:
                text_parts[0] = across(text_along, True, order.after)
            hold_attention(layer)

        def turned():
            if layer:
                read_text(layer)

        def attended():
            if layer:
                down_parts[layer] = across(downs[layer], False, order.after)
                hold_up(layer)
            else:
                cross_parts[layer] = across(crosses[layer], True, order.after)
                up_parts[layer] = across(ups[layer], False, order.after)
                hold_text()
                if coming:
                    skip_parts[coming] = across(skips[coming], True, order.after)
                read_text(layer)
                if coming:
                    order.need(skip_parts[coming][1])
            hold_cross(layer)
            if not layer:
                down_parts[layer] = across(downs[layer], False, order.after)

        def crossed():
            if not layer:
                hold_up(layer)
            if coming:
                attention_parts[coming] = across(attention[coming], False, order.after)

        def raised():
            hold_down(layer)
            if coming:
                order.need(attention_parts[coming][1])
                cross_parts[coming] = across(crosses[coming], True, order.after[:1])

        def lowered():
            if coming:
                hold_skip(coming)
                up_parts[coming] = across(ups[coming], False, order.after)

        steps.skipped, steps.turned, steps.attended = skipped, turned, attended
        steps.crossed, steps.raised, steps.lowered = crossed, raised, lowered
        return steps

    cond_float = wide(condition)
    cond_silu, silu_pull = jax.vjp(jax.nn.silu, cond_float)
    cond_all = gather_fsdp_small(low(cond_silu)).reshape(along * seqs, cond_float.shape[1])
    rows = mod_weight.shape[1]
    place = lax.axis_index(FSDP) * size + lax.axis_index(CONTEXT)
    cond_rows = lax.dynamic_slice_in_dim(cond_all, place * rows, rows, axis=1)
    mod_low = low(mod_weight)
    mod_part = contract(cond_rows, mod_low, 1, 1)
    mod_part = gate(mod_part, arrived).reshape((along, seqs) + mod_part.shape[1:])
    mod_part = sum_fsdp_small(mod_part)
    mod_part = low(sum_context(gate(mod_part, (skip_parts[0][-1],))))
    if paired():
        mod_full = tensor_order(mod_part, swap_tensor(mod_part), -1)
    else:
        mod_full = lax.all_gather(mod_part, TENSOR, axis=2, tiled=True)
    modulations = [
        jnp.split(wide(mod_full[:, layer])[:, None, :], 6, axis=-1) for layer in every
    ]

    quarter = HD // 4
    frequency = ROPE_BASE ** (-jnp.arange(quarter, dtype=jnp.float32) / quarter)
    grid = positions.reshape(seqs, 2, parts, tokens)
    if paired():
        mine = lax.axis_index(TENSOR)
        grid = jnp.concatenate(
            [
                lax.dynamic_slice_in_dim(grid, mine, 1, axis=2),
                lax.dynamic_slice_in_dim(grid, 1 - mine, 1, axis=2),
            ],
            axis=2,
        )
    grid = wide(grid.transpose(2, 0, 3, 1).reshape(parts * seqs * tokens, 2))
    row_angle = grid[:, :1] * frequency
    col_angle = grid[:, 1:] * frequency
    cos = jnp.concatenate([jnp.cos(row_angle)] * 2 + [jnp.cos(col_angle)] * 2, axis=-1)
    sin = jnp.concatenate(
        [-jnp.sin(row_angle), jnp.sin(row_angle), -jnp.sin(col_angle), jnp.sin(col_angle)], axis=-1
    )
    tables = spread_heads(cos, sin, proj_weight.shape[-1])

    own = (seqs * tokens, latents.shape[-1])
    residual = wide(latents).reshape(own)
    stored = []
    for layer in every:
        residual, kept = layer_forward(
            residual,
            skip_inputs[layer].reshape(own),
            modulations[layer],
            texts[layer],
            tables,
            weights[layer],
            order,
            steps_of(layer),
        )
        stored.append(kept)
    block_output = low(residual).reshape(latents.shape)

    grad_res = wide(cotangent).reshape(own)
    cond_parts = []
    text_total = 0.0
    skip_grads = [None] * layers
    gradients = [None] * layers

    def add_modulation(layer, mod_all):
        gradients[layer].mod = jnp.einsum(
            "bk,bc->kc", wide(cond_rows), mod_all, precision=PRECISE
        )
        cond_parts.append(
            jnp.einsum("bc,kc->bk", mod_all, wide(mod_low[layer]), precision=PRECISE)
        )

    later = SimpleNamespace(
        start=lambda: None, first=lambda: None, second=lambda: None, third=lambda: None, sums=lambda: (), more=lambda: (), most=lambda: ()
    )
    for layer in reversed(every):
        grad_res, skip_grads[layer], text_part, reduced, later = layer_backward(
            grad_res,
            stored[layer],
            weights[layer],
            modulations[layer],
            tables,
            texts[layer],
            text_low,
            order,
            later,
            paired() and layer == 0,
        )
        text_total = text_total + text_part
        gradients[layer] = reduced
        if layer:
            add_modulation(layer, later.columns())
    mod_all, text_sum = later.end(low(text_total))
    add_modulation(0, mod_all)
    gradients = [
        (
            wide(each.skip[0]),
            each.mod,
            wide(jnp.concatenate([each.attention[1:], each.cross[1:]], axis=0)).transpose(1, 0, 2),
            wide(jnp.stack([each.attention[0], each.cross[0]], axis=0)).transpose(0, 2, 1),
            wide(each.text).transpose(1, 0, 2),
            wide(each.up[0]),
            wide(each.down[0]).T,
        )
        for each in gradients
    ]
    text_sum = wide(text_sum).reshape(seqs, padded, -1)[:, :text_count]
    cond_total = sum(cond_parts)
    if paired():
        cond_total = cond_total + swap_tensor(cond_total)
    else:
        cond_total = lax.psum(cond_total, TENSOR)
    sent = cond_total.reshape(along, seqs, rows)
    here = lax.axis_index(FSDP)
    cond_sum = jnp.zeros((along, size, seqs, rows), jnp.float32)
    for step in range(along):
        part = lax.dynamic_index_in_dim(sent, (here + step) % along, 0, keepdims=False)
        if step:
            part = shift_fsdp(part, step)
        for offset, piece in gather_context(part):
            cond_sum = lax.dynamic_update_slice(
                cond_sum,
                piece[None, None],
                ((here - step + along) % along, lax.axis_index(CONTEXT) ^ offset, 0, 0),
            )
    cond_sum = cond_sum.transpose(2, 0, 1, 3).reshape(seqs, along * size * rows)
    condition_grad = silu_pull(cond_sum)[0]
    skips_grad = jnp.stack(skip_grads, axis=0).reshape(skip_inputs.shape)

    spreads = (
        (2 * D) ** (-0.5),
        D ** (-0.5),
        D ** (-0.5),
        (D // 16) ** (-0.5),
        DT ** (-0.5),
        D ** (-0.5),
        FF ** (-0.5),
    )
    tokens_total = seqs * along * tokens * size * parts
    new_weights = []
    new_momenta = []
    new_averages = []
    for index in range(len(masters)):
        gradient = jnp.stack([gradients[layer][index] for layer in every], axis=0)
        rate = RATE_FACTOR * spreads[index] / math.sqrt(tokens_total)
        moment_new = MOMENTUM * momenta[index] + gradient
        weight_new = masters[index] - rate * (gradient + MOMENTUM * moment_new)
        new_weights.append(weight_new)
        new_momenta.append(moment_new)
        new_averages.append(
            AVERAGE_DECAY * averages[index] + (1.0 - AVERAGE_DECAY) * weight_new
        )
    return (
        block_output,
        grad_res.reshape(latents.shape),
        skips_grad,
        text_sum,
        condition_grad,
        *new_weights,
        *new_momenta,
        *new_averages,
    )


def solution(mesh):
    weight_specs = (
        P(None, (FSDP, CONTEXT), TENSOR),
        P(None, (FSDP, CONTEXT), TENSOR),
        P(None, (FSDP, CONTEXT), None, TENSOR),
        P(None, None, TENSOR, (FSDP, CONTEXT)),
        P(None, (FSDP, CONTEXT), None, TENSOR),
        P(None, (FSDP, CONTEXT), TENSOR),
        P(None, TENSOR, (FSDP, CONTEXT)),
    )
    in_specs = (
        P(FSDP, (CONTEXT, TENSOR), None),
        P(None, FSDP, (CONTEXT, TENSOR), None),
        P(FSDP, None, None),
        P(FSDP, None),
        P(FSDP, None, CONTEXT),
        P(FSDP, (CONTEXT, TENSOR), None),
    ) + weight_specs * 3
    out_specs = (
        P(FSDP, (CONTEXT, TENSOR), None),
        P(FSDP, (CONTEXT, TENSOR), None),
        P(None, FSDP, (CONTEXT, TENSOR), None),
        P(FSDP, None, None),
        P(FSDP, None),
    ) + weight_specs * 3
    return jax.shard_map(shards, mesh=mesh, in_specs=in_specs, out_specs=out_specs, check_vma=False)
```

```python
import math
from types import SimpleNamespace
import jax
import jax.numpy as jnp
from jax import lax
from jax.experimental import pallas as pl
from jax.experimental.pallas import tpu as pltpu
from jax.sharding import PartitionSpec as P

HD = 88
EPSILON = 1e-06
SCORE_SCALE = 1.0 / math.sqrt(HD)
LOW = jnp.bfloat16
MIB = 1 << 20


def vmem(mebibytes):
    return pltpu.CompilerParams(vmem_limit_bytes=mebibytes * MIB)


TOKEN = jax.ShapeDtypeStruct((8, 128), jnp.float32)
TOKEN_SPEC = pl.BlockSpec((8, 128), lambda *place: (0, 0))
FREE = pl.BlockSpec(memory_space=pl.ANY)
IN_HBM = pl.BlockSpec(memory_space=pltpu.HBM)
WHOLE = pl.BlockSpec(memory_space=pltpu.VMEM)


def cost(flops, moved, transcendentals=0):
    share = 1000
    return pl.CostEstimate(
        flops=flops // share,
        bytes_accessed=moved // share,
        transcendentals=transcendentals // share,
    )


def mark(token_ref):
    token_ref[...] = jnp.zeros(token_ref.shape, jnp.float32)


def gate(operand, after):
    return pl.pallas_call(
        lambda *refs: None,
        in_specs=[IN_HBM] + [IN_HBM] * len(after),
        out_specs=IN_HBM,
        out_shape=jax.ShapeDtypeStruct(operand.shape, operand.dtype),
        input_output_aliases={0: 0},
    )(operand, *after)


def contract(left, right, left_dim, right_dim):
    return lax.dot_general(
        left, right, (((left_dim,), (right_dim,)), ((), ())), preferred_element_type=jnp.float32
    )


def head(operand, index):
    return operand[:, index * HD : (index + 1) * HD]


def head_marks(width):
    heads = width // HD
    column = lax.broadcasted_iota(jnp.int32, (width, heads), 0)
    first = lax.broadcasted_iota(jnp.int32, (width, heads), 1) * HD
    return jnp.where((column >= first) & (column < first + HD), 1.0, 0.0).astype(LOW)


def halves(operand):
    upper = operand.astype(LOW)
    return upper, (operand - upper.astype(jnp.float32)).astype(LOW)


def head_mean(operand, marks):
    return contract(operand.astype(LOW), marks, 1, 0) / HD


def to_columns(operand, marks):
    upper, lower = halves(operand)
    return contract(upper, marks, 1, 1) + contract(lower, marks, 1, 1)


def root_factor(operand, marks):
    return to_columns(lax.rsqrt(head_mean(operand * operand, marks) + EPSILON), marks)


def root_back(operand, upstream, marks):
    factor = root_factor(operand, marks)
    normed = operand * factor
    mean = head_mean(upstream * normed, marks).astype(LOW)
    return factor * (upstream - normed * contract(mean, marks, 1, 1))


def swap_quarters(operand):
    quarter = HD // 4
    column = lax.broadcasted_iota(jnp.int32, operand.shape, 1)
    left = jnp.concatenate([operand[:, quarter:], operand[:, :quarter]], axis=-1)
    right = jnp.concatenate([operand[:, -quarter:], operand[:, :-quarter]], axis=-1)
    return jnp.where(column % (2 * quarter) < quarter, left, right)


def turn_kernel(query_ref, key_ref, cos_ref, sin_ref, *refs):
    query_out, key_out, token_ref = refs[-3:]
    mark(token_ref)
    cos, sin = cos_ref[...], sin_ref[...]
    marks = head_marks(cos.shape[1])
    for source, target in ((query_ref, query_out), (key_ref, key_out)):
        value = source[...]
        value = value * root_factor(value, marks)
        target[...] = (value * cos + swap_quarters(value) * sin).astype(LOW)


def row_blocks(operand):
    rows, width = operand.shape
    return pl.BlockSpec((min(rows, 128), width), lambda i: (i, 0))


def turn(query_raw, key_raw, cos, sin, after):
    rows, width = query_raw.shape
    spec = row_blocks(query_raw)
    shape = jax.ShapeDtypeStruct((rows, width), LOW)
    return pl.pallas_call(
        turn_kernel,
        grid=(rows // min(rows, 128),),
        in_specs=[spec] * 4 + [IN_HBM] * len(after),
        out_specs=[spec, spec, TOKEN_SPEC],
        out_shape=[shape, shape, TOKEN],
        compiler_params=vmem(32),
        cost_estimate=cost(100 * rows * width, 20 * rows * width),
    )(query_raw, key_raw, cos, sin, *after)


def turn_back_kernel(grad_ref, raw_ref, cos_ref, sin_ref, *refs):
    out_ref, token_ref = refs[-2:]
    mark(token_ref)
    cos, sin = cos_ref[...], sin_ref[...]
    grad = grad_ref[...].astype(jnp.float32)
    grad = grad * cos - swap_quarters(grad) * sin
    out_ref[...] = root_back(raw_ref[...], grad, head_marks(cos.shape[1])).astype(LOW)


def turn_back(grad, raw, cos, sin, after):
    rows, width = raw.shape
    spec = row_blocks(raw)
    return pl.pallas_call(
        turn_back_kernel,
        grid=(rows // min(rows, 128),),
        in_specs=[spec] * 4 + [IN_HBM] * len(after),
        out_specs=[spec, TOKEN_SPEC],
        out_shape=[jax.ShapeDtypeStruct((rows, width), LOW), TOKEN],
        compiler_params=vmem(32),
        cost_estimate=cost(100 * rows * width, 16 * rows * width),
    )(grad, raw, cos, sin, *after)


def root_kernel(raw_ref, *refs):
    out_ref, token_ref = refs[-2:]
    mark(token_ref)
    raw = raw_ref[...]
    out_ref[...] = (raw * root_factor(raw, head_marks(raw.shape[1]))).astype(LOW)


def root(raw, after):
    rows, width = raw.shape
    spec = row_blocks(raw)
    return pl.pallas_call(
        root_kernel,
        grid=(rows // min(rows, 128),),
        in_specs=[spec] + [IN_HBM] * len(after),
        out_specs=[spec, TOKEN_SPEC],
        out_shape=[jax.ShapeDtypeStruct((rows, width), LOW), TOKEN],
        compiler_params=vmem(32),
        cost_estimate=cost(50 * rows * width, 6 * rows * width),
    )(raw, *after)


def flat(ref):
    value = ref[...]
    return value.reshape(value.shape[0] * value.shape[2], value.shape[3])


def attend_kernel(count, query_ref, *refs):
    keys, values = refs[:count], refs[count : 2 * count]
    out_ref, lse_ref = refs[-2:]
    query = flat(query_ref)
    keys = [flat(ref) for ref in keys]
    values = [flat(ref) for ref in values]
    pieces = []
    for index in range(query.shape[1] // HD):
        query_head = head(query, index)
        scores = [contract(head(key, index), query_head, 1, 1) for key in keys]
        peak = scores[0].max(axis=0, keepdims=True)
        for score in scores[1:]:
            peak = jnp.maximum(peak, score.max(axis=0, keepdims=True))
        mass = 0.0
        out = 0.0
        for score, value in zip(scores, values):
            weight = jnp.exp((score - peak) * SCORE_SCALE)
            mass = mass + weight.sum(axis=0, keepdims=True)
            out = out + contract(head(value, index), weight.astype(LOW), 0, 0)
        pieces.append((out / mass).T.astype(LOW))
        lse_ref[0, index : index + 1, :] = peak * SCORE_SCALE + jnp.log(mass)
    out_ref[...] = jnp.concatenate(pieces, axis=-1).reshape(out_ref.shape)


def block_of(operand):
    parts, _, tokens, width = operand.shape
    return pl.BlockSpec((parts, 1, tokens, width), lambda s: (0, s, 0, 0))


def attend(query, keys, values, after):
    parts, seqs, tokens, width = query.shape
    heads = width // HD
    count = len(keys)
    pairs = seqs * heads * (parts * tokens) ** 2 * count
    return pl.pallas_call(
        lambda *refs: attend_kernel(count, *refs),
        grid=(seqs,),
        in_specs=[block_of(query)] * (1 + 2 * count) + [IN_HBM] * len(after),
        out_specs=[
            block_of(query),
            pl.BlockSpec((1, heads, parts * tokens), lambda s: (s, 0, 0)),
        ],
        out_shape=[
            jax.ShapeDtypeStruct(query.shape, LOW),
            jax.ShapeDtypeStruct((seqs, heads, parts * tokens), jnp.float32),
        ],
        compiler_params=vmem(48),
        cost_estimate=cost(8 * pairs * 128, 20 * query.size, pairs),
    )(query, *keys, *values, *after)


def attend_back_kernel(count, query_ref, raw_ref, grad_ref, lse_ref, cos_ref, sin_ref, *refs):
    key_refs, value_refs = refs[:count], refs[count : 2 * count]
    outs = refs[-2 * count - 2 :]
    query_out, key_outs, value_outs = outs[0], outs[1 : count + 1], outs[count + 1 : -1]
    mark(outs[-1])
    query, raw, grad = flat(query_ref), flat(raw_ref), flat(grad_ref)
    cos, sin = flat(cos_ref), flat(sin_ref)
    keys = [flat(ref) for ref in key_refs]
    values = [flat(ref) for ref in value_refs]
    query_pieces = []
    key_pieces = [[] for _ in keys]
    value_pieces = [[] for _ in keys]
    for index in range(query.shape[1] // HD):
        query_head, grad_head = head(query, index), head(grad, index)
        lse = lse_ref[0, index : index + 1, :]
        weights = []
        weight_grads = []
        delta = 0.0
        for key, value in zip(keys, values):
            weight = jnp.exp(contract(head(key, index), query_head, 1, 1) * SCORE_SCALE - lse)
            weight_grad = contract(head(value, index), grad_head, 1, 1)
            delta = delta + (weight * weight_grad).sum(axis=0, keepdims=True)
            weights.append(weight)
            weight_grads.append(weight_grad)
        query_grad = 0.0
        for place, key in enumerate(keys):
            weight = weights[place]
            score_grad = (weight * (weight_grads[place] - delta)).astype(LOW)
            query_grad = query_grad + contract(head(key, index), score_grad, 0, 0)
            key_pieces[place].append(
                (contract(score_grad, query_head, 1, 0) * SCORE_SCALE).astype(LOW)
            )
            value_pieces[place].append(contract(weight.astype(LOW), grad_head, 1, 0).astype(LOW))
        query_pieces.append(query_grad.T * SCORE_SCALE)
    query_grad = jnp.concatenate(query_pieces, axis=-1)
    query_grad = query_grad * cos - swap_quarters(query_grad) * sin
    query_grad = root_back(raw, query_grad, head_marks(raw.shape[1]))
    query_out[...] = query_grad.astype(LOW).reshape(query_out.shape)
    for target, pieces in zip(key_outs, key_pieces):
        target[...] = jnp.concatenate(pieces, axis=-1).reshape(target.shape)
    for target, pieces in zip(value_outs, value_pieces):
        target[...] = jnp.concatenate(pieces, axis=-1).reshape(target.shape)


def attend_back(query, raw, grad, lse, cos, sin, keys, values, after):
    parts, seqs, tokens, width = query.shape
    heads = width // HD
    count = len(keys)
    pairs = seqs * heads * (parts * tokens) ** 2 * count
    shape = jax.ShapeDtypeStruct(query.shape, LOW)
    spec = block_of(query)
    outs = pl.pallas_call(
        lambda *refs: attend_back_kernel(count, *refs),
        grid=(seqs,),
        in_specs=[
            spec,
            spec,
            spec,
            pl.BlockSpec((1, heads, parts * tokens), lambda s: (s, 0, 0)),
            block_of(cos),
            block_of(sin),
        ]
        + [spec] * (2 * count)
        + [IN_HBM] * len(after),
        out_specs=[spec] * (1 + 2 * count) + [TOKEN_SPEC],
        out_shape=[shape] * (1 + 2 * count) + [TOKEN],
        compiler_params=vmem(56),
        cost_estimate=cost(20 * pairs * 128, 40 * query.size, pairs),
    )(query, raw, grad, lse, cos, sin, *keys, *values, *after)
    return outs[0], list(outs[1 : 1 + count]), list(outs[1 + count : -1]), outs[-1]


def text_probs(query, key, index, count):
    scores = contract(head(key, index), head(query, index), 1, 1) * SCORE_SCALE
    inside = lax.broadcasted_iota(jnp.int32, scores.shape, 0) < count
    scores = jnp.where(inside, scores, -1e30)
    weight = jnp.exp(scores - scores.max(axis=0, keepdims=True))
    return weight / weight.sum(axis=0, keepdims=True)


def cross_kernel(count, raw_ref, key_ref, value_ref, *refs):
    out_ref, token_ref = refs[-2:]
    mark(token_ref)
    raw, key, value = raw_ref[0], key_ref[0], value_ref[0]
    query = (raw * root_factor(raw, head_marks(raw.shape[1]))).astype(LOW)
    pieces = []
    for index in range(value.shape[1] // HD):
        probs = text_probs(query, key, index, count)
        pieces.append(contract(head(value, index), probs.astype(LOW), 0, 0).T.astype(LOW))
    out_ref[0] = jnp.concatenate(pieces, axis=-1)


def sequence_block(operand):
    return pl.BlockSpec((1,) + operand.shape[1:], lambda s: (s, 0, 0))


def cross(query_raw, key, value, count, after):
    seqs, tokens, width = query_raw.shape
    pairs = seqs * tokens * key.shape[1] * (width // HD)
    return pl.pallas_call(
        lambda *refs: cross_kernel(count, *refs),
        grid=(seqs,),
        in_specs=[sequence_block(operand) for operand in (query_raw, key, value)]
        + [IN_HBM] * len(after),
        out_specs=[sequence_block(query_raw), TOKEN_SPEC],
        out_shape=[jax.ShapeDtypeStruct(query_raw.shape, LOW), TOKEN],
        compiler_params=vmem(32),
        cost_estimate=cost(8 * pairs * 128, 6 * query_raw.size + 4 * key.size, pairs),
    )(query_raw, key, value, *after)


def cross_back_kernel(count, raw_ref, key_raw_ref, key_ref, value_ref, grad_ref, *refs):
    query_out, key_out, value_out, token_ref = refs[-4:]
    mark(token_ref)
    raw, key_raw = raw_ref[0], key_raw_ref[0]
    key, value, grad = key_ref[0], value_ref[0], grad_ref[0]
    marks = head_marks(raw.shape[1])
    query = (raw * root_factor(raw, marks)).astype(LOW)
    query_pieces, key_pieces, value_pieces = [], [], []
    for index in range(value.shape[1] // HD):
        probs = text_probs(query, key, index, count)
        grad_head = head(grad, index)
        probs_grad = contract(head(value, index), grad_head, 1, 1)
        delta = (probs * probs_grad).sum(axis=0, keepdims=True)
        score_grad = (probs * (probs_grad - delta)).astype(LOW)
        query_pieces.append(contract(head(key, index), score_grad, 0, 0).T * SCORE_SCALE)
        key_pieces.append(contract(score_grad, head(query, index), 1, 0) * SCORE_SCALE)
        value_pieces.append(contract(probs.astype(LOW), grad_head, 1, 0).astype(LOW))
    query_grad = jnp.concatenate(query_pieces, axis=-1)
    query_out[0] = root_back(raw, query_grad, marks).astype(LOW)
    key_grad = jnp.concatenate(key_pieces, axis=-1)
    key_out[0] = root_back(key_raw, key_grad, marks).astype(LOW)
    value_out[0] = jnp.concatenate(value_pieces, axis=-1)


def cross_back(query_raw, key_raw, key, value, grad, count, after):
    seqs, tokens, width = query_raw.shape
    pairs = seqs * tokens * key_raw.shape[1] * (width // HD)
    return pl.pallas_call(
        lambda *refs: cross_back_kernel(count, *refs),
        grid=(seqs,),
        in_specs=[sequence_block(operand) for operand in (query_raw, key_raw, key, value, grad)]
        + [IN_HBM] * len(after),
        out_specs=[sequence_block(operand) for operand in (query_raw, key_raw, value)]
        + [TOKEN_SPEC],
        out_shape=[
            jax.ShapeDtypeStruct(operand.shape, LOW) for operand in (query_raw, key_raw, value)
        ]
        + [TOKEN],
        compiler_params=vmem(40),
        cost_estimate=cost(20 * pairs * 128, 10 * query_raw.size + 10 * key_raw.size, pairs),
    )(query_raw, key_raw, key, value, grad, *after)


def spread_kernel(cos_ref, sin_ref, cos_out, sin_out):
    for source, target in ((cos_ref, cos_out), (sin_ref, sin_out)):
        target[...] = jnp.concatenate([source[...]] * (target.shape[1] // HD), axis=-1)


def spread_heads(cos, sin, width):
    shape = jax.ShapeDtypeStruct((cos.shape[0], width), jnp.float32)
    return pl.pallas_call(
        spread_kernel,
        in_specs=[WHOLE] * 2,
        out_specs=[WHOLE] * 2,
        out_shape=[shape] * 2,
        compiler_params=vmem(32),
    )(cos, sin)


def add_kernel(count, cut, *refs):
    outs = refs[-count - 1 : -1]
    mark(refs[-1])
    for index in range(count):
        left, right = refs[2 * index][0], refs[2 * index + 1][0]
        total = left.astype(jnp.float32) + right.astype(jnp.float32)
        if cut:
            total = total.reshape(cut, -1, total.shape[1])
            outs[index][:, 0] = total.astype(LOW)
        else:
            outs[index][0] = total.astype(LOW)


def add_pairs(pairs, cut, after):
    count, rows, width = pairs[0][0].shape
    spec = pl.BlockSpec((1, rows, width), lambda j: (j, 0, 0))
    if cut:
        out_spec = pl.BlockSpec((cut, 1, rows // cut, width), lambda j: (0, j, 0, 0))
        shape = jax.ShapeDtypeStruct((cut, count, rows // cut, width), LOW)
    else:
        out_spec = spec
        shape = jax.ShapeDtypeStruct((count, rows, width), LOW)
    operands = [operand for pair in pairs for operand in pair]
    return pl.pallas_call(
        lambda *refs: add_kernel(len(pairs), cut, *refs),
        grid=(count,),
        in_specs=[spec] * len(operands) + [IN_HBM] * len(after),
        out_specs=[out_spec] * len(pairs) + [TOKEN_SPEC],
        out_shape=[shape] * len(pairs) + [TOKEN],
        compiler_params=vmem(40),
        cost_estimate=cost(len(pairs) * pairs[0][0].size, 6 * len(pairs) * pairs[0][0].size),
    )(*operands, *after)


D = 1408
FF = 6144
DT = 1024
MOMENTUM = 0.9
AVERAGE_DECAY = 0.8
RATE_FACTOR = 0.5
ROPE_BASE = 10000.0
PRECISE = lax.Precision.HIGHEST
FSDP, CONTEXT, TENSOR = "fsdp", "context", "tensor"
MESH = pl.DeviceIdType.MESH


def low(operand):
    return operand.astype(LOW)


def wide(operand):
    return operand.astype(jnp.float32)


def layer_norm(operand):
    centred = operand - jnp.mean(operand, axis=-1, keepdims=True)
    return centred * lax.rsqrt(jnp.mean(centred * centred, axis=-1, keepdims=True) + EPSILON)


def layer_norm_back(operand, upstream):
    centred = operand - jnp.mean(operand, axis=-1, keepdims=True)
    factor = lax.rsqrt(jnp.mean(centred * centred, axis=-1, keepdims=True) + EPSILON)
    normed = centred * factor
    return factor * (
        upstream
        - jnp.mean(upstream, axis=-1, keepdims=True)
        - normed * jnp.mean(upstream * normed, axis=-1, keepdims=True)
    )


CORE, CHIP = 1, 2


def in_rows(operand):
    rows, width = operand.shape[-2:]
    if width % 128 and rows % 128 == 0:
        return operand.reshape(-1, 8, width)
    return operand


def swap_context(operand, bit):
    size = lax.axis_size(CONTEXT)
    pairs = [(i, i ^ bit) for i in range(size)]
    return lax.ppermute(in_rows(operand), CONTEXT, pairs).reshape(operand.shape)


def swap_tensor(operand):
    return lax.ppermute(in_rows(operand), TENSOR, [(0, 1), (1, 0)]).reshape(operand.shape)


def shift_fsdp(operand, step):
    size = lax.axis_size(FSDP)
    return lax.ppermute(operand, FSDP, [(i, (i + step) % size) for i in range(size)])


def paired():
    return lax.axis_size(TENSOR) == 2


def tensor_order(own, other, axis):
    first = lax.axis_index(TENSOR) == 0
    return jnp.concatenate(
        [jnp.where(first, own, other), jnp.where(first, other, own)], axis=axis
    )


def gather_tensor(own):
    if paired():
        return [own, swap_tensor(own)]
    return [lax.all_gather(own, TENSOR, axis=0, tiled=True)]


def term_shapes(rows, width):
    if paired():
        return [(rows // 2, width, jnp.float32), (rows // 2, width, LOW)]
    return [(rows, width, LOW)]


def split_terms(total):
    return own_and_other(total) if paired() else [total]


def sum_tensor(terms):
    if paired():
        return terms[0] + wide(swap_tensor(terms[1]))
    return wide(lax.psum_scatter(terms[0], TENSOR, scatter_dimension=0, tiled=True))


def columns_of(operand):
    parts = jnp.split(operand, lax.axis_size(TENSOR), axis=-1)
    if paired():
        first = lax.axis_index(TENSOR) == 0
        return [jnp.where(first, parts[0], parts[1]), jnp.where(first, parts[1], parts[0])]
    return parts


def join_columns(parts):
    if paired():
        return tensor_order(parts[0], parts[1], -1)
    return jnp.concatenate(parts, axis=-1)


def gather_fsdp_small(own):
    size = lax.axis_size(FSDP)
    place = lax.axis_index(FSDP)
    out = jnp.zeros((size,) + own.shape, own.dtype)
    out = lax.dynamic_update_index_in_dim(out, own, place, 0)
    for step in range(1, size):
        out = lax.dynamic_update_index_in_dim(
            out, shift_fsdp(own, step), (place - step + size) % size, 0
        )
    return out


def sum_fsdp_small(parts):
    size = lax.axis_size(FSDP)
    place = lax.axis_index(FSDP)
    total = lax.dynamic_index_in_dim(parts, place, 0, keepdims=False)
    for step in range(1, size):
        part = lax.dynamic_index_in_dim(parts, (place + step) % size, 0, keepdims=False)
        total = total + shift_fsdp(part, step)
    return total


def sum_context(total):
    for bit in (CORE, CHIP):
        total = total + swap_context(total, bit)
    return total


def gather_context(own):
    parts = [(0, own)]
    for bit in (CHIP, CORE):
        parts = parts + [(offset ^ bit, swap_context(part, bit)) for offset, part in parts]
    return parts


def multiply(body, lefts, rights, turned, extras, outs, after, tile=512):
    width = outs[0][1]
    tile = min(tile, width)
    counts = [len(lefts), len(rights), len(extras)]
    first, second, third = counts[0], sum(counts[:2]), sum(counts)

    def kernel(*refs):
        results, token_ref = refs[-len(outs) - 1 : -1], refs[-1]
        mark(token_ref)
        values = [ref[...] for ref in refs[:third]]
        for result, value in zip(
            results, body(values[:first], values[first:second], values[second:third])
        ):
            result[...] = value.astype(result.dtype)

    def column_block(rows):
        return pl.BlockSpec((rows, tile), lambda j: (0, j))

    def right_block(right):
        if turned:
            return pl.BlockSpec((tile, right.shape[1]), lambda j: (j, 0))
        return column_block(right.shape[0])

    flops = 2 * sum(right.size for right in rights) * outs[0][0]
    return pl.pallas_call(
        kernel,
        grid=(pl.cdiv(width, tile),),
        in_specs=[pl.BlockSpec(left.shape, lambda j: (0, 0)) for left in lefts]
        + [right_block(right) for right in rights]
        + [column_block(extra.shape[0]) for extra in extras]
        + [IN_HBM] * len(after),
        out_specs=[column_block(rows) for rows, _, _ in outs] + [TOKEN_SPEC],
        out_shape=[jax.ShapeDtypeStruct((rows, wide_by), kind) for rows, wide_by, kind in outs]
        + [TOKEN],
        compiler_params=vmem(40),
        cost_estimate=cost(flops, 2 * sum(right.size for right in rights)),
    )(*lefts, *rights, *extras, *after)


def stacked(pieces, right, dim):
    parts = [contract(piece, right, 1, dim) for piece in pieces]
    return parts[0] if len(parts) == 1 else jnp.concatenate(parts, axis=0)


def own_and_other(total):
    rows = total.shape[0] // 2
    return [total[:rows], total[rows:]]


GELU_SCALE, GELU_CUBE = math.sqrt(2.0 / math.pi), 0.044715


def gelu(value):
    return 0.5 * value * (1.0 + jnp.tanh(GELU_SCALE * (value + GELU_CUBE * value**3)))


def gelu_slope(value):
    bend = jnp.tanh(GELU_SCALE * (value + GELU_CUBE * value**3))
    slope = GELU_SCALE * (1.0 + 3.0 * GELU_CUBE * value * value)
    return 0.5 * (1.0 + bend) + 0.5 * value * (1.0 - bend * bend) * slope


def meet_core():
    place = lax.axis_index(CONTEXT)
    other = {CONTEXT: place + 1 - 2 * (place % 2)}
    barrier = pltpu.get_barrier_semaphore()
    pl.semaphore_signal(barrier, inc=1, device_id=other, device_id_type=MESH)
    pl.semaphore_wait(barrier, 1)
    return other


FAR = "far"


def partner(kind):
    if isinstance(kind, list):
        return {**partner(kind[0]), **partner(kind[1])}
    return partner_on_axis(kind)


def partner_on_axis(kind):
    place = lax.axis_index(CONTEXT)
    if kind == TENSOR:
        return {TENSOR: 1 - lax.axis_index(TENSOR)}
    if kind == CORE:
        return {CONTEXT: place + 1 - 2 * (place % 2)}
    if kind == CHIP:
        return {CONTEXT: (place + CHIP) % 4}
    if kind == FAR:
        return {CONTEXT: (place + CHIP + 1 - 2 * (place % 2)) % 4}
    size = lax.axis_size(FSDP)
    return {FSDP: (lax.axis_index(FSDP) + kind[0]) % size}


def meet(kinds):
    barrier = pltpu.get_barrier_semaphore()
    for kind in kinds:
        pl.semaphore_signal(barrier, inc=1, device_id=partner(kind), device_id_type=MESH)
    pl.semaphore_wait(barrier, len(kinds))


def sending(source, target, sems, index, kind):
    return pltpu.make_async_remote_copy(
        src_ref=source,
        dst_ref=target,
        send_sem=sems.at[0, index],
        recv_sem=sems.at[1, index],
        device_id=partner(kind),
        device_id_type=MESH,
    )


def distinct(kinds):
    return [kind for index, kind in enumerate(kinds) if kind not in kinds[:index]]


def exchange_kernel(kinds, *refs):
    count = len(kinds)
    sources, targets, token_ref, sems = refs[:count], refs[-count - 2 : -2], refs[-2], refs[-1]
    mark(token_ref)
    meet(distinct(kinds))
    copies = [
        sending(source, target, sems, index, kind)
        for index, (source, target, kind) in enumerate(zip(sources, targets, kinds))
    ]
    for copy in copies:
        copy.start()
    for copy in copies:
        copy.wait()


def exchange(items, after, ident):
    operands, kinds = zip(*items)
    return pl.pallas_call(
        lambda *refs: exchange_kernel(list(kinds), *refs),
        in_specs=[FREE] * len(items) + [IN_HBM] * len(after),
        out_specs=[FREE] * len(items) + [WHOLE],
        out_shape=[jax.ShapeDtypeStruct(operand.shape, operand.dtype) for operand in operands]
        + [TOKEN],
        scratch_shapes=[pltpu.SemaphoreType.DMA((2, len(items)))],
        compiler_params=pltpu.CompilerParams(
            collective_id=ident, has_side_effects=True, vmem_limit_bytes=16 * MIB
        ),
        cost_estimate=cost(0, 0),
    )(*operands, *after)


def share_kernel(count, places, *refs):
    widths = len(places)
    total = 1 + places[-1][0]
    sources, outs = refs[:count], refs[-count // 2 * total - 4 :]
    targets, token_ref = outs[:-4], outs[-4]
    local_sem, send_sem, recv_sem = outs[-3:]
    mark(token_ref)
    place = lax.axis_index(CONTEXT)
    other = meet_core()
    copies = []
    for source_at in range(count):
        part, chip = source_at // 2, source_at % 2
        slot = (place + CHIP * chip) % 4
        for index in range(widths):
            sem = source_at * widths + index
            source = sources[source_at].at[:, index]
            out_at, half = places[index]
            target = targets[part * total + out_at]
            target = target.at[:, slot] if half is None else target.at[:, slot, half]
            remote = pltpu.make_async_remote_copy(
                src_ref=source,
                dst_ref=target,
                send_sem=send_sem.at[sem],
                recv_sem=recv_sem.at[sem],
                device_id=other,
                device_id_type=MESH,
            )
            remote.start()
            own = pltpu.make_async_copy(source, target, local_sem.at[sem])
            own.start()
            copies += [remote, own]
    for copy in copies:
        copy.wait()


def share_core(pieces, after, ident, halved=False):
    along, widths, rows, width = pieces[0].shape
    count = len(pieces)
    size = lax.axis_size(CONTEXT)
    places = [(index, None) for index in range(widths)]
    shapes = [(along, size, rows, width)] * widths
    if halved:
        places = [(0, 0), (0, 1)] + [(index, None) for index in range(1, widths - 1)]
        shapes = [(along, size, 2, rows, width)] + shapes[2:]
    total = count // 2 * len(shapes)
    outs = pl.pallas_call(
        lambda *refs: share_kernel(count, places, *refs),
        in_specs=[WHOLE] * count + [IN_HBM] * len(after),
        out_specs=[IN_HBM] * total + [WHOLE],
        out_shape=[jax.ShapeDtypeStruct(shape, LOW) for shape in shapes] * (count // 2) + [TOKEN],
        scratch_shapes=[pltpu.SemaphoreType.DMA((count * widths,))] * 3,
        compiler_params=pltpu.CompilerParams(
            collective_id=ident, has_side_effects=True, vmem_limit_bytes=40 * MIB
        ),
        cost_estimate=cost(0, 6 * count * pieces[0].size * 2),
    )(*pieces, *after)
    held = [out.reshape(-1, width) for out in outs[:-1]]
    each = len(shapes)
    return [held[part * each : (part + 1) * each] for part in range(count // 2)], outs[-1]


def pack_of(shards):
    return jnp.stack([low(shard) for shard in shards], axis=0)


def gather_fsdp(shards, after):
    return lax.all_gather(gate(pack_of(shards), after), FSDP, axis=0, tiled=False)


def across(along, spread, after):
    along = gate(along, after) if after else along
    parts = [along, swap_context(along, CHIP)]
    if not spread:
        return parts
    if paired():
        first = swap_tensor(along)
        parts[1] = gate(parts[1], (first,))
        return parts + [first, swap_tensor(parts[1])]
    many = [lax.all_gather(part, TENSOR, axis=0) for part in parts]
    return [part[i] for i in range(lax.axis_size(TENSOR)) for part in many]


class Order:
    def __init__(self):
        self.after = ()
        self.count = 0

    def ident(self):
        self.count += 1
        return self.count - 1

    def need(self, *operands):
        self.after = self.after + operands

    def put(self, outs):
        *outs, token = outs
        self.after = (token,)
        return outs

    def multiply(self, body, lefts, rights, turned, extras, outs, tile=512):
        return self.put(multiply(body, lefts, rights, turned, extras, outs, self.after, tile))


def grad_kernel(which, spread, tile, counts, waits, *refs):
    count = sum(counts)
    lefts, rights = refs[:count], refs[count : count + len(which)]
    outs = refs[count + len(which) + waits :]
    kept, given = outs[: max(spread, 1)], outs[max(spread, 1) : 2 * max(spread, 1)]
    token_ref = outs[2 * max(spread, 1)]
    turned, cut, sent, came, send_sem, recv_sem = outs[2 * max(spread, 1) + 1 :]
    mark(token_ref)
    other = meet_core()
    place = lax.axis_index(CONTEXT)
    tiles = rights[0].shape[1] // tile
    rows = cut.shape[3]
    along = lax.axis_size(FSDP)
    block = rows // along
    for index, pieces in enumerate(counts):
        start = sum(counts[:index])
        depth = 0
        for left in lefts[start : start + pieces]:
            turned[:, depth : depth + left.shape[0]] = left[...].astype(jnp.float32).T
            depth += left.shape[0]
        for core in range(2):
            for chip in range(2):
                at = (place // 2 + chip) % 2 * 2 + (place % 2 + core) % 2
                pieces = [
                    turned[pl.ds(pl.multiple_of((4 * z + at) * block, 8), block), :]
                    for z in range(along)
                ]
                cut[index, core, chip] = low(jnp.concatenate(pieces, axis=0))
    units = []
    for job, left in enumerate(which):
        for chip in range(2):
            out = (kept, given)[chip]
            out = out[job % spread].at[job // spread] if spread else out[0].at[job]
            units.append((left, rights[job], chip, out))

    def columns(index):
        if isinstance(index, int):
            return pl.ds(index * tile, tile)
        return pl.ds(pl.multiple_of(index * tile, tile), tile)

    def copy(unit, index):
        sem = unit * tiles + index
        return pltpu.make_async_remote_copy(
            src_ref=sent.at[unit, index],
            dst_ref=came.at[unit, index],
            send_sem=send_sem.at[sem],
            recv_sem=recv_sem.at[sem],
            device_id=other,
            device_id_type=MESH,
        )

    def each(step):
        if tiles == 1:
            step(0)
        else:
            lax.fori_loop(0, tiles, lambda index, carry: (step(index), carry)[1], 0)

    for unit, (left, right, chip, out) in enumerate(units):

        def give(index, unit=unit, left=left, right=right, chip=chip):
            sent[unit, index] = low(contract(cut[left, 1, chip], right[:, columns(index)], 1, 0))
            copy(unit, index).start()

        each(give)
    for unit, (left, right, chip, out) in enumerate(units):

        def keep(index, unit=unit, left=left, right=right, chip=chip, out=out):
            term = contract(cut[left, 0, chip], right[:, columns(index)], 1, 0)
            copy(unit, index).wait_recv()
            out[:, columns(index)] = low(term + wide(came[unit, index]))

        each(keep)
    for unit in range(len(units)):

        def done(index, unit=unit):
            copy(unit, index).wait_send()

        each(done)


def grad_core(lefts, rights, which, spread, after, ident):
    depth, width = rights[0].shape
    counts = [len(pieces) for pieces in lefts]
    lefts = [piece for pieces in lefts for piece in pieces]
    features = lefts[0].shape[1]
    rows = features // 4
    jobs = len(which)
    count = max(spread, 1)
    tile = width
    for candidate in (512, 384):
        if width > 1408 and width % candidate == 0:
            tile = candidate
            break
    tiles = width // tile
    shape = jax.ShapeDtypeStruct((jobs // count, rows, width), LOW)
    outs = pl.pallas_call(
        lambda *refs: grad_kernel(which, spread, tile, counts, len(after), *refs),
        in_specs=[WHOLE] * (len(lefts) + jobs) + [IN_HBM] * len(after),
        out_specs=[WHOLE] * (2 * count + 1),
        out_shape=[shape] * (2 * count) + [TOKEN],
        scratch_shapes=[
            pltpu.VMEM((features, depth), jnp.float32),
            pltpu.VMEM((len(counts), 2, 2, rows, depth), LOW),
            pltpu.VMEM((2 * jobs, tiles, rows, tile), LOW),
            pltpu.VMEM((2 * jobs, tiles, rows, tile), LOW),
            pltpu.SemaphoreType.DMA((2 * jobs * tiles,)),
            pltpu.SemaphoreType.DMA((2 * jobs * tiles,)),
        ],
        compiler_params=pltpu.CompilerParams(
            collective_id=ident, has_side_effects=True, vmem_limit_bytes=56 * MIB
        ),
        cost_estimate=cost(8 * jobs * rows * width * depth, 6 * jobs * width * rows),
    )(*lefts, *rights, *after)
    if spread:
        return list(outs[:count]), list(outs[count:-1]), outs[-1]
    return outs


def sum_parts(kept, given, order):
    if paired():
        pairs = [(kept[0], swap_tensor(kept[1])), (given[0], swap_tensor(given[1]))]
        return order.put(add_pairs(pairs, 0, order.after))
    return [
        lax.psum_scatter(jnp.stack(parts), TENSOR, scatter_dimension=0, tiled=False)
        for parts in (kept, given)
    ]


def sum_rest(kept, came, order):
    (total,) = order.put(add_pairs([(kept, came)], lax.axis_size(FSDP), order.after))
    return lax.psum_scatter(total, FSDP, scatter_dimension=0, tiled=False)


def sum_text(total):
    place = lax.axis_index(CONTEXT)
    steps = [
        (lambda operand: swap_context(operand, CORE), place % 2),
        (lambda operand: swap_context(operand, CHIP), place // 2),
    ]
    if paired():
        steps.append((swap_tensor, lax.axis_index(TENSOR)))
    for swap, bit in steps:
        half = total.shape[0] // 2
        kept = lax.dynamic_slice_in_dim(total, bit * half, half, axis=0)
        given = lax.dynamic_slice_in_dim(total, (1 - bit) * half, half, axis=0)
        total = low(wide(kept) + wide(swap(given)))
    if not paired():
        total = lax.psum(total, TENSOR)
    for swap, bit in reversed(steps):
        other = swap(total)
        first = bit == 0
        total = jnp.concatenate(
            [jnp.where(first, total, other), jnp.where(first, other, total)], axis=0
        )
    return total


def per_token(operand, rows):
    seqs, _, width = operand.shape
    return jnp.broadcast_to(operand, (seqs, rows // seqs, width)).reshape(rows, width)


def per_sequence(operand, seqs):
    return operand.reshape(seqs, -1, operand.shape[-1]).sum(axis=1)


def layer_forward(residual, skip_rows, modulation, text, tables, weights, order, steps):
    rows, features = residual.shape
    parts = lax.axis_size(TENSOR)
    every = rows * parts
    seqs = modulation[0].shape[0]
    shift_a, scale_a, gate_a, shift_m, scale_m, gate_m = [
        per_token(piece, rows) for piece in modulation
    ]
    cos, sin = tables
    kept = SimpleNamespace()
    kept.concat = jnp.concatenate([residual, wide(skip_rows)], axis=-1)
    kept.concat_low = low(layer_norm(kept.concat))
    width = weights.skip[0].shape[1]
    skipped = order.multiply(
        lambda lefts, rights, _: [contract(lefts[0], right, 1, 0) for right in rights],
        [kept.concat_low],
        weights.skip,
        False,
        [],
        [(rows, width, LOW)] * parts,
    )
    after_skip = wide(join_columns(skipped))
    kept.after_skip = after_skip
    kept.attn_all = gather_tensor(low(layer_norm(after_skip) * (1.0 + scale_a) + shift_a))
    steps.skipped()
    kept.query_raw, kept.key_raw, value_low = order.multiply(
        lambda lefts, rights, _: [stacked(lefts, right, 0) for right in rights],
        kept.attn_all,
        [weights.query, weights.key, weights.value],
        False,
        [],
        [(every, width, jnp.float32)] * 2 + [(every, width, LOW)],
    )
    blocks = (parts, seqs, rows // seqs, width)
    query_low, key_low = order.put(turn(kept.query_raw, kept.key_raw, cos, sin, order.after))
    kept.query_low = query_low.reshape(blocks)
    kept.keys = [part.reshape(blocks) for _, part in gather_context(key_low)]
    kept.values = [part.reshape(blocks) for _, part in gather_context(value_low)]
    steps.turned()
    attn_low, kept.attn_lse = attend(kept.query_low, kept.keys, kept.values, order.after)
    order.after = (kept.attn_lse,)
    kept.attn_low = attn_low.reshape(-1, width)
    terms = order.multiply(
        lambda lefts, rights, _: split_terms(contract(lefts[0], rights[0], 1, 1)),
        [kept.attn_low],
        [weights.attn_out],
        True,
        [],
        term_shapes(every, features),
    )
    kept.attn_branch = sum_tensor(terms)
    steps.attended()
    kept.after_attn = after_skip + gate_a * kept.attn_branch
    kept.cross_in = low(layer_norm(kept.after_attn))
    raws = order.multiply(
        lambda lefts, rights, _: [contract(lefts[0], right, 1, 0) for right in rights],
        [kept.cross_in],
        weights.cross_query,
        False,
        [],
        [(rows, width, jnp.float32)] * parts,
    )
    kept.cross_raw = [raw.reshape(blocks[1:]) for raw in raws]
    kept.cross_low = []
    for raw, key, value in zip(kept.cross_raw, text.keys, text.values):
        (out,) = order.put(cross(raw, key, value, text.count, order.after))
        kept.cross_low.append(out.reshape(rows, width))
    (kept.after_cross,) = order.multiply(
        lambda lefts, rights, extras: [
            sum((contract(left, right, 1, 1) for left, right in zip(lefts, rights)), extras[0])
        ],
        kept.cross_low,
        weights.cross_out,
        True,
        [kept.after_attn],
        [(rows, features, jnp.float32)],
    )
    after_cross = kept.after_cross
    kept.mlp_all = gather_tensor(low(layer_norm(after_cross) * (1.0 + scale_m) + shift_m))
    steps.crossed()

    def raise_and_bend(lefts, rights, _):
        upward = stacked(lefts, rights[0], 0)
        return [upward, gelu(upward)]

    hidden = weights.up.shape[1]
    kept.upward, kept.hidden_low = order.multiply(
        raise_and_bend,
        kept.mlp_all,
        [weights.up],
        False,
        [],
        [(every, hidden, jnp.float32), (every, hidden, LOW)],
    )
    steps.raised()
    terms = order.multiply(
        lambda lefts, rights, _: split_terms(contract(lefts[0], rights[0], 1, 1)),
        [kept.hidden_low],
        [weights.down],
        True,
        [],
        term_shapes(every, features),
    )
    kept.mlp_branch = sum_tensor(terms)
    steps.lowered()
    return after_cross + gate_m * kept.mlp_branch, kept


def modulate(columns):
    if paired():
        total = columns[0] + swap_tensor(columns[1])
    else:
        total = lax.psum_scatter(jnp.stack(columns), TENSOR, scatter_dimension=0, tiled=False)
    mod_all = gather_fsdp_small(sum_context(total))
    return mod_all.reshape(-1, mod_all.shape[-1])


def layer_backward(grad_res, kept, weights, modulation, tables, text, text_low, order, earlier, last):
    rows, features = grad_res.shape
    parts = lax.axis_size(TENSOR)
    every = rows * parts
    seqs = modulation[0].shape[0]
    shift_a, scale_a, gate_a, shift_m, scale_m, gate_m = [
        per_token(piece, rows) for piece in modulation
    ]
    cos, sin = tables
    reduced = SimpleNamespace()

    def product(lefts, rights, which, spread):
        outs = order.put(grad_core(lefts, rights, which, spread, order.after, order.ident()))
        return outs if spread else (outs[0], swap_context(outs[1], CHIP))

    mlp_grad = gather_tensor(low(gate_m * grad_res))
    earlier.start()
    grad_gate_m = per_sequence(grad_res * kept.mlp_branch, seqs)
    (up_grad,) = order.multiply(
        lambda lefts, rights, extras: [stacked(lefts, rights[0], 0) * gelu_slope(extras[0])],
        mlp_grad,
        [weights.down],
        False,
        [kept.upward],
        [(every, kept.upward.shape[1], LOW)],
    )
    terms = order.multiply(
        lambda lefts, rights, _: split_terms(contract(lefts[0], rights[0], 1, 1)),
        [up_grad],
        [weights.up],
        True,
        [],
        term_shapes(every, features),
    )
    mlp_in_grad = sum_tensor(terms)
    order.need(*earlier.sums())
    down = product([mlp_grad], [kept.hidden_low], (0,), 0)
    earlier.first()
    up = product([kept.mlp_all], [up_grad], (0,), 0)
    grad_shift_m = per_sequence(mlp_in_grad, seqs)
    grad_scale_m = per_sequence(mlp_in_grad * layer_norm(kept.after_cross), seqs)
    grad_res = grad_res + layer_norm_back(kept.after_cross, mlp_in_grad * (1.0 + scale_m))

    cross_grad = low(grad_res)
    width = weights.cross_out[0].shape[1]
    out_grads = order.multiply(
        lambda lefts, rights, _: [contract(lefts[0], right, 1, 0) for right in rights],
        [cross_grad],
        weights.cross_out,
        False,
        [],
        [(rows, width, LOW)] * parts,
    )
    cross_q, text_key_grad, text_value_grad = [], [], []
    for part, out_grad in enumerate(out_grads):
        raw = kept.cross_raw[part]
        query_grad, key_grad, value_grad = order.put(
            cross_back(
                raw,
                text.raws[part],
                text.keys[part],
                text.values[part],
                out_grad.reshape(raw.shape),
                text.count,
                order.after,
            )
        )
        cross_q.append(query_grad.reshape(rows, width))
        text_key_grad.append(key_grad.reshape(-1, width))
        text_value_grad.append(value_grad.reshape(-1, width))
    (cross_in_grad,) = order.multiply(
        lambda lefts, rights, _: [
            sum(contract(left, right, 1, 1) for left, right in zip(lefts, rights))
        ],
        cross_q,
        weights.cross_query,
        True,
        [],
        [(rows, features, jnp.float32)],
    )
    grad_res = grad_res + layer_norm_back(kept.after_attn, cross_in_grad)

    attn_grad = gather_tensor(low(gate_a * grad_res))
    earlier.second()
    grad_gate_a = per_sequence(grad_res * kept.attn_branch, seqs)
    crossed = product(
        [[cross_grad], [kept.cross_in]],
        kept.cross_low + cross_q,
        (0,) * parts + (1,) * parts,
        parts,
    )
    texts = product([[text_low]], text_key_grad + text_value_grad, (0,) * (2 * parts), parts)
    (out_grad,) = order.multiply(
        lambda lefts, rights, _: [stacked(lefts, rights[0], 0)],
        attn_grad,
        [weights.attn_out],
        False,
        [],
        [(every, width, LOW)],
    )
    blocks = kept.query_low.shape
    order.need(*earlier.more())
    query_grad, key_parts, value_parts = order.put(
        attend_back(
            kept.query_low,
            kept.query_raw.reshape(blocks),
            out_grad.reshape(blocks),
            kept.attn_lse,
            cos.reshape(blocks),
            sin.reshape(blocks),
            kept.keys,
            kept.values,
            order.after,
        )
    )
    query_grad = query_grad.reshape(-1, width)

    key_parts, value_parts = [
        [piece.reshape(1, -1, width) for piece in pieces] for pieces in (key_parts, value_parts)
    ]
    near = [
        (pieces[place], swap_context(pieces[place + 2], CORE))
        for pieces in (key_parts, value_parts)
        for place in range(2)
    ]
    reduced.down = sum_rest(*down, order)
    key_near, key_far, value_near, value_far = order.put(add_pairs(near, 0, order.after))
    whole = [
        (key_near, swap_context(key_far, CHIP)),
        (value_near, swap_context(value_far, CHIP)),
    ]
    reduced.up = sum_rest(*up, order)
    (text_part,) = order.multiply(
        lambda lefts, rights, _: [
            sum(contract(left, right, 1, 1) for left, right in zip(lefts, rights))
        ],
        text_key_grad + text_value_grad,
        weights.text_key + weights.text_value,
        True,
        [],
        [(text_low.shape[0], text_low.shape[1], jnp.float32)],
        256,
    )
    earlier.third()
    key_grad, value_grad = order.put(add_pairs(whole, 0, order.after))
    (key_grad,) = order.put(turn_back(key_grad[0], kept.key_raw, cos, sin, order.after))
    value_grad = value_grad[0]
    terms = order.multiply(
        lambda lefts, rights, _: split_terms(
            sum(contract(left, right, 1, 1) for left, right in zip(lefts, rights))
        ),
        [query_grad, key_grad, value_grad],
        [weights.query, weights.key, weights.value],
        True,
        [],
        term_shapes(every, features),
    )
    attn_in_grad = sum_tensor(terms)
    order.need(*earlier.most())
    attn_own, attn_given = order.put(
        grad_core(
            [attn_grad, kept.attn_all],
            [kept.attn_low, query_grad, key_grad, value_grad],
            (0, 1, 1, 1),
            0,
            order.after,
            order.ident(),
        )
    )
    attended = (attn_own,) if last else (attn_own, swap_context(attn_given, CHIP))
    crossed = sum_parts(*crossed, order)
    crossed = (crossed[0], swap_context(crossed[1], CHIP))
    if last:
        texts = sum_parts(*texts, order)
        texts = (texts[0], swap_context(texts[1], CHIP))
    grad_shift_a = per_sequence(attn_in_grad, seqs)
    grad_scale_a = per_sequence(attn_in_grad * layer_norm(kept.after_skip), seqs)
    grad_res = grad_res + layer_norm_back(kept.after_skip, attn_in_grad * (1.0 + scale_a))

    skip_grad = columns_of(low(grad_res))
    (concat_grad,) = order.multiply(
        lambda lefts, rights, _: [
            sum(contract(left, right, 1, 1) for left, right in zip(lefts, rights))
        ],
        skip_grad,
        weights.skip,
        True,
        [],
        [(rows, 2 * features, jnp.float32)],
    )
    mod_grad = jnp.concatenate(
        [grad_shift_a, grad_scale_a, grad_gate_a, grad_shift_m, grad_scale_m, grad_gate_m], axis=-1
    )
    later = SimpleNamespace()

    def start():
        later.skipped = product([[kept.concat_low]], skip_grad, (0,) * parts, parts)
        reduced.cross = sum_rest(*crossed, order)
        later.texts = sum_parts(*texts, order)
        later.texts = (later.texts[0], swap_context(later.texts[1], CHIP))

    def first():
        reduced.attention = sum_rest(*attended, order)

    def second():
        reduced.text = sum_rest(*later.texts, order)
        kept, given = sum_parts(*later.skipped, order)
        later.skipped = (kept, swap_context(given, CHIP))

    def third():
        reduced.skip = sum_rest(*later.skipped, order)

    def end(text_total):
        if not last:
            start()
            first()
            second()
            third()
            return modulate(columns_of(mod_grad)), sum_text(text_total)
        order.need(reduced.up)
        (own, other), (chip_own, chip_other) = product(
            [[kept.concat_low]], skip_grad, (0,) * parts, parts
        )
        order.need(*earlier.rest())
        reduced.cross = sum_rest(*crossed, order)
        reduced.text = sum_rest(*texts, order)
        columns = columns_of(mod_grad)
        came = order.put(
            exchange(
                [
                    (other, TENSOR),
                    (chip_other, TENSOR),
                    (attn_given, CHIP),
                    (columns[1], TENSOR),
                ],
                order.after,
                order.ident(),
            )
        )
        columns_came = came[3]
        order.need(reduced.cross, reduced.text)
        reduced.attention = sum_rest(attended[0], came[2], order)
        own, chip_own = order.put(
            add_pairs([(own, came[0]), (chip_own, came[1])], 0, order.after)
        )
        total = columns[0] + columns_came
        chip_came, *totals = order.put(
            exchange(
                [(chip_own, CHIP), (total, CHIP), (total, CORE), (total, FAR)],
                order.after,
                order.ident(),
            )
        )
        text_total = gate(text_total, order.after)
        order.need(reduced.attention)
        reduced.skip = sum_rest(own, chip_came, order)
        mod_all = gather_fsdp_small(total + totals[0] + totals[1] + totals[2])
        return mod_all.reshape(-1, mod_all.shape[-1]), sum_text(text_total)

    later.start, later.first, later.second, later.third = start, first, second, third
    later.end = end
    concat_grad = layer_norm_back(kept.concat, concat_grad)
    later.columns = lambda: modulate(columns_of(mod_grad))
    later.sums = lambda: (reduced.down, reduced.up)
    later.more = lambda: (reduced.cross, reduced.attention)
    later.most = lambda: (reduced.text,)
    later.rest = lambda: (reduced.skip,)
    return concat_grad[:, :features], concat_grad[:, features:], text_part, reduced, later


def shards(
    latents,
    skip_inputs,
    text_states,
    condition,
    positions,
    cotangent,
    *tensors,
):
    masters, momenta, averages = tensors[:7], tensors[7:14], tensors[14:]
    (
        skip_weight,
        mod_weight,
        proj_weight,
        output_weight,
        text_weight,
        up_weight,
        down_weight,
    ) = masters
    layers = skip_weight.shape[0]
    along = lax.axis_size(FSDP)
    size = lax.axis_size(CONTEXT)
    parts = lax.axis_size(TENSOR)
    seqs, tokens = latents.shape[0], latents.shape[1]
    text_count = text_states.shape[1]
    every = range(layers)

    def cross_of(layer):
        return [proj_weight[layer, :, 3], output_weight[layer, 1].T]

    def halves_of(shard):
        half = shard.shape[0] // 2
        return [shard[:half], shard[half:]]

    def attention_of(layer):
        return [proj_weight[layer, :, j] for j in range(3)] + [output_weight[layer, 0].T]

    order = Order()
    weights = [SimpleNamespace() for _ in every]
    skip_along = gather_fsdp_small(pack_of([skip_weight[0]]))
    arrived = (skip_along,)
    skip_parts = across(skip_along, True, ())
    started = (skip_parts[1],)
    mixed = gather_fsdp(attention_of(0) + cross_of(0), arrived)
    attention, crosses, skips = [mixed[:, :4]], [mixed[:, 4:]], [None]
    text_along = gather_fsdp([text_weight[i, :, j] for i in every for j in range(2)], arrived)
    ups = [gather_fsdp([up_weight[0]], arrived)]
    downs = [gather_fsdp([down_weight[0].T], arrived)]
    for layer in every[1:]:
        mixed = gather_fsdp(
            attention_of(layer) + cross_of(layer) + halves_of(skip_weight[layer]), started
        )
        attention.append(mixed[:, :4])
        crosses.append(mixed[:, 4:6])
        skips.append(mixed[:, 6:])
        ups.append(gather_fsdp([up_weight[layer]], started))
        downs.append(gather_fsdp([down_weight[layer].T], started))

    attention_parts, cross_parts, up_parts, down_parts = {}, {}, {}, {}
    skip_parts = {0: skip_parts}

    def hold_skip(layer):
        (held,) = order.put(
            share_core(skip_parts[layer], order.after, order.ident(), layer > 0)
        )
        weights[layer].skip = [part[0] for part in held]

    def hold_attention(layer):
        (held,) = order.put(share_core(attention_parts[layer], order.after, order.ident()))
        place = weights[layer]
        place.query, place.key, place.value, place.attn_out = held[0]

    def hold_cross(layer):
        (held,) = order.put(share_core(cross_parts[layer], order.after, order.ident()))
        weights[layer].cross_query = [part[0] for part in held]
        weights[layer].cross_out = [part[1] for part in held]

    def hold_up(layer):
        (held,) = order.put(share_core(up_parts[layer], order.after, order.ident()))
        weights[layer].up = held[0][0]

    def hold_down(layer):
        (held,) = order.put(share_core(down_parts[layer], order.after, order.ident()))
        weights[layer].down = held[0][0]

    padded = -(-text_count // 128) * 128
    text_low = jnp.pad(text_states, ((0, 0), (0, padded - text_count), (0, 0)))
    text_low = text_low.reshape(seqs * padded, -1)
    texts = [SimpleNamespace(count=text_count) for _ in every]

    def hold_text():
        (held,) = order.put(share_core(text_parts[0], order.after, order.ident()))
        for layer in every:
            weights[layer].text_key = [part[2 * layer] for part in held]
            weights[layer].text_value = [part[2 * layer + 1] for part in held]

    def read_text(layer):
        text = texts[layer]
        place = weights[layer]
        width = place.text_key[0].shape[1]
        outs = order.multiply(
            lambda lefts, rights, _: [contract(lefts[0], right, 1, 0) for right in rights],
            [text_low],
            place.text_key + place.text_value,
            False,
            [],
            [(seqs * padded, width, jnp.float32)] * parts + [(seqs * padded, width, LOW)] * parts,
            256,
        )
        blocks = (seqs, padded, width)
        keys = [order.put(root(raw, order.after))[0] for raw in outs[:parts]]
        text.raws = [raw.reshape(blocks) for raw in outs[:parts]]
        text.keys = [key.reshape(blocks) for key in keys]
        text.values = [value.reshape(blocks) for value in outs[parts:]]

    text_parts = {}
    attention_parts[0] = across(attention[0], False, (skip_parts[0][-1],))
    hold_skip(0)

    def steps_of(layer):
        steps = SimpleNamespace()
        coming = layer + 1 if layer + 1 < layers else None

        def skipped():
            if not layer:
                text_parts[0] = across(text_along, True, order.after)
            hold_attention(layer)

        def turned():
            if layer:
                read_text(layer)

        def attended():
            if layer:
                down_parts[layer] = across(downs[layer], False, order.after)
                hold_up(layer)
            else:
                cross_parts[layer] = across(crosses[layer], True, order.after)
                up_parts[layer] = across(ups[layer], False, order.after)
                hold_text()
                if coming:
                    skip_parts[coming] = across(skips[coming], True, order.after)
                read_text(layer)
                if coming:
                    order.need(skip_parts[coming][1])
            hold_cross(layer)
            if not layer:
                down_parts[layer] = across(downs[layer], False, order.after)

        def crossed():
            if not layer:
                hold_up(layer)
            if coming:
                attention_parts[coming] = across(attention[coming], False, order.after)

        def raised():
            hold_down(layer)
            if coming:
                order.need(attention_parts[coming][1])
                cross_parts[coming] = across(crosses[coming], True, order.after[:1])

        def lowered():
            if coming:
                hold_skip(coming)
                up_parts[coming] = across(ups[coming], False, order.after)

        steps.skipped, steps.turned, steps.attended = skipped, turned, attended
        steps.crossed, steps.raised, steps.lowered = crossed, raised, lowered
        return steps

    cond_float = wide(condition)
    cond_silu, silu_pull = jax.vjp(jax.nn.silu, cond_float)
    cond_all = gather_fsdp_small(low(cond_silu)).reshape(along * seqs, cond_float.shape[1])
    rows = mod_weight.shape[1]
    place = lax.axis_index(FSDP) * size + lax.axis_index(CONTEXT)
    cond_rows = lax.dynamic_slice_in_dim(cond_all, place * rows, rows, axis=1)
    mod_low = low(mod_weight)
    mod_part = contract(cond_rows, mod_low, 1, 1)
    mod_part = gate(mod_part, arrived).reshape((along, seqs) + mod_part.shape[1:])
    mod_part = sum_fsdp_small(mod_part)
    mod_part = low(sum_context(gate(mod_part, (skip_parts[0][-1],))))
    if paired():
        mod_full = tensor_order(mod_part, swap_tensor(mod_part), -1)
    else:
        mod_full = lax.all_gather(mod_part, TENSOR, axis=2, tiled=True)
    modulations = [
        jnp.split(wide(mod_full[:, layer])[:, None, :], 6, axis=-1) for layer in every
    ]

    quarter = HD // 4
    frequency = ROPE_BASE ** (-jnp.arange(quarter, dtype=jnp.float32) / quarter)
    grid = positions.reshape(seqs, 2, parts, tokens)
    if paired():
        mine = lax.axis_index(TENSOR)
        grid = jnp.concatenate(
            [
                lax.dynamic_slice_in_dim(grid, mine, 1, axis=2),
                lax.dynamic_slice_in_dim(grid, 1 - mine, 1, axis=2),
            ],
            axis=2,
        )
    grid = wide(grid.transpose(2, 0, 3, 1).reshape(parts * seqs * tokens, 2))
    row_angle = grid[:, :1] * frequency
    col_angle = grid[:, 1:] * frequency
    cos = jnp.concatenate([jnp.cos(row_angle)] * 2 + [jnp.cos(col_angle)] * 2, axis=-1)
    sin = jnp.concatenate(
        [-jnp.sin(row_angle), jnp.sin(row_angle), -jnp.sin(col_angle), jnp.sin(col_angle)], axis=-1
    )
    tables = spread_heads(cos, sin, proj_weight.shape[-1])

    own = (seqs * tokens, latents.shape[-1])
    residual = wide(latents).reshape(own)
    stored = []
    for layer in every:
        residual, kept = layer_forward(
            residual,
            skip_inputs[layer].reshape(own),
            modulations[layer],
            texts[layer],
            tables,
            weights[layer],
            order,
            steps_of(layer),
        )
        stored.append(kept)
    block_output = low(residual).reshape(latents.shape)

    grad_res = wide(cotangent).reshape(own)
    cond_parts = []
    text_total = 0.0
    skip_grads = [None] * layers
    gradients = [None] * layers

    def add_modulation(layer, mod_all):
        gradients[layer].mod = jnp.einsum(
            "bk,bc->kc", wide(cond_rows), mod_all, precision=PRECISE
        )
        cond_parts.append(
            jnp.einsum("bc,kc->bk", mod_all, wide(mod_low[layer]), precision=PRECISE)
        )

    later = SimpleNamespace(
        start=lambda: None, first=lambda: None, second=lambda: None, third=lambda: None, sums=lambda: (), more=lambda: (), most=lambda: ()
    )
    for layer in reversed(every):
        grad_res, skip_grads[layer], text_part, reduced, later = layer_backward(
            grad_res,
            stored[layer],
            weights[layer],
            modulations[layer],
            tables,
            texts[layer],
            text_low,
            order,
            later,
            paired() and layer == 0,
        )
        text_total = text_total + text_part
        gradients[layer] = reduced
        if layer:
            add_modulation(layer, later.columns())
    mod_all, text_sum = later.end(low(text_total))
    add_modulation(0, mod_all)
    gradients = [
        (
            wide(each.skip[0]),
            each.mod,
            wide(jnp.concatenate([each.attention[1:], each.cross[1:]], axis=0)).transpose(1, 0, 2),
            wide(jnp.stack([each.attention[0], each.cross[0]], axis=0)).transpose(0, 2, 1),
            wide(each.text).transpose(1, 0, 2),
            wide(each.up[0]),
            wide(each.down[0]).T,
        )
        for each in gradients
    ]
    text_sum = wide(text_sum).reshape(seqs, padded, -1)[:, :text_count]
    cond_total = sum(cond_parts)
    if paired():
        cond_total = cond_total + swap_tensor(cond_total)
    else:
        cond_total = lax.psum(cond_total, TENSOR)
    sent = cond_total.reshape(along, seqs, rows)
    here = lax.axis_index(FSDP)
    cond_sum = jnp.zeros((along, size, seqs, rows), jnp.float32)
    for step in range(along):
        part = lax.dynamic_index_in_dim(sent, (here + step) % along, 0, keepdims=False)
        if step:
            part = shift_fsdp(part, step)
        for offset, piece in gather_context(part):
            cond_sum = lax.dynamic_update_slice(
                cond_sum,
                piece[None, None],
                ((here - step + along) % along, lax.axis_index(CONTEXT) ^ offset, 0, 0),
            )
    cond_sum = cond_sum.transpose(2, 0, 1, 3).reshape(seqs, along * size * rows)
    condition_grad = silu_pull(cond_sum)[0]
    skips_grad = jnp.stack(skip_grads, axis=0).reshape(skip_inputs.shape)

    spreads = (
        (2 * D) ** (-0.5),
        D ** (-0.5),
        D ** (-0.5),
        (D // 16) ** (-0.5),
        DT ** (-0.5),
        D ** (-0.5),
        FF ** (-0.5),
    )
    tokens_total = seqs * along * tokens * size * parts
    new_weights = []
    new_momenta = []
    new_averages = []
    for index in range(len(masters)):
        gradient = jnp.stack([gradients[layer][index] for layer in every], axis=0)
        rate = RATE_FACTOR * spreads[index] / math.sqrt(tokens_total)
        moment_new = MOMENTUM * momenta[index] + gradient
        weight_new = masters[index] - rate * (gradient + MOMENTUM * moment_new)
        new_weights.append(weight_new)
        new_momenta.append(moment_new)
        new_averages.append(
            AVERAGE_DECAY * averages[index] + (1.0 - AVERAGE_DECAY) * weight_new
        )
    return (
        block_output,
        grad_res.reshape(latents.shape),
        skips_grad,
        text_sum,
        condition_grad,
        *new_weights,
        *new_momenta,
        *new_averages,
    )


def solution(mesh):
    weight_specs = (
        P(None, (FSDP, CONTEXT), TENSOR),
        P(None, (FSDP, CONTEXT), TENSOR),
        P(None, (FSDP, CONTEXT), None, TENSOR),
        P(None, None, TENSOR, (FSDP, CONTEXT)),
        P(None, (FSDP, CONTEXT), None, TENSOR),
        P(None, (FSDP, CONTEXT), TENSOR),
        P(None, TENSOR, (FSDP, CONTEXT)),
    )
    in_specs = (
        P(FSDP, (CONTEXT, TENSOR), None),
        P(None, FSDP, (CONTEXT, TENSOR), None),
        P(FSDP, None, None),
        P(FSDP, None),
        P(FSDP, None, CONTEXT),
        P(FSDP, (CONTEXT, TENSOR), None),
    ) + weight_specs * 3
    out_specs = (
        P(FSDP, (CONTEXT, TENSOR), None),
        P(FSDP, (CONTEXT, TENSOR), None),
        P(None, FSDP, (CONTEXT, TENSOR), None),
        P(FSDP, None, None),
        P(FSDP, None),
    ) + weight_specs * 3
    return jax.shard_map(shards, mesh=mesh, in_specs=in_specs, out_specs=out_specs, check_vma=False)
```
